32 devices in a mesh: rep: 2 (over y), shard: 16 (over z, x, core).
Axes of the slice: x: 2, y: 2, z: 4, core: 2. Of those that a mesh axis runs over, the one named last changes fastest.
Arguments:
- inputs: bfloat16 [32, 1024, 768], P(('rep', 'shard')), may hold values from -6 to 6
- token_types: int32 [32, 1024], P(('rep', 'shard')), may hold values from 0 to 2
- buckets: int32 [2047], replicated, may hold values from 0 to 2047
- w_query: bfloat16 [768, 768], P('shard'), may hold values from -0.21875 to 0.21875
- w_key: bfloat16 [768, 768], P('shard'), may hold values from -0.21875 to 0.21875
- w_value: bfloat16 [768, 768], P('shard'), may hold values from -0.21875 to 0.21875
- b_value: bfloat16 [768], P('shard'), may hold values from -0.29882812 to 0.29882812
- w_pos: bfloat16 [768, 768], P('shard'), may hold values from -0.21875 to 0.21875
- bias_content: bfloat16 [768], P('shard'), may hold values from -5 to 5
- bias_position: bfloat16 [768], P('shard'), may hold values from -5 to 5
- bias_type: bfloat16 [768], P('shard'), may hold values from -5 to 5
- type_embed: bfloat16 [2, 768], P(None, 'shard'), may hold values from -5 to 5
- w_out: bfloat16 [768, 768], P('shard'), may hold values from -1.75 to 1.75
- b_out: bfloat16 [768], P('shard'), may hold values from -1 to 1
- gain_attn: bfloat16 [768], P('shard'), may hold values from 0.5 to 1.5
- shift_attn: bfloat16 [768], P('shard'), may hold values from -1 to 1
- w_inner: bfloat16 [768, 3072], P('shard'), may hold values from -0.21875 to 0.21875
- b_inner: bfloat16 [3072], P('shard'), may hold values from -2.5 to 2.5
- w_outer: bfloat16 [3072, 768], P('shard'), may hold values from -0.109375 to 0.109375
- b_outer: bfloat16 [768], P('shard'), may hold values from -1 to 1
- gain_ffn: bfloat16 [768], P('shard'), may hold values from 0.5 to 1.5
- shift_ffn: bfloat16 [768], P('shard'), may hold values from -1 to 1
- cotangent: bfloat16 [32, 1024, 768], P(('rep', 'shard')), may hold values from -6 to 6
Outputs:
- output: bfloat16 [32, 1024, 768], P(('rep', 'shard'))
- grad_inputs: float32 [32, 1024, 768], P(('rep', 'shard'))
- grad_w_query: float32 [768, 768], P('shard')
- grad_w_key: float32 [768, 768], P('shard')
- grad_w_value: float32 [768, 768], P('shard')
- grad_b_value: float32 [768], P('shard')
- grad_w_pos: float32 [768, 768], P('shard')
- grad_bias_content: float32 [768], P('shard')
- grad_bias_position: float32 [768], P('shard')
- grad_bias_type: float32 [768], P('shard')
- grad_type_embed: float32 [2, 768], P(None, 'shard')
- grad_w_out: float32 [768, 768], P('shard')
- grad_b_out: float32 [768], P('shard')
- grad_gain_attn: float32 [768], P('shard')
- grad_shift_attn: float32 [768], P('shard')
- grad_w_inner: float32 [768, 3072], P('shard')
- grad_b_inner: float32 [3072], P('shard')
- grad_w_outer: float32 [3072, 768], P('shard')
- grad_b_outer: float32 [768], P('shard')
- grad_gain_ffn: float32 [768], P('shard')
- grad_shift_ffn: float32 [768], P('shard')
The draws below stay inside these ranges and needn't reach their ends.
All inputs are finite; a program needn't handle non-finite values.
Results may differ from the reference program's by a relative error of at most 0.035.
Values may be sent and summed in bfloat16 or wider, within the bound.
A program may use at most 320 MiB of HBM per device.

```python
import math
import jax
import jax.numpy as jnp
from jax import lax

D = 768
HEADS = 12
FF = 3072
LEN = 1024
SEQS = 32


def set_ends(values, key, least, largest):
    longest = values.shape.index(max(values.shape))
    spots = []
    for shift in (0, 1):
        where = [jax.random.randint(jax.random.fold_in(key, axis), (), 0, length) for axis, length in enumerate(values.shape)]
        where[longest] = (where[longest] + shift) % values.shape[longest]
        spots.append(tuple(where))
    return values.at[spots[0]].set(least).at[spots[1]].set(largest)


def steps_of(stream_key, extent, cuts, smallest, top_value):
    level = 1.0
    for dim, blocks in cuts:
        steps = jax.random.uniform(jax.random.fold_in(jax.random.fold_in(stream_key, 6), dim), (blocks,), jnp.float32, smallest / len(cuts), top_value / len(cuts))
        level = level * jnp.repeat(jnp.exp(steps), extent[dim] // blocks).reshape((-1,) + (1,) * (len(extent) - 1 - dim))
    return level


def gaussian(own_key, extent, deviation, most, shards=(), kind=jnp.bfloat16):
    level = steps_of(own_key, extent, shards, -0.22, 0.18) if shards else 1.0
    array = jax.random.normal(own_key, extent, jnp.float32) * deviation * level
    return jnp.minimum(jnp.maximum(array, -most), most).astype(kind)


def setup_inputs(seed: int = 0) -> dict:
    seeds = jax.random.split(jax.random.key(seed), 24)
    return {
        "inputs": gaussian(seeds[0], (SEQS, LEN, D), 1.0, 6.0, ((0, 32),)),
        "token_types": set_ends(jax.random.randint(seeds[1], (SEQS, LEN), 0, 3), jax.random.fold_in(seeds[1], 1), 0, 2).astype(jnp.int32),
        "buckets": set_ends(jax.random.randint(seeds[2], (2 * LEN - 1,), 0, 2 * LEN), jax.random.fold_in(seeds[2], 1), 0, (2 * LEN) - 1).astype(jnp.int32),
        "w_query": gaussian(seeds[3], (D, D), D ** -0.5, 0.21875, ((0, 16),)),
        "w_key": gaussian(seeds[4], (D, D), D ** -0.5, 0.21875, ((0, 16),)),
        "w_value": gaussian(seeds[5], (D, D), D ** -0.5, 0.21875, ((0, 16),)),
        "b_value": gaussian(seeds[6], (D,), 0.05, 0.29882812, ((0, 16),)),
        "w_pos": gaussian(seeds[7], (D, D), D ** -0.5, 0.21875, ((0, 16),)),
        "bias_content": gaussian(seeds[8], (D,), 1.0, 5.0, ((0, 16),)),
        "bias_position": gaussian(seeds[9], (D,), 1.0, 5.0, ((0, 16),)),
        "bias_type": gaussian(seeds[10], (D,), 1.0, 5.0, ((0, 16),)),
        "type_embed": gaussian(seeds[11], (2, D), 1.0, 5.0, ((1, 16),)),
        "w_out": gaussian(seeds[12], (D, D), (D // 64) ** -0.5, 1.75, ((0, 16),)),
        "b_out": gaussian(seeds[13], (D,), 0.2, 1.0, ((0, 16),)),
        "gain_attn": jnp.clip(1.0 + 0.1 * jax.random.normal(seeds[14], (D,), jnp.float32), 0.5, 1.5).astype(jnp.bfloat16),
        "shift_attn": gaussian(seeds[15], (D,), 0.2, 1.0, ((0, 16),)),
        "w_inner": gaussian(seeds[16], (D, FF), D ** -0.5, 0.21875, ((0, 16),)),
        "b_inner": gaussian(seeds[17], (FF,), 0.5, 2.5, ((0, 16),)),
        "w_outer": gaussian(seeds[18], (FF, D), FF ** -0.5, 0.109375, ((0, 16),)),
        "b_outer": gaussian(seeds[19], (D,), 0.2, 1.0, ((0, 16),)),
        "gain_ffn": jnp.clip(1.0 + 0.1 * jax.random.normal(seeds[20], (D,), jnp.float32), 0.5, 1.5).astype(jnp.bfloat16),
        "shift_ffn": gaussian(seeds[21], (D,), 0.2, 1.0, ((0, 16),)),
        "cotangent": gaussian(seeds[22], (SEQS, LEN, D), 1.0, 6.0, ((0, 32),)),
    }


@jax.custom_vjp
def low(v):
    return lax.optimization_barrier(v.astype(jnp.bfloat16)).astype(jnp.float32)

@jax.custom_vjp
def low_back(v):
    return v

def low_keep(v):
    return (low(v), None)

def low_pass(kept, grad):
    return (grad,)

def back_keep(v):
    return (v, None)

def back_low(kept, grad):
    return (low(grad),)
low.defvjp(low_keep, low_pass)
low_back.defvjp(back_keep, back_low)
PRECISION = lax.Precision.HIGHEST
EPSILON = 1e-06

def narrow(value):
    return low_back(low(value))

def product(left, right):
    return jnp.dot(left, right, precision=PRECISION, preferred_element_type=jnp.float32)

def layer_norm(value, gain, shift):
    center = lax.optimization_barrier(jnp.mean(value, axis=-1, keepdims=True))
    centred = value - center
    spread = lax.optimization_barrier(jnp.mean(centred * centred, axis=-1, keepdims=True))
    return centred * lax.rsqrt(spread + EPSILON) * gain + shift

def sinusoid(buckets, width):
    half = width // 2
    span = (buckets.shape[0] + 1) // 2
    rates = jnp.exp(jnp.arange(half, dtype=jnp.float32) * (-2.0 * math.log(10000.0) / width))
    angles = (buckets - span).astype(jnp.float32)[:, None] * rates[None, :]
    return jnp.concatenate([jnp.sin(angles), jnp.cos(angles)], axis=1)

def skew_rows(position_all, first, length):
    heads, block, span = position_all.shape
    flat = position_all.reshape(heads, block * span)
    flat = jnp.pad(flat, ((0, 0), (0, length)))
    moved = lax.dynamic_slice_in_dim(flat, first, block * (span - 1), 1)
    return moved.reshape(heads, block, span - 1)[:, :, :length]

def attend(content_block, position_block, type_block, kinds_block, start, keys, values, relative, kinds):
    block, heads, head_size = content_block.shape
    length = keys.shape[0]
    window = lax.dynamic_slice_in_dim(relative, (length - block - start).astype(jnp.int32), length + block - 1, 0)
    content = jnp.einsum('bne,lne->nbl', content_block, keys, precision=PRECISION, preferred_element_type=jnp.float32)
    position_all = jnp.einsum('bne,mne->nbm', position_block, window, precision=PRECISION, preferred_element_type=jnp.float32)
    position = skew_rows(position_all, block - 1, length)
    same = (kinds_block[:, None] == kinds[None, :]).astype(jnp.float32)
    base = jnp.transpose(type_block[:, :, 0])[:, :, None]
    lift = jnp.transpose(type_block[:, :, 1] - type_block[:, :, 0])[:, :, None]
    scores = low_back(content + position + base + lift * same[None])
    probs = low(jax.nn.softmax(scores, axis=-1))
    mixed = jnp.einsum('nbl,lne->bne', probs, values, precision=PRECISION, preferred_element_type=jnp.float32)
    return mixed.reshape(block, heads * head_size)

def attn_layer(rows, kinds, buckets, weights):
    w_query, w_key, w_value, b_value, w_pos, bias_content, bias_position, bias_type, type_embed, w_out, b_out, gain_attn, shift_attn = weights
    length, width = rows.shape
    head_size = width // HEADS
    scale = 1.0 / math.sqrt(head_size)
    query = low_back(product(rows, w_query))
    content_q = narrow((query + bias_content) * scale).reshape(length, HEADS, head_size)
    position_q = narrow((query + bias_position) * scale).reshape(length, HEADS, head_size)
    type_q = ((query + bias_type) * scale).reshape(length, HEADS, head_size)
    keys = narrow(product(rows, w_key)).reshape(length, HEADS, head_size)
    values = narrow(product(rows, w_value) + b_value).reshape(length, HEADS, head_size)
    embed = low(sinusoid(buckets, width))
    relative = narrow(product(embed, w_pos)).reshape(2 * length - 1, HEADS, head_size)
    type_score = jnp.einsum('lne,cne->lnc', type_q, type_embed.reshape(2, HEADS, head_size), precision=lax.Precision.HIGHEST, preferred_element_type=jnp.float32)
    block = min(512, length)
    count = length // block

    def one_block(pieces):
        return jax.checkpoint(attend)(pieces[0], pieces[1], pieces[2], pieces[3], pieces[4], keys, values, relative, kinds)
    starts = jnp.arange(count, dtype=jnp.int32) * block
    mixed = lax.map(one_block, (content_q.reshape(count, block, HEADS, head_size), position_q.reshape(count, block, HEADS, head_size), type_score.reshape(count, block, HEADS, 2), kinds.reshape(count, block), starts))
    attended = narrow(mixed.reshape(length, width))
    branch = low_back(product(attended, w_out))
    return layer_norm(rows + branch + b_out, gain_attn, shift_attn)

def ffn_layer(middle, weights):
    w_inner, b_inner, w_outer, b_outer, gain_ffn, shift_ffn = weights
    inner = low_back(product(low(middle), w_inner) + b_inner)
    hidden = narrow(jax.nn.gelu(inner, approximate=True))
    branch = low_back(product(hidden, w_outer))
    return layer_norm(middle + branch + b_outer, gain_ffn, shift_ffn)

def reference(inputs, token_types, buckets, w_query, w_key, w_value, b_value, w_pos, bias_content, bias_position, bias_type, type_embed, w_out, b_out, gain_attn, shift_attn, w_inner, b_inner, w_outer, b_outer, gain_ffn, shift_ffn, cotangent):
    params = tuple((item.astype(jnp.float32) for item in (w_query, w_key, w_value, b_value, w_pos, bias_content, bias_position, bias_type, type_embed, w_out, b_out, gain_attn, shift_attn, w_inner, b_inner, w_outer, b_outer, gain_ffn, shift_ffn)))

    def forward(data, weights):

        def single(pair):
            middle = attn_layer(pair[0], pair[1], buckets, weights[:13])
            return ffn_layer(middle, weights[13:])
        return lax.map(jax.checkpoint(single), (data, token_types))
    result, pull = jax.vjp(forward, inputs.astype(jnp.float32), params)
    grad_inputs, grads = pull(cotangent.astype(jnp.float32))
    return (result.astype(jnp.bfloat16), grad_inputs, grads[0], grads[1], grads[2], grads[3], grads[4], grads[5], grads[6], grads[7], grads[8], grads[9], grads[10], grads[11], grads[12], grads[13], grads[14], grads[15], grads[16], grads[17], grads[18])
```

```python
import functools, math
import jax, jax.numpy as jnp
from jax import lax
from jax.experimental import pallas as pl
from jax.experimental.pallas import tpu as pltpu
from jax.sharding import PartitionSpec as P
F32=jnp.float32; BF=jnp.bfloat16
HEADS=12
LOG2E=math.log2(math.e); LN2=math.log(2.0)
NT=(((1,),(1,)),((),())); NN=(((1,),(0,)),((),())); TN=(((0,),(0,)),((),()))
def dot(a,b,dims=NN): return lax.dot_general(a,b,dims,preferred_element_type=F32)

BI=256

def lane_half(rows, lanes):
    lane=lax.broadcasted_iota(jnp.int32,(rows,lanes),1)
    return (lane//64)%2

def split_hi_lo(v):
    hi=v.astype(BF); return hi,(v-hi.astype(F32)).astype(BF)

def queries(q, vec, oh):
    s=0.125*LOG2E
    cq=((q+vec[0:1])*s).astype(BF)
    pq=((q+vec[1:2])*s).astype(BF)
    tq=(q+vec[2:3])*0.125
    return cq,pq,tq

def fwd_kernel(roll_bf, q_ref,k_ref,v_ref,r_ref,oh_ref,vec_ref,e_ref,att_ref,linv_ref):
    bi=q_ref.shape[0]; L=k_ref.shape[0]; W=L+bi
    i=pl.program_id(1)
    vec=vec_ref[0]
    q=q_ref[...]
    oh_i=oh_ref[pl.ds(pl.multiple_of(i*bi,bi),bi),:]
    cq,pq,tq=queries(q,vec,None)
    rr=lax.broadcasted_iota(jnp.int32,(256,128),0)%128
    cc=lax.broadcasted_iota(jnp.int32,(256,128),1)
    M=jnp.where((rr//64==cc//64)&(cc%64<6),1.0,0.0).astype(BF)
    def tt(te):
        hi,lo=split_hi_lo(tq*(te*LOG2E))
        return dot(jnp.concatenate([hi,lo],axis=1),M)
    t0=tt(vec[3:4]); t1=tt(vec[4:5])
    tv=jnp.where(oh_i>0,t1,t0)
    hi=tv.astype(BF).astype(F32)
    lane=lax.broadcasted_iota(jnp.int32,(bi,128),1)
    tv=jnp.where(lane%64<3,hi,tv-hi).astype(BF)
    half=lane_half(bi,128)
    kext=jnp.concatenate([k_ref[...],oh_ref[...]],axis=1)
    vext=jnp.concatenate([v_ref[...],jnp.ones((L,128),BF)],axis=1)
    w0=pl.multiple_of(L-bi-i*bi,bi)
    rwin=r_ref[pl.ds(w0,W),:]
    z=jnp.zeros((),BF)
    outs=[]
    for h in range(2):
        qx=jnp.concatenate([jnp.where(half==h,cq,z),jnp.where(half==h,tv,z)],axis=1)
        pos=dot(jnp.where(half==h,pq,z),rwin,NT)
        if roll_bf: pos=pos.astype(BF)
        pos=pltpu.roll(pos,W-(bi-1),1,stride=1,stride_axis=0)[:,:L]
        s=dot(qx,kext,NT)+pos.astype(F32)
        m=jnp.max(s,axis=1,keepdims=True)
        e=jnp.exp2(s-m).astype(BF)
        e_ref[h]=e
        o=dot(e,vext)
        li=1.0/o[:,128:]
        outs.append((o[:,:128]*li,li))
    att_ref[...]=jnp.where(half==0,outs[0][0],outs[1][0]).astype(BF)
    linv_ref[...]=jnp.where(half==0,outs[0][1],outs[1][1])

def att_fwd(q,k,v,r,oh,vec,bi=BI,roll_bf=False):
    L,D=q.shape; P=D//128; nb=L//bi
    return pl.pallas_call(functools.partial(fwd_kernel,roll_bf),
        grid=(P,nb),
        in_specs=[pl.BlockSpec((bi,128),lambda p,i:(i,p)),
            pl.BlockSpec((L,128),lambda p,i:(0,p)),
            pl.BlockSpec((L,128),lambda p,i:(0,p)),
            pl.BlockSpec((2*L,128),lambda p,i:(0,p)),
            pl.BlockSpec((L,128),lambda p,i:(0,0)),
            pl.BlockSpec((1,8,128),lambda p,i:(p,0,0))],
        out_specs=[pl.BlockSpec((2,bi,L),lambda p,i:(p,i,0)),
            pl.BlockSpec((bi,128),lambda p,i:(i,p)),
            pl.BlockSpec((bi,128),lambda p,i:(i,p))],
        out_shape=[jax.ShapeDtypeStruct((2*P,L,L),BF),jax.ShapeDtypeStruct((L,D),BF),jax.ShapeDtypeStruct((L,D),F32)],
        compiler_params=pltpu.CompilerParams(vmem_limit_bytes=56*2**20,dimension_semantics=("arbitrary","arbitrary")),
        name="attend")(q,k,v,r,oh,vec)

def bwd_kernel(roll_bf,q_ref,k_ref,v_ref,r_ref,oh_ref,vec_ref,e_ref,att_ref,linv_ref,datt_ref,
               dq_ref,dk_ref,dv_ref,dr_ref,dvec_ref, dk_acc,dv_acc,dr_acc):
    bi=q_ref.shape[0]; L=k_ref.shape[0]; W=L+bi
    i=pl.program_id(1); nb=pl.num_programs(1)
    vec=vec_ref[0]
    q=q_ref[...]
    oh_i=oh_ref[pl.ds(pl.multiple_of(i*bi,bi),bi),:].astype(F32)
    cq,pq,tq=queries(q,vec,None)
    half=lane_half(bi,128)
    lane=lax.broadcasted_iota(jnp.int32,(bi,128),1)
    @pl.when(i==0)
    def _():
        dk_acc[...]=jnp.zeros_like(dk_acc); dv_acc[...]=jnp.zeros_like(dv_acc); dr_acc[...]=jnp.zeros_like(dr_acc)
        dvec_ref[...]=jnp.zeros_like(dvec_ref)
    P=jnp.where(lax.broadcasted_iota(jnp.int32,(bi,bi),0)+lax.broadcasted_iota(jnp.int32,(bi,bi),1)==bi-1,1.0,0.0).astype(BF)
    pqr=dot(P,pq).astype(BF)
    kext=jnp.concatenate([k_ref[...],oh_ref[...]],axis=1)
    ones2=jnp.where(lax.broadcasted_iota(jnp.int32,(L,128),1)<2,1.0,0.0).astype(BF)
    vext=jnp.concatenate([v_ref[...],ones2],axis=1)
    w0=pl.multiple_of(L-bi-i*bi,bi)
    rwin=r_ref[pl.ds(w0,W),:]
    z=jnp.zeros((),BF)
    dattl=datt_ref[...].astype(F32)*linv_ref[...]
    prod=dattl*att_ref[...].astype(F32)
    dattl=dattl.astype(BF)
    dcs=[];dps=[];dts=[];tes=[]
    dk=None; dv=None; dr=None
    for h in range(2):
        delta=-jnp.sum(jnp.where(half==h,prod,0.0),axis=1,keepdims=True)
        dhi=delta.astype(BF).astype(F32)
        dx=jnp.where(lane==0,dhi,jnp.where(lane==1,delta-dhi,0.0)).astype(BF)
        dm=jnp.where(half==h,dattl,z)
        dpd=dot(jnp.concatenate([dm,dx],axis=1),vext,NT)
        e=e_ref[h]
        ds=(e.astype(F32)*dpd).astype(BF)
        dvh=dot(e,dm,TN)
        dkh=dot(ds,jnp.where(half==h,cq,z),TN)
        dc=dot(ds,kext)
        rev=dot(P,ds)
        if roll_bf: rev=rev.astype(BF)
        rev=jnp.concatenate([rev,jnp.zeros((bi,W-L),rev.dtype)],axis=1)
        dpr=pltpu.roll(rev,0,1,stride=1,stride_axis=0).astype(BF)
        dp=dot(dpr,rwin)
        drh=dot(dpr,jnp.where(half==h,pqr,z),TN)
        dv=dvh if dv is None else dv+dvh
        dk=dkh if dk is None else dk+dkh
        dr=drh if dr is None else dr+drh
        D=jnp.where(lane<3,dc[:,128:],0.0)
        dall=jnp.sum(D,axis=1,keepdims=True)
        d1=jnp.sum(D*oh_i,axis=1,keepdims=True)
        d0=dall-d1
        dcs.append(dc[:,:128]); dps.append(dp)
        dts.append(d0*vec[3:4]+d1*vec[4:5])
        tes.append((d0,d1))
    dv_acc[...]+=dv
    dk_acc[...]+=dk
    dr_acc[pl.ds(w0,W),:]+=dr
    dcq=jnp.where(half==0,dcs[0],dcs[1]).astype(BF).astype(F32)
    dpr=jnp.where(half==0,dps[0],dps[1]).astype(BF)
    dpq=dot(P,dpr)
    dtq=jnp.where(half==0,dts[0],dts[1])
    dq_ref[...]=((dcq+dpq+dtq)*0.125).astype(BF)
    d0=jnp.where(half==0,tes[0][0],tes[1][0]); d1=jnp.where(half==0,tes[0][1],tes[1][1])
    rows=[dcq*0.125,dpq*0.125,dtq*0.125,d0*tq,d1*tq]
    sums=[jnp.sum(v,axis=0,keepdims=True) for v in rows]+[jnp.zeros((3,128),F32)]
    dvec_ref[...]+=jnp.concatenate(sums,axis=0)[None]
    @pl.when(i==nb-1)
    def _():
        dk_ref[...]=(dk_acc[...]*LN2).astype(BF)
        dv_ref[...]=dv_acc[...].astype(BF)
        dr_ref[...]=(dr_acc[...]*LN2).astype(BF)

def att_bwd(q,k,v,r,oh,vec,e,att,linv,datt,bi=BI,roll_bf=False):
    L,D=q.shape; P=D//128; nb=L//bi
    return pl.pallas_call(functools.partial(bwd_kernel,roll_bf),
        grid=(P,nb),
        in_specs=[pl.BlockSpec((bi,128),lambda p,i:(i,p)),
            pl.BlockSpec((L,128),lambda p,i:(0,p)),
            pl.BlockSpec((L,128),lambda p,i:(0,p)),
            pl.BlockSpec((2*L,128),lambda p,i:(0,p)),
            pl.BlockSpec((L,128),lambda p,i:(0,0)),
            pl.BlockSpec((1,8,128),lambda p,i:(p,0,0)),
            pl.BlockSpec((2,bi,L),lambda p,i:(p,i,0)),
            pl.BlockSpec((bi,128),lambda p,i:(i,p)),
            pl.BlockSpec((bi,128),lambda p,i:(i,p)),
            pl.BlockSpec((bi,128),lambda p,i:(i,p))],
        out_specs=[pl.BlockSpec((bi,128),lambda p,i:(i,p)),
            pl.BlockSpec((L,128),lambda p,i:(0,p)),
            pl.BlockSpec((L,128),lambda p,i:(0,p)),
            pl.BlockSpec((2*L,128),lambda p,i:(0,p)),
            pl.BlockSpec((1,8,128),lambda p,i:(p,0,0))],
        out_shape=[jax.ShapeDtypeStruct((L,D),BF),jax.ShapeDtypeStruct((L,D),BF),jax.ShapeDtypeStruct((L,D),BF),
            jax.ShapeDtypeStruct((2*L,D),BF),jax.ShapeDtypeStruct((P,8,128),F32)],
        scratch_shapes=[pltpu.VMEM((L,128),F32),pltpu.VMEM((L,128),F32),pltpu.VMEM((2*L,128),F32)],
        compiler_params=pltpu.CompilerParams(vmem_limit_bytes=56*2**20,dimension_semantics=("arbitrary","arbitrary")),
        name="attend_back")(q,k,v,r,oh,vec,e,att,linv,datt)

CP=lambda **k: pltpu.CompilerParams(vmem_limit_bytes=60*2**20,**k)
C0=math.sqrt(2.0/math.pi); C1=0.044715
EPS=1e-6
ONE=pl.Buffered(1)

def proj_kernel(x_ref,em_ref,wq_ref,wk_ref,wv_ref,wp_ref,bv_ref,q_ref,k_ref,v_ref,r_ref):
    x=x_ref[...]
    q_ref[...]=dot(x,wq_ref[...])
    k_ref[...]=dot(x,wk_ref[...]).astype(BF)
    v_ref[...]=(dot(x,wv_ref[...])+bv_ref[...]).astype(BF)
    r_ref[...]=dot(em_ref[...],wp_ref[...]).astype(BF)

def project(x,em,wq,wk,wv,wp,bv,bi=256):
    L,D=x.shape; nb=L//bi
    w=pl.BlockSpec((D,D),lambda i:(0,0),pipeline_mode=ONE)
    row=pl.BlockSpec((bi,D),lambda i:(i,0)); row2=pl.BlockSpec((2*bi,D),lambda i:(i,0))
    return pl.pallas_call(proj_kernel,grid=(nb,),
        in_specs=[row,row2,w,w,w,w,pl.BlockSpec((1,D),lambda i:(0,0))],
        out_specs=[row,row,row,row2],
        out_shape=[jax.ShapeDtypeStruct((L,D),F32),jax.ShapeDtypeStruct((L,D),BF),jax.ShapeDtypeStruct((L,D),BF),jax.ShapeDtypeStruct((2*L,D),BF)],
        compiler_params=CP(),name="project")(x,em,wq,wk,wv,wp,bv)

def ln_stats(z):
    n=z.shape[1]
    mu=jnp.sum(z,axis=1,keepdims=True)*(1.0/n)
    c=z-mu
    var=jnp.sum(c*c,axis=1,keepdims=True)*(1.0/n)
    r=lax.rsqrt(var+EPS)
    return c*r,r

def ln_back(g,zhat,r):
    n=g.shape[1]
    a=jnp.sum(g,axis=1,keepdims=True)*(1.0/n)
    b=jnp.sum(g*zhat,axis=1,keepdims=True)*(1.0/n)
    return r*(g-a-zhat*b)

def rowsum(v): return jnp.sum(v,axis=0,keepdims=True)

def mid_kernel(nb,bi,fc,x_ref,att_ref,cot_ref,wo_ref,wi_ref,wu_ref,vec_ref,bi_ref,
        out_ref,dz1_ref,datt_ref,dwo_ref,dwi_ref,dwu_ref,dvec_ref,dbi_ref,
        mid_s,att_s,dffn_s,dattn_s,hid_s,din_s,acc_s):
    t=pl.program_id(0)
    D=x_ref.shape[1]; FF=wi_ref.shape[1]; nc=FF//fc
    @pl.when(t==0)
    def _():
        dvec_ref[...]=jnp.zeros_like(dvec_ref); dbi_ref[...]=jnp.zeros_like(dbi_ref)
    @pl.when(t<nb)
    def _():
        rows=pl.ds(pl.multiple_of(t*bi,bi),bi)
        b_out,ga,sa,b_outer,gf,sf=[vec_ref[k:k+1,:] for k in range(6)]
        att=att_ref[...]
        att_s[rows,:]=att
        z1=x_ref[...].astype(F32)+dot(att,wo_ref[...])+b_out
        zh1,r1=ln_stats(z1)
        middle=zh1*ga+sa
        mid=middle.astype(BF)
        mid_s[rows,:]=mid
        acc_s[...]=middle+b_outer
        for c in range(nc):
            cs=slice(c*fc,(c+1)*fc)
            v=dot(mid,wi_ref[:,cs])+bi_ref[:,cs]
            u=v*v
            th=jnp.tanh(v*(C0+(C0*C1)*u))
            hv=0.5*v
            hid=(hv+hv*th).astype(BF)
            dg=0.5+0.5*th+hv*(1.0-th*th)*(C0+(3*C0*C1)*u)
            hid_s[rows,cs]=hid
            din_s[rows,cs]=dg.astype(BF)
            acc_s[...]+=dot(hid,wu_ref[cs,:])
        zh2,r2=ln_stats(acc_s[...])
        out_ref[...]=(zh2*gf+sf).astype(BF)
        g=cot_ref[...].astype(F32)
        dz2=ln_back(g*gf,zh2,r2)
        dffn=dz2.astype(BF)
        dffn_s[rows,:]=dffn
        acc_s[...]=dz2
        dbs=[]
        for c in range(nc):
            cs=slice(c*fc,(c+1)*fc)
            dh=dot(dffn,wu_ref[cs,:],NT)
            din=(dh*din_s[rows,cs].astype(F32)).astype(BF)
            din_s[rows,cs]=din
            dbi_ref[:,cs]+=rowsum(din.astype(F32))
            acc_s[...]+=dot(din,wi_ref[:,cs],NT)
        dm=acc_s[...]
        dz1=ln_back(dm*ga,zh1,r1)
        dz1_ref[...]=dz1
        dattn=dz1.astype(BF)
        dattn_s[rows,:]=dattn
        datt_ref[...]=dot(dattn,wo_ref[...],NT).astype(BF)
        dvec_ref[...]+=jnp.concatenate([rowsum(dz1),rowsum(dm*zh1),rowsum(dm),rowsum(dz2),rowsum(g*zh2),rowsum(g),jnp.zeros((2,D),F32)],axis=0)
    @pl.when(t==nb)
    def _():
        dwo_ref[...]=dot(att_s[...],dattn_s[...],TN).astype(BF)
    for c in range(nc):
        cs=slice(c*fc,(c+1)*fc)
        @pl.when(t==nb+c)
        def _():
            dwi_ref[...]=dot(mid_s[...],din_s[:,cs],TN).astype(BF)
            dwu_ref[...]=dot(hid_s[:,cs],dffn_s[...],TN).astype(BF)

def middle(x,att,cot,wo,wi,wu,vec,b_inner,bi=256,fc=512):
    L,D=x.shape; FF=wi.shape[1]; nb=L//bi; nc=FF//fc
    row=pl.BlockSpec((bi,D),lambda t:(jnp.minimum(t,nb-1),0))
    full=lambda s: pl.BlockSpec(s,lambda t:(0,0),pipeline_mode=ONE)
    cc=lambda t: jnp.clip(t-nb,0,nc-1)
    return pl.pallas_call(functools.partial(mid_kernel,nb,bi,fc),grid=(nb+nc,),
        in_specs=[row,row,row,full((D,D)),full((D,FF)),full((FF,D)),full((8,D)),full((1,FF))],
        out_specs=[row,row,row,pl.BlockSpec((D,D),lambda t:(0,0)),pl.BlockSpec((D,fc),lambda t:(0,cc(t))),pl.BlockSpec((fc,D),lambda t:(cc(t),0)),
            pl.BlockSpec((8,D),lambda t:(0,0)),pl.BlockSpec((1,FF),lambda t:(0,0))],
        out_shape=[jax.ShapeDtypeStruct((L,D),BF),jax.ShapeDtypeStruct((L,D),F32),jax.ShapeDtypeStruct((L,D),BF),
            jax.ShapeDtypeStruct((D,D),BF),jax.ShapeDtypeStruct((D,FF),BF),jax.ShapeDtypeStruct((FF,D),BF),
            jax.ShapeDtypeStruct((8,D),F32),jax.ShapeDtypeStruct((1,FF),F32)],
        scratch_shapes=[pltpu.VMEM((L,D),BF)]*4+[pltpu.VMEM((L,FF),BF)]*2+[pltpu.VMEM((bi,D),F32)],
        compiler_params=CP(),name="middle")(x,att,cot,wo,wi,wu,vec,b_inner)

def last_kernel(nb,bi,x_ref,dq_ref,dk_ref,dv_ref,dz_ref,em_ref,dr_ref,wq_ref,wk_ref,wv_ref,
        gi_ref,dwq_ref,dwk_ref,dwv_ref,dwp_ref,dbv_ref):
    t=pl.program_id(0)
    @pl.when(t<nb)
    def _():
        rows=pl.ds(pl.multiple_of(t*bi,bi),bi)
        gi_ref[...]=dz_ref[...]+dot(dq_ref[rows,:],wq_ref[...],NT)+dot(dk_ref[rows,:],wk_ref[...],NT)+dot(dv_ref[rows,:],wv_ref[...],NT)
    @pl.when(t==nb)
    def _(): dwq_ref[...]=dot(x_ref[...],dq_ref[...],TN).astype(BF)
    @pl.when(t==nb+1)
    def _(): dwk_ref[...]=dot(x_ref[...],dk_ref[...],TN).astype(BF)
    @pl.when(t==nb+2)
    def _():
        dwv_ref[...]=dot(x_ref[...],dv_ref[...],TN).astype(BF)
        dbv_ref[...]=rowsum(dv_ref[...].astype(F32))
    @pl.when(t==nb+3)
    def _(): dwp_ref[...]=dot(em_ref[...],dr_ref[...],TN).astype(BF)

def last(x,dq,dk,dv,dz1,em,dr,wq,wk,wv,bi=256):
    L,D=x.shape; nb=L//bi
    row=pl.BlockSpec((bi,D),lambda t:(jnp.minimum(t,nb-1),0))
    full=lambda s: pl.BlockSpec(s,lambda t:(0,0),pipeline_mode=ONE)
    o=pl.BlockSpec((D,D),lambda t:(0,0))
    W=jax.ShapeDtypeStruct((D,D),BF)
    return pl.pallas_call(functools.partial(last_kernel,nb,bi),grid=(nb+4,),
        in_specs=[full((L,D))]*4+[row,full((2*L,D)),full((2*L,D))]+[full((D,D))]*3,
        out_specs=[row,o,o,o,o,pl.BlockSpec((1,D),lambda t:(0,0))],
        out_shape=[jax.ShapeDtypeStruct((L,D),F32),W,W,W,W,jax.ShapeDtypeStruct((1,D),F32)],
        compiler_params=CP(),name="last")(x,dq,dk,dv,dz1,em,dr,wq,wk,wv)

def sinusoid(buckets,width):
    half=width//2; span=(buckets.shape[0]+1)//2
    rates=jnp.exp(jnp.arange(half,dtype=F32)*(-2.0*math.log(10000.0)/width))
    ang=(buckets-span).astype(F32)[:,None]*rates[None,:]
    return jnp.concatenate([jnp.sin(ang),jnp.cos(ang)],axis=1).astype(BF)

def layer(x,kinds,buckets,wq,wk,wv,bv,wp,bc,bp,bt,te,wo,bo,ga,sa,wi,b_i,wu,bu,gf,sf,cot):
    L,D=x.shape
    P=D//128
    em=sinusoid(jnp.concatenate([buckets,buckets[-1:]]) if False else buckets,D)
    em=jnp.concatenate([em,jnp.zeros((1,D),BF)])
    ln=jnp.arange(128)%64
    oh=((ln[None]%3==kinds[:,None])&(ln[None]<6)).astype(BF)
    f=lambda v: v.astype(F32)
    vec=jnp.stack([f(bc),f(bp),f(bt),f(te[0]),f(te[1])]+[jnp.zeros((D,),F32)]*3).reshape(8,P,128).transpose(1,0,2)
    q,k,v,r=project(x,em,wq,wk,wv,wp,f(bv)[None])
    e,att,linv=att_fwd(q,k,v,r,oh,vec)
    v2=jnp.stack([f(a) for a in (bo,ga,sa,bu,gf,sf)]+[jnp.zeros((D,),F32)]*2)
    out,dz1,datt,dwo,dwi,dwu,dvec2,dbi=middle(x,att,cot,wo,wi,wu,v2,f(b_i)[None])
    dq,dk,dv,dr,dvec=att_bwd(q,k,v,r,oh,vec,e,att,linv,datt)
    dvec=dvec.transpose(1,0,2).reshape(8,D)
    gi,dwq,dwk,dwv,dwp,dbv=last(x,dq,dk,dv,dz1,em,dr,wq,wk,wv)
    return (out,gi,dwq,dwk,dwv,dbv[0],dwp,dvec[0],dvec[1],dvec[2],dvec[3:5],dwo,dvec2[0],dvec2[1],dvec2[2],dwi,dbi[0],dwu,dvec2[3],dvec2[4],dvec2[5])

def local(inputs,token_types,buckets,wq,wk,wv,bv,wp,bc,bp,bt,te,wo,bo,ga,sa,wi,b_i,wu,bu,gf,sf,cot):
    s,D=wq.shape; n=D//s; FF=wi.shape[1]; fs=FF//n
    small=jnp.concatenate([bv,bc,bp,bt,te[0],te[1],bo,ga,sa,bu,gf,sf,b_i])
    nv=small.shape[0]; pad=-nv%D
    small=jnp.concatenate([small,jnp.zeros((pad,),BF)]).reshape(-1,D)
    first=lax.all_gather(jnp.concatenate([wq,wk,wv,wp,small]),"shard",axis=0,tiled=False)
    second=lax.all_gather(jnp.concatenate([wo,wi.reshape(s*FF//D,D),wu]),"shard",axis=0,tiled=False)
    part=lambda g,a,b: g[:,a:b].reshape(n*(b-a),D)
    gq,gk,gv,gp=[part(first,j*s,(j+1)*s) for j in range(4)]
    sm=first[:,4*s:].reshape(n,-1)[:,:nv]
    vs=sm[:,:12*s].reshape(n,12,s).transpose(1,0,2).reshape(12,D)
    fb=sm[:,12*s:].reshape(FF)
    k=s*FF//D
    go=part(second,0,s); gi_=second[:,s:s+k].reshape(D,FF); gu=part(second,s+k,s+k+fs)
    o=layer(inputs[0],token_types[0],buckets,gq,gk,gv,vs[0],gp,vs[1],vs[2],vs[3],vs[4:6],go,vs[6],vs[7],vs[8],gi_,fb,gu,vs[9],vs[10],vs[11],cot[0])
    (out,gin,dwq,dwk,dwv,dbv,dwp,dbc,dbp,dbt,dte,dwo,dbo,dga,dsa,dwi,dbi,dwu,dbu,dgf,dsf)=o
    blk=lambda a: a.reshape(n,-1,D)
    r1=jnp.concatenate([blk(dwo),blk(dwi),blk(dwu)],axis=1)
    dv=jnp.stack([dbv,dbc,dbp,dbt,dte[0],dte[1],dbo,dga,dsa,dbu,dgf,dsf]).reshape(12,n,s).transpose(1,0,2).reshape(n,12*s)
    dv=jnp.concatenate([dv,dbi.reshape(n,fs),jnp.zeros((n,pad),F32)],axis=1).astype(BF).reshape(n,-1,D)
    r2=jnp.concatenate([blk(dwq),blk(dwk),blk(dwv),blk(dwp),dv],axis=1)
    t1=lax.psum_scatter(r1,"shard",scatter_dimension=0,tiled=False).astype(F32)
    t1=lax.psum(t1,"rep")
    t2=lax.psum_scatter(r2,"shard",scatter_dimension=0,tiled=False).astype(F32)
    t2=lax.psum(t2,"rep")
    tv=t2[4*s:].reshape(-1)
    c=lambda j: tv[j*s:(j+1)*s]
    return (out[None],gin[None],t2[:s],t2[s:2*s],t2[2*s:3*s],c(0),t2[3*s:4*s],c(1),c(2),c(3),jnp.stack([c(4),c(5)]),
        t1[:s],c(6),c(7),c(8),t1[s:s+k].reshape(s,FF),tv[12*s:12*s+fs],t1[s+k:],c(9),c(10),c(11))

def solution(mesh):
    both=("rep","shard")
    v=P("shard"); w=P("shard",None); a3=P(both,None,None)
    in_specs=(a3,P(both,None),P(),w,w,w,v,w,v,v,v,P(None,"shard"),w,v,v,v,w,v,w,v,v,v,a3)
    out_specs=(a3,a3,w,w,w,v,w,v,v,v,P(None,"shard"),w,v,v,v,w,v,w,v,v,v)
    return jax.shard_map(local,mesh=mesh,in_specs=in_specs,out_specs=out_specs,check_vma=False)
```

```python
import functools, math
import jax, jax.numpy as jnp
from jax import lax
from jax.experimental import pallas as pl
from jax.experimental.pallas import tpu as pltpu
from jax.sharding import PartitionSpec as P
import numpy as np
F32=jnp.float32; BF=jnp.bfloat16
LOG2E=math.log2(math.e); LN2=math.log(2.0)
NT=(((1,),(1,)),((),())); NN=(((1,),(0,)),((),())); TN=(((0,),(0,)),((),()))
def dot(a,b,dims=NN): return lax.dot_general(a,b,dims,preferred_element_type=F32)

def shape_of(n):
    Z=4 if n%8==0 else 1
    return Z,n//(2*Z)

class Place:
    def __init__(self,n,R):
        self.n=n; self.R=R; self.rep=lax.axis_index("rep"); self.Z,self.X=shape_of(n)
        me=lax.axis_index("shard")
        self.me=me; self.c=lax.rem(me,2); q=lax.div(me,2)
        self.x=lax.rem(q,self.X); self.z=lax.div(q,self.X)
    def at(self,z,x,c): return (z*self.X+x)*2+c
    def neighbours(self):
        z,x,c=self.z,self.x,self.c
        out=[(None,self.at(z,x,1-c))]
        if self.Z>1: out+=[(z>0,self.at(z-1,x,c)),(z<self.Z-1,self.at(z+1,x,c))]
        if self.X>1: out+=[(x>0,self.at(z,x-1,c)),(x<self.X-1,self.at(z,x+1,c))]
        return out

def when(cond,fn):
    if cond is None: fn()
    else: pl.when(cond)(fn)

def both(*conds):
    out=None
    for k in conds:
        if k is not None: out=k if out is None else jnp.logical_and(out,k)
    return out

def greet(place):
    bar=pltpu.get_barrier_semaphore()
    total=jnp.int32(0)
    for ok,idx in place.neighbours():
        when(ok,lambda idx=idx: pl.semaphore_signal(bar,inc=1,device_id={"shard":idx},device_id_type=pl.DeviceIdType.MESH))
        total=total+(1 if ok is None else ok.astype(jnp.int32))
    for d in range(1,place.R):
        pl.semaphore_signal(bar,inc=1,device_id={"rep":lax.rem(place.rep+d,place.R)},device_id_type=pl.DeviceIdType.MESH)
    total=total+(place.R-1)
    pl.semaphore_wait(bar,total)

def gather_sems(n):
    Z,X=shape_of(n); A=1+2*(Z-1); J=1+2*(X-1)
    return [pltpu.SemaphoreType.DMA((max(1,2*(Z-1)),2)),pltpu.SemaphoreType.DMA((max(1,A*2*(X-1)),2)),pltpu.SemaphoreType.DMA((A*J,2))]

def gather_events(place,G,sems,t0,dz,dx,last):
    p=place; Z,X=p.Z,p.X; zs,xs,cs=sems
    z,x,c=p.z,p.x,p.c
    def copy(idx,sem,k,to):
        return pltpu.make_async_remote_copy(src_ref=G.at[idx],dst_ref=G.at[idx],send_sem=sem.at[k,0],recv_sem=sem.at[k,1],
            device_id={"shard":to},device_id_type=pl.DeviceIdType.MESH)
    ev=[]; sends=[]
    A=1+2*(Z-1); J=1+2*(X-1)
    def slot(a):
        if a==0: return z,None
        s=(a-1)//2
        return (z-1-s,z-1-s>=0) if a%2 else (z+1+s,z+1+s<Z)
    def col(j):
        if j==0: return x,None
        k=(j-1)//2
        return (x-1-k,x-1-k>=0) if j%2 else (x+1+k,x+1+k<X)
    def zmsg(d,s):
        lev=z-s if d==0 else z+s
        ok=both(z+1<Z,z-s>=0) if d==0 else both(z>0,z+s<Z)
        return ok,copy(p.at(lev,x,c),zs,2*s+d,p.at(z+1 if d==0 else z-1,x,c))
    def zarr(d,s):
        lev,ok=slot(1+2*s+d)
        return ok,copy(p.at(lev,x,c),zs,2*s+d,p.at(z,x,1-c))
    def xmsg(a,d,k):
        lev,va=slot(a)
        cx=x-k if d==0 else x+k
        ok=both(va,x+1<X,x-k>=0) if d==0 else both(va,x>0,x+k<X)
        return ok,copy(p.at(lev,cx,c),xs,(a*(X-1)+k)*2+d,p.at(lev*0+z,x+1 if d==0 else x-1,c))
    def xarr(a,d,k):
        lev,va=slot(a); cx,vc=col(1+2*k+d)
        return both(va,vc),copy(p.at(lev,cx,c),xs,(a*(X-1)+k)*2+d,p.at(z,x,1-c))
    def cmsg(a,j):
        lev,va=slot(a); cx,vc=col(j)
        return both(va,vc),copy(p.at(lev,cx,c),cs,a*J+j,p.at(z,x,1-c))
    def carr(a,j):
        lev,va=slot(a); cx,vc=col(j)
        return both(va,vc),copy(p.at(lev,cx,1-c),cs,a*J+j,p.at(z,x,1-c))
    def add(t,order,fn): ev.append((min(t,last),order,fn))
    def starter(ms):
        def fn():
            for ok,m in ms: when(ok,m.start)
        return fn
    def waiter(ms):
        def fn():
            for ok,m in ms: when(ok,m.wait_recv)
        return fn
    for s in range(Z):
        t=t0+s*dz
        if s>0: add(t,(0,s,0),waiter([zarr(d,s-1) for d in range(2)]))
        if s<Z-1:
            ms=[zmsg(d,s) for d in range(2)]; sends+=ms
            add(t,(0,s,1),starter(ms))
    for a in range(A):
        ra=(a+1)//2; ta=t0+ra*dz
        for k in range(X):
            t=ta+k*dx
            if k>0: add(t,(1,k,a,0),waiter([xarr(a,d,k-1) for d in range(2)]))
            if k<X-1:
                ms=[xmsg(a,d,k) for d in range(2)]; sends+=ms
                add(t,(1,k,a,1),starter(ms))
            ms=[cmsg(a,j) for j in range(J) if (j+1)//2==k]; sends+=ms
            add(t,(1,k,a,2),starter(ms))
    add(last,(2,),waiter([carr(a,j) for a in range(A) for j in range(J)]))
    def done():
        for ok,m in sends: when(ok,m.wait_send)
    add(last,(3,),done)
    ev.sort(key=lambda e:(e[0],e[1]))
    return ev

def square_sems(n):
    Z,X=shape_of(n); A=1+2*(Z-1)
    return [pltpu.SemaphoreType.DMA((2*(Z-1),2)),pltpu.SemaphoreType.DMA((A,2)),pltpu.SemaphoreType.DMA((A,2)),pltpu.SemaphoreType.DMA((3*A,2))]

def square_events(place,G,sems,t0,dz,dx,dy,last):
    p=place; Z=p.Z; zs,xs,ys,cs=sems
    z,x,c,rep=p.z,p.x,p.c,p.rep
    parts=G.shape[1]; cut=(parts+1)//2
    halves=((0,cut),(cut,parts-cut))
    A=1+2*(Z-1)
    def copy(idx,part,sem,k,to):
        ref=G.at[idx] if part is None else G.at[idx,pl.ds(*halves[part])]
        return pltpu.make_async_remote_copy(src_ref=ref,dst_ref=ref,send_sem=sem.at[k,0],recv_sem=sem.at[k,1],
            device_id=to,device_id_type=pl.DeviceIdType.MESH)
    def slot(a):
        if a==0: return z,None
        s=(a-1)//2
        return (z-1-s,z-1-s>=0) if a%2 else (z+1+s,z+1+s<Z)
    other={"shard":p.at(z,x,1-c)}; across={"shard":p.at(z,1-x,c)}; above={"rep":1-rep}
    def zmsg(d,s):
        lev=z-s if d==0 else z+s
        ok=both(z+1<Z,z-s>=0) if d==0 else both(z>0,z+s<Z)
        return ok,copy(p.at(lev,x,c),None,zs,2*s+d,{"shard":p.at(z+1 if d==0 else z-1,x,c)})
    def zarr(d,s):
        lev,ok=slot(1+2*s+d)
        return ok,copy(p.at(lev,x,c),None,zs,2*s+d,other)
    def xmsg(a,h):
        lev,va=slot(a)
        return both(va,rep==h),copy(p.at(lev,x,c),h,xs,a,across)
    def xarr(a,h):
        lev,va=slot(a)
        return both(va,rep==h),copy(p.at(lev,1-x,c),h,xs,a,across)
    def ymsg(a,h):
        lev,va=slot(a)
        return both(va,rep==h),copy(p.at(lev,1-x,c),h,ys,a,above)
    def yarr(a,h):
        lev,va=slot(a)
        return both(va,rep==1-h),copy(p.at(lev,1-x,c),h,ys,a,above)
    def cmsg(a,h,core):
        lev,va=slot(a); cc=c if core==0 else 1-c
        if h is None: return [(va,copy(p.at(lev,x,cc),None,cs,3*a,other))]
        return [(both(va,rep==(g if h==0 else 1-g)),copy(p.at(lev,1-x,cc),g,cs,3*a+1+h,other)) for g in range(2)]
    ev=[]; sends=[]
    def add(t,order,fn): ev.append((min(t,last),order,fn))
    def start(t,order,ms):
        sends.extend(ms)
        def fn():
            for ok,m in ms: when(ok,m.start)
        add(t,order,fn)
    def await_(t,order,ms):
        def fn():
            for ok,m in ms: when(ok,m.wait_recv)
        add(t,order,fn)
    for s in range(Z):
        t=t0+s*dz
        if s>0: await_(t,(0,s,0),[zarr(d,s-1) for d in range(2)])
        if s<Z-1: start(t,(0,s,1),[zmsg(d,s) for d in range(2)])
        for a in ([0] if s==0 else [2*s-1,2*s]):
            start(t,(1,s,a),[xmsg(a,h) for h in range(2)]+cmsg(a,None,0))
            await_(t+dx,(2,s,a,0),[xarr(a,h) for h in range(2)])
            start(t+dx,(2,s,a,1),[ymsg(a,h) for h in range(2)]+cmsg(a,0,0))
            await_(t+dx+dy,(3,s,a,0),[yarr(a,h) for h in range(2)])
            start(t+dx+dy,(3,s,a,1),cmsg(a,1,0))
    await_(last,(4,),[m for a in range(A) for h in (None,0,1) for m in cmsg(a,h,1)])
    def done():
        for ok,m in sends: when(ok,m.wait_send)
    add(last,(5,),done)
    ev.sort(key=lambda e:(e[0],e[1]))
    return ev

def is_square(n,R): return R==2 and shape_of(n)==(4,2)
def spread_sems(n,R): return square_sems(n) if is_square(n,R) else gather_sems(n)
def spread_events(place,G,sems,t0,dz,dx,dy,last):
    if is_square(place.n,place.R): return square_events(place,G,sems,t0,dz,dx,dy,last)
    return gather_events(place,G,sems,t0,dz,dx,last)

def run_events(step,events):
    times=sorted({e[0] for e in events})
    for t in times:
        fns=[e[2] for e in events if e[0]==t]
        def fire(fns=fns):
            for f in fns: f()
        pl.when(step==t)(fire)

STRIDE=32
def tables(length,width):
    half=width//2; count=2*length//STRIDE
    rates=np.exp(np.arange(half)*(-2.0*math.log(10000.0)/width))
    def pack(angles):
        full=np.concatenate([np.sin(angles),np.cos(angles)],axis=1).astype(np.float32)
        hi=full.astype(jnp.bfloat16); lo=(full-hi.astype(np.float32)).astype(jnp.bfloat16)
        return np.concatenate([hi,lo],axis=0)
    coarse=(np.arange(count)*STRIDE-length)[:,None]*rates[None]
    fine=np.arange(STRIDE)[:,None]*rates[None]
    return pack(coarse),pack(fine)

def front_kernel(n,R,wq_ref,wk_ref,wv_ref,wp_ref,small_ref,kinds_ref,buckets_ref,ta_ref,tb_ref,
        g_ref,vec_ref,bi_ref,em_ref,oh_ref,all_s,mine,own,ssem,*sems):
    place=Place(n,R); me=place.me
    ws=(wq_ref,wk_ref,wv_ref,wp_ref)
    owns=[pltpu.make_async_copy(w,mine.at[j],own.at[j]) for j,w in enumerate(ws)]
    keep=pltpu.make_async_copy(mine,g_ref.at[me],own.at[4])
    for m in owns: m.start()
    bar=pltpu.get_barrier_semaphore()
    def hello(d,_):
        pl.semaphore_signal(bar,inc=1,device_id={"shard":lax.rem(me+d,n)},device_id_type=pl.DeviceIdType.MESH)
        return 0
    lax.fori_loop(1,n,hello,0)
    for d in range(1,R):
        pl.semaphore_signal(bar,inc=1,device_id={"rep":lax.rem(place.rep+d,R)},device_id_type=pl.DeviceIdType.MESH)
    all_s[me]=small_ref[...]
    for m in owns: m.wait()
    keep.start()
    pl.semaphore_wait(bar,n+R-2)
    keep.wait()
    def send(d):
        return pltpu.make_async_remote_copy(src_ref=all_s.at[me],dst_ref=all_s.at[me],send_sem=ssem.at[d,0],recv_sem=ssem.at[d,1],
            device_id={"shard":lax.rem(me+d,n)},device_id_type=pl.DeviceIdType.MESH)
    def arrive(d):
        w=lax.rem(me-d+n,n)
        return pltpu.make_async_remote_copy(src_ref=all_s.at[w],dst_ref=all_s.at[w],send_sem=ssem.at[d,0],recv_sem=ssem.at[d,1],
            device_id={"shard":lax.rem(me+d,n)},device_id_type=pl.DeviceIdType.MESH)
    def prepare():
        def go(d,_):
            send(d).start()
            return 0
        lax.fori_loop(1,n,go,0)
        L2=buckets_ref.shape[1]; L=L2//2
        count=L2//STRIDE
        def body(j,_):
            rows=pl.ds(pl.multiple_of(j*256,256),256)
            b=buckets_ref[:,rows]
            hot=lambda v,m: jnp.where(v==lax.rem(lax.broadcasted_iota(jnp.int32,(2*m,256),0),m),1.0,0.0).astype(BF)
            A=dot(hot(lax.div(b,STRIDE),count),ta_ref[...],TN)
            B=dot(hot(lax.rem(b,STRIDE),STRIDE),tb_ref[...],TN)
            h=A.shape[1]//2
            sa,ca,sb,cb=A[:,:h],A[:,h:],B[:,:h],B[:,h:]
            em_ref[rows,:]=jnp.concatenate([sa*cb+ca*sb,ca*cb-sa*sb],axis=1).astype(BF)
            return 0
        lax.fori_loop(0,L2//256,body,0)
        for j in range(L//256):
            kinds=kinds_ref[:,j*256:(j+1)*256]
            lane=lax.rem(lax.broadcasted_iota(jnp.int32,(128,256),0),64)
            hot=jnp.where((lax.rem(lane,3)==kinds)&(lane<6),1.0,0.0)
            oh_ref[j*256:(j+1)*256,:]=hot.T.astype(BF)
        def come(d,_):
            arrive(d).wait_recv()
            send(d).wait_send()
            return 0
        lax.fori_loop(1,n,come,0)
        s=wq_ref.shape[0]; fs=bi_ref.shape[1]//n
        for w in range(n):
            a=all_s[w].astype(F32)
            vec_ref[:,w*s:(w+1)*s]=a[:,:s]
            bi_ref[:,w*fs:(w+1)*fs]=a[14:15,:fs]
    ev=spread_events(place,g_ref,sems,0,1,1,1,99)
    ev=sorted(ev+[(0,(9,),prepare)],key=lambda e:(e[0],e[1]))
    for e in ev: e[2]()

def front(R,wq,wk,wv,wp,small,kinds,buckets,FF):
    s,D=wq.shape; n=D//s; L=kinds.shape[1]; SL=small.shape[1]
    ta,tb=tables(L,D)
    hbm=pl.BlockSpec(memory_space=pl.ANY); vm=pl.BlockSpec(memory_space=pltpu.VMEM)
    return pl.pallas_call(functools.partial(front_kernel,n,R),
        in_specs=[hbm]*4+[vm]*5,out_specs=[hbm]+[vm]*4,
        out_shape=[jax.ShapeDtypeStruct((n,4,s,D),BF),jax.ShapeDtypeStruct((16,D),F32),jax.ShapeDtypeStruct((1,FF),F32),
            jax.ShapeDtypeStruct((2*L,D),BF),jax.ShapeDtypeStruct((L,128),BF)],
        scratch_shapes=[pltpu.VMEM((n,16,SL),BF),pltpu.VMEM((4,s,D),BF),pltpu.SemaphoreType.DMA((5,)),pltpu.SemaphoreType.DMA((n,2))]+spread_sems(n,R),
        compiler_params=CP(collective_id=0,has_side_effects=True),name="front")(wq,wk,wv,wp,small,kinds,buckets,jnp.asarray(ta),jnp.asarray(tb))

BI=256


def lane_half(rows, lanes):
    lane=lax.broadcasted_iota(jnp.int32,(rows,lanes),1)
    return (lane//64)%2

def split_hi_lo(v):
    hi=v.astype(BF); return hi,(v-hi.astype(F32)).astype(BF)

def queries(q, vec, oh):
    s=0.125*LOG2E
    cq=((q+vec[0:1])*s).astype(BF)
    pq=((q+vec[1:2])*s).astype(BF)
    tq=(q+vec[2:3])*0.125
    return cq,pq,tq

def fwd_kernel(n,R,roll_bf,q_ref,k_ref,v_ref,r_ref,oh_ref,vec_ref,wo_ref,wi_ref,wu_ref,e_ref,att_ref,linv_ref,g_ref,mine,own,*sems):
    bi=q_ref.shape[0]; L=k_ref.shape[0]; W=L+bi
    i=pl.program_id(1); nb=L//bi
    step=pl.program_id(0)*nb+i; steps=6*nb
    place=Place(n,R)
    kk=wu_ref.shape[0]; D=wo_ref.shape[1]
    owns=[pltpu.make_async_copy(wu_ref,mine.at[pl.ds(0,kk)],own.at[0]),pltpu.make_async_copy(wo_ref,mine.at[kk],own.at[1])]
    owns+=[pltpu.make_async_copy(wi_ref.at[:,pl.ds(j*D,D)],mine.at[kk+1+j],own.at[2+j]) for j in range(kk)]
    keep=pltpu.make_async_copy(mine,g_ref.at[place.me],own.at[2+kk])
    def enter():
        for m in owns: m.start()
        for m in owns: m.wait()
        keep.start()
        greet(place)
        keep.wait()
    run_events(step,[(0,(-1,),enter)]+spread_events(place,g_ref,sems,0,7,4,4,steps-1))
    vec=vec_ref[...]
    q=q_ref[...]
    oh_i=oh_ref[pl.ds(pl.multiple_of(i*bi,bi),bi),:]
    cq,pq,tq=queries(q,vec,None)
    rr=lax.broadcasted_iota(jnp.int32,(256,128),0)%128
    cc=lax.broadcasted_iota(jnp.int32,(256,128),1)
    M=jnp.where((rr//64==cc//64)&(cc%64<6),1.0,0.0).astype(BF)
    def tt(te):
        hi,lo=split_hi_lo(tq*(te*LOG2E))
        return dot(jnp.concatenate([hi,lo],axis=1),M)
    t0=tt(vec[3:4]); t1=tt(vec[4:5])
    tv=jnp.where(oh_i>0,t1,t0)
    hi=tv.astype(BF).astype(F32)
    lane=lax.broadcasted_iota(jnp.int32,(bi,128),1)
    tv=jnp.where(lane%64<3,hi,tv-hi).astype(BF)
    half=lane_half(bi,128)
    kext=jnp.concatenate([k_ref[...],oh_ref[...]],axis=1)
    vext=jnp.concatenate([v_ref[...],jnp.ones((L,128),BF)],axis=1)
    w0=pl.multiple_of(L-bi-i*bi,bi)
    rwin=r_ref[pl.ds(w0,W),:]
    z=jnp.zeros((),BF)
    outs=[]
    for h in range(2):
        qx=jnp.concatenate([jnp.where(half==h,cq,z),jnp.where(half==h,tv,z)],axis=1)
        pos=dot(jnp.where(half==h,pq,z),rwin,NT)
        if roll_bf: pos=pos.astype(BF)
        pos=pltpu.roll(pos,W-(bi-1),1,stride=1,stride_axis=0)[:,:L]
        s=dot(qx,kext,NT)+pos.astype(F32)
        m=jnp.max(s,axis=1,keepdims=True)
        e=jnp.exp2(s-m).astype(BF)
        e_ref[h]=e
        o=dot(e,vext)
        li=1.0/o[:,128:]
        outs.append((o[:,:128]*li,li))
    att_ref[...]=jnp.where(half==0,outs[0][0],outs[1][0]).astype(BF)
    linv_ref[...]=jnp.where(half==0,outs[0][1],outs[1][1])

def att_fwd(R,q,k,v,r,oh,vec,wo,wi,wu,bi=BI,roll_bf=False):
    L,D=q.shape; P=D//128; nb=L//bi; s=wo.shape[0]; n=D//s; kk=wu.shape[0]//s
    hbm=pl.BlockSpec(memory_space=pl.ANY)
    return pl.pallas_call(functools.partial(fwd_kernel,n,R,roll_bf),
        grid=(P,nb),
        in_specs=[pl.BlockSpec((bi,128),lambda p,i:(i,p)),
            pl.BlockSpec((L,128),lambda p,i:(0,p)),
            pl.BlockSpec((L,128),lambda p,i:(0,p)),
            pl.BlockSpec((2*L,128),lambda p,i:(0,p)),
            pl.BlockSpec((L,128),lambda p,i:(0,0)),
            pl.BlockSpec((8,128),lambda p,i:(0,p)),hbm,hbm,hbm],
        out_specs=[pl.BlockSpec((2,bi,L),lambda p,i:(p,i,0)),
            pl.BlockSpec((bi,128),lambda p,i:(i,p)),
            pl.BlockSpec((bi,128),lambda p,i:(i,p)),hbm],
        out_shape=[jax.ShapeDtypeStruct((2*P,L,L),BF),jax.ShapeDtypeStruct((L,D),BF),jax.ShapeDtypeStruct((L,D),F32),
            jax.ShapeDtypeStruct((n,2*kk+1,s,D),BF)],
        scratch_shapes=[pltpu.VMEM((2*kk+1,s,D),BF),pltpu.SemaphoreType.DMA((3+kk,))]+spread_sems(n,R),
        compiler_params=pltpu.CompilerParams(vmem_limit_bytes=56*2**20,dimension_semantics=("arbitrary","arbitrary"),collective_id=1,has_side_effects=True),
        name="attend")(q,k,v,r,oh,vec,wo,wi,wu.reshape(kk,s,D))

def bwd_kernel(roll_bf,q_ref,k_ref,v_ref,r_ref,oh_ref,vec_ref,e_ref,att_ref,linv_ref,datt_ref,
               dq_ref,dk_ref,dv_ref,dr_ref,dvec_ref, dk_acc,dv_acc,dr_acc):
    bi=q_ref.shape[0]; L=k_ref.shape[0]; W=L+bi
    i=pl.program_id(1); nb=pl.num_programs(1)
    vec=vec_ref[...]
    q=q_ref[...]
    oh_i=oh_ref[pl.ds(pl.multiple_of(i*bi,bi),bi),:].astype(F32)
    cq,pq,tq=queries(q,vec,None)
    half=lane_half(bi,128)
    lane=lax.broadcasted_iota(jnp.int32,(bi,128),1)
    @pl.when(i==0)
    def _():
        dk_acc[...]=jnp.zeros_like(dk_acc); dv_acc[...]=jnp.zeros_like(dv_acc); dr_acc[...]=jnp.zeros_like(dr_acc)
        dvec_ref[...]=jnp.zeros_like(dvec_ref)
    P=jnp.where(lax.broadcasted_iota(jnp.int32,(bi,bi),0)+lax.broadcasted_iota(jnp.int32,(bi,bi),1)==bi-1,1.0,0.0).astype(BF)
    pqr=dot(P,pq).astype(BF)
    kext=jnp.concatenate([k_ref[...],oh_ref[...]],axis=1)
    ones2=jnp.where(lax.broadcasted_iota(jnp.int32,(L,128),1)<2,1.0,0.0).astype(BF)
    vext=jnp.concatenate([v_ref[...],ones2],axis=1)
    w0=pl.multiple_of(L-bi-i*bi,bi)
    rwin=r_ref[pl.ds(w0,W),:]
    z=jnp.zeros((),BF)
    dattl=datt_ref[...].astype(F32)*linv_ref[...]
    prod=dattl*att_ref[...].astype(F32)
    dattl=dattl.astype(BF)
    dcs=[];dps=[];dts=[];tes=[]
    dk=None; dv=None; dr=None
    for h in range(2):
        delta=-jnp.sum(jnp.where(half==h,prod,0.0),axis=1,keepdims=True)
        dhi=delta.astype(BF).astype(F32)
        dx=jnp.where(lane==0,dhi,jnp.where(lane==1,delta-dhi,0.0)).astype(BF)
        dm=jnp.where(half==h,dattl,z)
        dpd=dot(jnp.concatenate([dm,dx],axis=1),vext,NT)
        e=e_ref[h]
        ds=(e.astype(F32)*dpd).astype(BF)
        dvh=dot(e,dm,TN)
        dkh=dot(ds,jnp.where(half==h,cq,z),TN)
        dc=dot(ds,kext)
        rev=dot(P,ds)
        if roll_bf: rev=rev.astype(BF)
        rev=jnp.concatenate([rev,jnp.zeros((bi,W-L),rev.dtype)],axis=1)
        dpr=pltpu.roll(rev,0,1,stride=1,stride_axis=0).astype(BF)
        dp=dot(dpr,rwin)
        drh=dot(dpr,jnp.where(half==h,pqr,z),TN)
        dv=dvh if dv is None else dv+dvh
        dk=dkh if dk is None else dk+dkh
        dr=drh if dr is None else dr+drh
        D=jnp.where(lane<3,dc[:,128:],0.0)
        dall=jnp.sum(D,axis=1,keepdims=True)
        d1=jnp.sum(D*oh_i,axis=1,keepdims=True)
        d0=dall-d1
        dcs.append(dc[:,:128]); dps.append(dp)
        dts.append(d0*vec[3:4]+d1*vec[4:5])
        tes.append((d0,d1))
    dv_acc[...]+=dv
    dk_acc[...]+=dk
    dr_acc[pl.ds(w0,W),:]+=dr
    dcq=jnp.where(half==0,dcs[0],dcs[1]).astype(BF).astype(F32)
    dpr=jnp.where(half==0,dps[0],dps[1]).astype(BF)
    dpq=dot(P,dpr)
    dtq=jnp.where(half==0,dts[0],dts[1])
    dq_ref[...]=((dcq+dpq+dtq)*0.125).astype(BF)
    d0=jnp.where(half==0,tes[0][0],tes[1][0]); d1=jnp.where(half==0,tes[0][1],tes[1][1])
    rows=[dcq*0.125,dpq*0.125,dtq*0.125,d0*tq,d1*tq]
    sums=[jnp.sum(v,axis=0,keepdims=True) for v in rows]+[jnp.zeros((3,128),F32)]
    dvec_ref[...]+=jnp.concatenate(sums,axis=0)
    @pl.when(i==nb-1)
    def _():
        dk_ref[...]=(dk_acc[...]*LN2).astype(BF)
        dv_ref[...]=dv_acc[...].astype(BF)
        dr_ref[...]=(dr_acc[...]*LN2).astype(BF)

def att_bwd(q,k,v,r,oh,vec,e,att,linv,datt,bi=BI,roll_bf=False):
    L,D=q.shape; P=D//128; nb=L//bi
    return pl.pallas_call(functools.partial(bwd_kernel,roll_bf),
        grid=(P,nb),
        in_specs=[pl.BlockSpec((bi,128),lambda p,i:(i,p)),
            pl.BlockSpec((L,128),lambda p,i:(0,p)),
            pl.BlockSpec((L,128),lambda p,i:(0,p)),
            pl.BlockSpec((2*L,128),lambda p,i:(0,p)),
            pl.BlockSpec((L,128),lambda p,i:(0,0)),
            pl.BlockSpec((8,128),lambda p,i:(0,p)),
            pl.BlockSpec((2,bi,L),lambda p,i:(p,i,0)),
            pl.BlockSpec((bi,128),lambda p,i:(i,p)),
            pl.BlockSpec((bi,128),lambda p,i:(i,p)),
            pl.BlockSpec((bi,128),lambda p,i:(i,p))],
        out_specs=[pl.BlockSpec((bi,128),lambda p,i:(i,p)),
            pl.BlockSpec((L,128),lambda p,i:(0,p)),
            pl.BlockSpec((L,128),lambda p,i:(0,p)),
            pl.BlockSpec((2*L,128),lambda p,i:(0,p)),
            pl.BlockSpec((8,128),lambda p,i:(0,p))],
        out_shape=[jax.ShapeDtypeStruct((L,D),BF),jax.ShapeDtypeStruct((L,D),BF),jax.ShapeDtypeStruct((L,D),BF),
            jax.ShapeDtypeStruct((2*L,D),BF),jax.ShapeDtypeStruct((8,D),F32)],
        scratch_shapes=[pltpu.VMEM((L,128),F32),pltpu.VMEM((L,128),F32),pltpu.VMEM((2*L,128),F32)],
        compiler_params=pltpu.CompilerParams(vmem_limit_bytes=56*2**20,dimension_semantics=("arbitrary","arbitrary")),
        name="attend_back")(q,k,v,r,oh,vec,e,att,linv,datt)

CP=lambda **k: pltpu.CompilerParams(vmem_limit_bytes=60*2**20,**k)
C0=math.sqrt(2.0/math.pi); C1=0.044715
EPS=1e-6
ONE=pl.Buffered(1)

def whole(ref):
    a=ref[...]
    return a.reshape(-1,a.shape[-1])

def proj_kernel(x_ref,em_ref,wq_ref,wk_ref,wv_ref,wp_ref,vec_ref,q_ref,k_ref,v_ref,r_ref):
    x=x_ref[...]
    q_ref[...]=dot(x,whole(wq_ref))
    k_ref[...]=dot(x,whole(wk_ref)).astype(BF)
    v_ref[...]=(dot(x,whole(wv_ref))+vec_ref[5:6,:]).astype(BF)
    r_ref[...]=dot(em_ref[...],whole(wp_ref)).astype(BF)

def project(x,em,g,vec,bi=256):
    L,D=x.shape; nb=L//bi; n,_,s,_=g.shape
    w=[pl.BlockSpec((n,1,s,D),lambda i,j=j:(0,j,0,0),pipeline_mode=ONE) for j in range(4)]
    row=pl.BlockSpec((bi,D),lambda i:(i,0)); row2=pl.BlockSpec((2*bi,D),lambda i:(i,0))
    return pl.pallas_call(proj_kernel,grid=(nb,),
        in_specs=[row,row2]+w+[pl.BlockSpec((8,D),lambda i:(0,0))],
        out_specs=[row,row,row,row2],
        out_shape=[jax.ShapeDtypeStruct((L,D),F32),jax.ShapeDtypeStruct((L,D),BF),jax.ShapeDtypeStruct((L,D),BF),jax.ShapeDtypeStruct((2*L,D),BF)],
        compiler_params=CP(),name="project")(x,em,g,g,g,g,vec)

def ln_stats(z):
    n=z.shape[1]
    mu=jnp.sum(z,axis=1,keepdims=True)*(1.0/n)
    c=z-mu
    var=jnp.sum(c*c,axis=1,keepdims=True)*(1.0/n)
    r=lax.rsqrt(var+EPS)
    return c*r,r

def ln_back(g,zhat,r):
    n=g.shape[1]
    a=jnp.sum(g,axis=1,keepdims=True)*(1.0/n)
    b=jnp.sum(g*zhat,axis=1,keepdims=True)*(1.0/n)
    return r*(g-a-zhat*b)

def rowsum(v): return jnp.sum(v,axis=0,keepdims=True)

def mid_kernel(nb,bi,nc,x_ref,att_ref,cot_ref,wo_ref,wu_ref,*rest):
    wi_refs=rest[:nc]
    (vec_ref,bi_ref,out_ref,dz1_ref,datt_ref,dwo_ref,dwi_ref,dwu_ref,dvec_ref,dbi_ref,
        mid_s,att_s,dffn_s,dattn_s,hid_s,din_s,acc_s)=rest[nc:]
    t=pl.program_id(0)
    D=x_ref.shape[1]; fc=D
    n=wu_ref.shape[0]; per=n//nc
    wu=lambda c: wu_ref[c*per:(c+1)*per].reshape(fc,D)
    wi=lambda c: whole(wi_refs[c])
    @pl.when(t==0)
    def _():
        dvec_ref[...]=jnp.zeros_like(dvec_ref); dbi_ref[...]=jnp.zeros_like(dbi_ref)
    @pl.when(t<nb)
    def _():
        rows=pl.ds(pl.multiple_of(t*bi,bi),bi)
        b_out,ga,sa,b_outer,gf,sf=[vec_ref[k:k+1,:] for k in range(6)]
        att=att_ref[...]
        att_s[rows,:]=att
        z1=x_ref[...].astype(F32)+dot(att,whole(wo_ref))+b_out
        zh1,r1=ln_stats(z1)
        middle=zh1*ga+sa
        mid=middle.astype(BF)
        mid_s[rows,:]=mid
        acc_s[...]=middle+b_outer
        for c in range(nc):
            cs=slice(c*fc,(c+1)*fc)
            v=dot(mid,wi(c))+bi_ref[:,cs]
            u=v*v
            th=jnp.tanh(v*(C0+(C0*C1)*u))
            hv=0.5*v
            hid=(hv+hv*th).astype(BF)
            dg=0.5+0.5*th+hv*(1.0-th*th)*(C0+(3*C0*C1)*u)
            hid_s[rows,cs]=hid
            din_s[rows,cs]=dg.astype(BF)
            acc_s[...]+=dot(hid,wu(c))
        zh2,r2=ln_stats(acc_s[...])
        out_ref[...]=(zh2*gf+sf).astype(BF)
        g=cot_ref[...].astype(F32)
        dz2=ln_back(g*gf,zh2,r2)
        dffn=dz2.astype(BF)
        dffn_s[rows,:]=dffn
        acc_s[...]=dz2
        dbs=[]
        for c in range(nc):
            cs=slice(c*fc,(c+1)*fc)
            dh=dot(dffn,wu(c),NT)
            din=(dh*din_s[rows,cs].astype(F32)).astype(BF)
            din_s[rows,cs]=din
            dbi_ref[:,cs]+=rowsum(din.astype(F32))
            acc_s[...]+=dot(din,wi(c),NT)
        dm=acc_s[...]
        dz1=ln_back(dm*ga,zh1,r1)
        dz1_ref[...]=dz1
        dattn=dz1.astype(BF)
        dattn_s[rows,:]=dattn
        datt_ref[...]=dot(dattn,whole(wo_ref),NT).astype(BF)
        dvec_ref[...]+=jnp.concatenate([rowsum(dz1),rowsum(dm*zh1),rowsum(dm),rowsum(dz2),rowsum(g*zh2),rowsum(g),jnp.zeros((2,D),F32)],axis=0)
    @pl.when(t==nb)
    def _():
        dwo_ref[...]=dot(att_s[...],dattn_s[...],TN).astype(BF).reshape(dwo_ref.shape)
    for c in range(nc):
        cs=slice(c*fc,(c+1)*fc)
        @pl.when(t==nb+c)
        def _():
            dwi_ref[...]=dot(mid_s[...],din_s[:,cs],TN).astype(BF).reshape(dwi_ref.shape)
            dwu_ref[...]=dot(hid_s[:,cs],dffn_s[...],TN).astype(BF).reshape(dwu_ref.shape)

def middle(x,att,cot,g,vec,b_inner,bi=256):
    L,D=x.shape; n,parts,s,_=g.shape; nc=(parts-1)//2; FF=nc*D; nb=L//bi; per=n//nc
    row=pl.BlockSpec((bi,D),lambda t:(jnp.minimum(t,nb-1),0))
    cc=lambda t: jnp.clip(t-nb,0,nc-1)
    w=lambda j: pl.BlockSpec((n,1,s,D),lambda t:(0,j,0,0),pipeline_mode=ONE)
    return pl.pallas_call(functools.partial(mid_kernel,nb,bi,nc),grid=(nb+nc,),
        in_specs=[row,row,row,w(nc),pl.BlockSpec((n,nc,s,D),lambda t:(0,0,0,0),pipeline_mode=ONE)]+[w(nc+1+j) for j in range(nc)]
            +[pl.BlockSpec((8,D),lambda t:(1,0)),pl.BlockSpec((1,FF),lambda t:(0,0))],
        out_specs=[row,row,row,pl.BlockSpec((n,s,D),lambda t:(0,0,0)),pl.BlockSpec((n,1,s,D),lambda t:(0,cc(t),0,0)),
            pl.BlockSpec((per,nc,s,D),lambda t:(cc(t),0,0,0)),
            pl.BlockSpec((8,D),lambda t:(0,0)),pl.BlockSpec((1,FF),lambda t:(0,0))],
        out_shape=[jax.ShapeDtypeStruct((L,D),BF),jax.ShapeDtypeStruct((L,D),F32),jax.ShapeDtypeStruct((L,D),BF),
            jax.ShapeDtypeStruct((n,s,D),BF),jax.ShapeDtypeStruct((n,nc,s,D),BF),jax.ShapeDtypeStruct((n,nc,s,D),BF),
            jax.ShapeDtypeStruct((8,D),F32),jax.ShapeDtypeStruct((1,FF),F32)],
        scratch_shapes=[pltpu.VMEM((L,D),BF)]*4+[pltpu.VMEM((L,FF),BF)]*2+[pltpu.VMEM((bi,D),F32)],
        compiler_params=CP(),name="middle")(x,att,cot,*([g]*(2+nc)),vec,b_inner)

def last_kernel(nb,bi,x_ref,dq_ref,dk_ref,dv_ref,dz_ref,em_ref,dr_ref,wq_ref,wk_ref,wv_ref,
        gi_ref,dwq_ref,dwk_ref,dwv_ref,dwp_ref,dbv_ref):
    t=pl.program_id(0)
    @pl.when(t<nb)
    def _():
        rows=pl.ds(pl.multiple_of(t*bi,bi),bi)
        gi_ref[...]=dz_ref[...]+dot(dq_ref[rows,:],whole(wq_ref),NT)+dot(dk_ref[rows,:],whole(wk_ref),NT)+dot(dv_ref[rows,:],whole(wv_ref),NT)
    @pl.when(t==nb)
    def _(): dwq_ref[...]=dot(x_ref[...],dq_ref[...],TN).astype(BF)
    @pl.when(t==nb+1)
    def _(): dwk_ref[...]=dot(x_ref[...],dk_ref[...],TN).astype(BF)
    @pl.when(t==nb+2)
    def _():
        dwv_ref[...]=dot(x_ref[...],dv_ref[...],TN).astype(BF)
        dbv_ref[...]=rowsum(dv_ref[...].astype(F32))
    @pl.when(t==nb+3)
    def _(): dwp_ref[...]=dot(em_ref[...],dr_ref[...],TN).astype(BF)

def last(x,dq,dk,dv,dz1,em,dr,g,bi=256):
    L,D=x.shape; nb=L//bi; n,_,s,_=g.shape
    w=[pl.BlockSpec((n,1,s,D),lambda t,j=j:(0,j,0,0),pipeline_mode=ONE) for j in range(3)]
    row=pl.BlockSpec((bi,D),lambda t:(jnp.minimum(t,nb-1),0))
    full=lambda s: pl.BlockSpec(s,lambda t:(0,0),pipeline_mode=ONE)
    o=pl.BlockSpec((D,D),lambda t:(0,0))
    W=jax.ShapeDtypeStruct((D,D),BF)
    return pl.pallas_call(functools.partial(last_kernel,nb,bi),grid=(nb+4,),
        in_specs=[full((L,D))]*4+[row,full((2*L,D)),full((2*L,D))]+w,
        out_specs=[row,o,o,o,o,pl.BlockSpec((1,D),lambda t:(0,0))],
        out_shape=[jax.ShapeDtypeStruct((L,D),F32),W,W,W,W,jax.ShapeDtypeStruct((1,D),F32)],
        compiler_params=CP(),name="last")(x,dq,dk,dv,dz1,em,dr,g,g,g)


def local(R,inputs,token_types,buckets,wq,wk,wv,bv,wp,bc,bp,bt,te,wo,bo,ga,sa,wi,b_i,wu,bu,gf,sf,cot):
    s,D=wq.shape; n=D//s; FF=wi.shape[1]; fs=FF//n; kk=FF//D
    SL=-(-max(s,fs)//128)*128
    z=jnp.zeros((s,),BF)
    wide=lambda a: jnp.pad(a,((0,0),(0,SL-a.shape[1])))
    small=jnp.concatenate([wide(jnp.stack([bc,bp,bt,te[0],te[1],bv,z,z,bo,ga,sa,bu,gf,sf])),wide(b_i[None]),jnp.zeros((1,SL),BF)])
    x=inputs[0]
    bk=jnp.pad(buckets,(0,1))[None]
    g1,vec,fb,em,oh=front(R,wq,wk,wv,wp,small,token_types,bk,FF)
    q,k,v,r=project(x,em,g1,vec)
    e,att,linv,g2=att_fwd(R,q,k,v,r,oh,vec,wo,wi,wu)
    out,dz1,datt,dwo,dwi,dwu,dvec2,dbi=middle(x,att,cot[0],g2,vec,fb)
    dq,dk,dv,dr,dvec=att_bwd(q,k,v,r,oh,vec,e,att,linv,datt)
    gin,dwq,dwk,dwv,dwp,dbv=last(x,dq,dk,dv,dz1,em,dr,g1)
    blk=lambda a: a.reshape(n,-1,D)
    r1=jnp.concatenate([blk(dwo),blk(dwi),blk(dwu)],axis=1)
    sv=jnp.concatenate([dbv,dvec[:5],dvec2[:6]]).reshape(12,n,s).transpose(1,0,2).reshape(n,12*s)
    pad=-(12*s+fs)%D
    sv=jnp.concatenate([sv,dbi.reshape(n,fs),jnp.zeros((n,pad),F32)],axis=1).astype(BF).reshape(n,-1,D)
    r2=jnp.concatenate([blk(dwq),blk(dwk),blk(dwv),blk(dwp),sv],axis=1)
    t1=lax.psum_scatter(r1,"shard",scatter_dimension=0,tiled=False).astype(F32)
    t1=lax.psum(t1,"rep")
    t2=lax.psum_scatter(r2,"shard",scatter_dimension=0,tiled=False).astype(F32)
    t2=lax.psum(t2,"rep")
    tv=t2[4*s:].reshape(-1)
    c=lambda j: tv[j*s:(j+1)*s]
    return (out[None],gin[None],t2[:s],t2[s:2*s],t2[2*s:3*s],c(0),t2[3*s:4*s],c(1),c(2),c(3),jnp.stack([c(4),c(5)]),
        t1[:s],c(6),c(7),c(8),jnp.concatenate([t1[(1+j)*s:(2+j)*s] for j in range(kk)],axis=1),tv[12*s:12*s+fs],t1[(1+kk)*s:],c(9),c(10),c(11))

def solution(mesh):
    both=("rep","shard")
    v=P("shard"); w=P("shard",None); a3=P(both,None,None)
    in_specs=(a3,P(both,None),P(),w,w,w,v,w,v,v,v,P(None,"shard"),w,v,v,v,w,v,w,v,v,v,a3)
    out_specs=(a3,a3,w,w,w,v,w,v,v,v,P(None,"shard"),w,v,v,v,w,v,w,v,v,v)
    return jax.shard_map(functools.partial(local,mesh.shape["rep"]),mesh=mesh,in_specs=in_specs,out_specs=out_specs,check_vma=False)
```

```python
import functools, math
import jax, jax.numpy as jnp
from jax import lax
from jax.experimental import pallas as pl
from jax.experimental.pallas import tpu as pltpu
from jax.sharding import PartitionSpec as P
import numpy as np
F32=jnp.float32; BF=jnp.bfloat16
LOG2E=math.log2(math.e); LN2=math.log(2.0)
NT=(((1,),(1,)),((),())); NN=(((1,),(0,)),((),())); TN=(((0,),(0,)),((),()))
def dot(a,b,dims=NN): return lax.dot_general(a,b,dims,preferred_element_type=F32)

def shape_of(n):
    Z=4 if n%8==0 else 1
    return Z,n//(2*Z)

class Place:
    def __init__(self,n,R):
        self.n=n; self.R=R; self.rep=lax.axis_index("rep"); self.Z,self.X=shape_of(n)
        me=lax.axis_index("shard")
        self.me=me; self.c=lax.rem(me,2); q=lax.div(me,2)
        self.x=lax.rem(q,self.X); self.z=lax.div(q,self.X)
    def at(self,z,x,c): return (z*self.X+x)*2+c
    def neighbours(self):
        z,x,c=self.z,self.x,self.c
        out=[(None,self.at(z,x,1-c))]
        if self.Z>1: out+=[(z>0,self.at(z-1,x,c)),(z<self.Z-1,self.at(z+1,x,c))]
        if self.X>1: out+=[(x>0,self.at(z,x-1,c)),(x<self.X-1,self.at(z,x+1,c))]
        return out

def when(cond,fn):
    if cond is None: fn()
    else: pl.when(cond)(fn)

def both(*conds):
    out=None
    for k in conds:
        if k is not None: out=k if out is None else jnp.logical_and(out,k)
    return out

def greet(place):
    bar=pltpu.get_barrier_semaphore()
    total=jnp.int32(0)
    for ok,idx in place.neighbours():
        when(ok,lambda idx=idx: pl.semaphore_signal(bar,inc=1,device_id={"shard":idx},device_id_type=pl.DeviceIdType.MESH))
        total=total+(1 if ok is None else ok.astype(jnp.int32))
    for d in range(1,place.R):
        pl.semaphore_signal(bar,inc=1,device_id={"rep":lax.rem(place.rep+d,place.R)},device_id_type=pl.DeviceIdType.MESH)
    total=total+(place.R-1)
    pl.semaphore_wait(bar,total)

def gather_sems(n):
    Z,X=shape_of(n); A=1+2*(Z-1); J=1+2*(X-1)
    return [pltpu.SemaphoreType.DMA((max(1,2*(Z-1)),2)),pltpu.SemaphoreType.DMA((max(1,A*2*(X-1)),2)),pltpu.SemaphoreType.DMA((A*J,2))]

def gather_events(place,G,sems,t0,dz,dx,last):
    p=place; Z,X=p.Z,p.X; zs,xs,cs=sems
    z,x,c=p.z,p.x,p.c
    def copy(idx,sem,k,to):
        return pltpu.make_async_remote_copy(src_ref=G.at[idx],dst_ref=G.at[idx],send_sem=sem.at[k,0],recv_sem=sem.at[k,1],
            device_id={"shard":to},device_id_type=pl.DeviceIdType.MESH)
    ev=[]; sends=[]
    A=1+2*(Z-1); J=1+2*(X-1)
    def slot(a):
        if a==0: return z,None
        s=(a-1)//2
        return (z-1-s,z-1-s>=0) if a%2 else (z+1+s,z+1+s<Z)
    def col(j):
        if j==0: return x,None
        k=(j-1)//2
        return (x-1-k,x-1-k>=0) if j%2 else (x+1+k,x+1+k<X)
    def zmsg(d,s):
        lev=z-s if d==0 else z+s
        ok=both(z+1<Z,z-s>=0) if d==0 else both(z>0,z+s<Z)
        return ok,copy(p.at(lev,x,c),zs,2*s+d,p.at(z+1 if d==0 else z-1,x,c))
    def zarr(d,s):
        lev,ok=slot(1+2*s+d)
        return ok,copy(p.at(lev,x,c),zs,2*s+d,p.at(z,x,1-c))
    def xmsg(a,d,k):
        lev,va=slot(a)
        cx=x-k if d==0 else x+k
        ok=both(va,x+1<X,x-k>=0) if d==0 else both(va,x>0,x+k<X)
        return ok,copy(p.at(lev,cx,c),xs,(a*(X-1)+k)*2+d,p.at(lev*0+z,x+1 if d==0 else x-1,c))
    def xarr(a,d,k):
        lev,va=slot(a); cx,vc=col(1+2*k+d)
        return both(va,vc),copy(p.at(lev,cx,c),xs,(a*(X-1)+k)*2+d,p.at(z,x,1-c))
    def cmsg(a,j):
        lev,va=slot(a); cx,vc=col(j)
        return both(va,vc),copy(p.at(lev,cx,c),cs,a*J+j,p.at(z,x,1-c))
    def carr(a,j):
        lev,va=slot(a); cx,vc=col(j)
        return both(va,vc),copy(p.at(lev,cx,1-c),cs,a*J+j,p.at(z,x,1-c))
    def add(t,order,fn): ev.append((min(t,last),order,fn))
    def starter(ms):
        def fn():
            for ok,m in ms: when(ok,m.start)
        return fn
    def waiter(ms):
        def fn():
            for ok,m in ms: when(ok,m.wait_recv)
        return fn
    for s in range(Z):
        t=t0+s*dz
        if s>0: add(t,(0,s,0),waiter([zarr(d,s-1) for d in range(2)]))
        if s<Z-1:
            ms=[zmsg(d,s) for d in range(2)]; sends+=ms
            add(t,(0,s,1),starter(ms))
    for a in range(A):
        ra=(a+1)//2; ta=t0+ra*dz
        for k in range(X):
            t=ta+k*dx
            if k>0: add(t,(1,k,a,0),waiter([xarr(a,d,k-1) for d in range(2)]))
            if k<X-1:
                ms=[xmsg(a,d,k) for d in range(2)]; sends+=ms
                add(t,(1,k,a,1),starter(ms))
            ms=[cmsg(a,j) for j in range(J) if (j+1)//2==k]; sends+=ms
            add(t,(1,k,a,2),starter(ms))
    add(last,(2,),waiter([carr(a,j) for a in range(A) for j in range(J)]))
    def done():
        for ok,m in sends: when(ok,m.wait_send)
    add(last,(3,),done)
    ev.sort(key=lambda e:(e[0],e[1]))
    return ev

def square_sems(n):
    Z,X=shape_of(n); A=1+2*(Z-1)
    return [pltpu.SemaphoreType.DMA((2*(Z-1),2)),pltpu.SemaphoreType.DMA((A,2)),pltpu.SemaphoreType.DMA((A,2)),pltpu.SemaphoreType.DMA((3*A,2))]

def square_events(place,G,sems,t0,dz,dx,dy,last):
    p=place; Z=p.Z; zs,xs,ys,cs=sems
    z,x,c,rep=p.z,p.x,p.c,p.rep
    parts=G.shape[1]; cut=(parts+1)//2
    halves=((0,cut),(cut,parts-cut))
    A=1+2*(Z-1)
    def copy(idx,part,sem,k,to):
        ref=G.at[idx] if part is None else G.at[idx,pl.ds(*halves[part])]
        return pltpu.make_async_remote_copy(src_ref=ref,dst_ref=ref,send_sem=sem.at[k,0],recv_sem=sem.at[k,1],
            device_id=to,device_id_type=pl.DeviceIdType.MESH)
    def slot(a):
        if a==0: return z,None
        s=(a-1)//2
        return (z-1-s,z-1-s>=0) if a%2 else (z+1+s,z+1+s<Z)
    other={"shard":p.at(z,x,1-c)}; across={"shard":p.at(z,1-x,c)}; above={"rep":1-rep}
    def zmsg(d,s):
        lev=z-s if d==0 else z+s
        ok=both(z+1<Z,z-s>=0) if d==0 else both(z>0,z+s<Z)
        return ok,copy(p.at(lev,x,c),None,zs,2*s+d,{"shard":p.at(z+1 if d==0 else z-1,x,c)})
    def zarr(d,s):
        lev,ok=slot(1+2*s+d)
        return ok,copy(p.at(lev,x,c),None,zs,2*s+d,other)
    def xmsg(a,h):
        lev,va=slot(a)
        return both(va,rep==h),copy(p.at(lev,x,c),h,xs,a,across)
    def xarr(a,h):
        lev,va=slot(a)
        return both(va,rep==h),copy(p.at(lev,1-x,c),h,xs,a,across)
    def ymsg(a,h):
        lev,va=slot(a)
        return both(va,rep==h),copy(p.at(lev,1-x,c),h,ys,a,above)
    def yarr(a,h):
        lev,va=slot(a)
        return both(va,rep==1-h),copy(p.at(lev,1-x,c),h,ys,a,above)
    def cmsg(a,h,core):
        lev,va=slot(a); cc=c if core==0 else 1-c
        if h is None: return [(va,copy(p.at(lev,x,cc),None,cs,3*a,other))]
        return [(both(va,rep==(g if h==0 else 1-g)),copy(p.at(lev,1-x,cc),g,cs,3*a+1+h,other)) for g in range(2)]
    ev=[]; sends=[]
    def add(t,order,fn): ev.append((min(t,last),order,fn))
    def start(t,order,ms):
        sends.extend(ms)
        def fn():
            for ok,m in ms: when(ok,m.start)
        add(t,order,fn)
    def await_(t,order,ms):
        def fn():
            for ok,m in ms: when(ok,m.wait_recv)
        add(t,order,fn)
    for s in range(Z):
        t=t0+s*dz
        if s>0: await_(t,(0,s,0),[zarr(d,s-1) for d in range(2)])
        if s<Z-1: start(t,(0,s,1),[zmsg(d,s) for d in range(2)])
        for a in ([0] if s==0 else [2*s-1,2*s]):
            start(t,(1,s,a),[xmsg(a,h) for h in range(2)]+cmsg(a,None,0))
            await_(t+dx,(2,s,a,0),[xarr(a,h) for h in range(2)])
            start(t+dx,(2,s,a,1),[ymsg(a,h) for h in range(2)]+cmsg(a,0,0))
            await_(t+dx+dy,(3,s,a,0),[yarr(a,h) for h in range(2)])
            start(t+dx+dy,(3,s,a,1),cmsg(a,1,0))
    await_(last,(4,),[m for a in range(A) for h in (None,0,1) for m in cmsg(a,h,1)])
    def done():
        for ok,m in sends: when(ok,m.wait_send)
    add(last,(5,),done)
    ev.sort(key=lambda e:(e[0],e[1]))
    return ev

def is_square(n,R): return R==2 and shape_of(n)==(4,2)
def spread_sems(n,R): return square_sems(n) if is_square(n,R) else gather_sems(n)
def spread_events(place,G,sems,t0,dz,dx,dy,last):
    if is_square(place.n,place.R): return square_events(place,G,sems,t0,dz,dx,dy,last)
    return gather_events(place,G,sems,t0,dz,dx,last)

def run_events(step,events):
    times=sorted({e[0] for e in events})
    for t in times:
        fns=[e[2] for e in events if e[0]==t]
        def fire(fns=fns):
            for f in fns: f()
        pl.when(step==t)(fire)

def sum_scratch(n,Q,s,D,parts):
    Z,X=shape_of(n); dma=pltpu.SemaphoreType.DMA
    V=lambda *sh: pltpu.VMEM(sh,BF)
    return [V(Z,X,Q,s,D),V(Z,X,Q,s,D),V(Z,Q,s,D//2),V(Z,Q,s,D//2),V(2,Z-1,Q,s,D),V(Q,s,D),
        dma((parts,)),dma((parts,2)),dma((Z,2)),dma((Z,2)),dma((2*(Z-1),2)),dma((1,2))]
SUM_REFS=12

def sum_events(place,srcs,refs,times,store):
    p=place; Z=p.Z
    z,x,c,rep=p.z,p.x,p.c,p.rep
    S,B,YB,XB,ZB,FB,ls,cs,ys,xs,zs,fs=refs
    Q=S.shape[2]; H=S.shape[4]//2
    tc,ta,ty,tx,tz,tend=times
    half=lambda r: pl.ds(pl.multiple_of(r*H,128),H)
    other={"shard":p.at(z,x,1-c)}; across={"shard":p.at(z,1-x,c)}; above={"rep":1-rep}
    def rc(src,dst,sem,k,to):
        return pltpu.make_async_remote_copy(src_ref=src,dst_ref=dst,send_sem=sem.at[k,0],recv_sem=sem.at[k,1],device_id=to,device_id_type=pl.DeviceIdType.MESH)
    ev=[]; sends=[]
    def add(t,order,fn): ev.append((t,order,fn))
    def start(t,order,ms):
        sends.extend(ms)
        def fn():
            for ok,m in ms: when(ok,m.start)
        add(t,order,fn)
    loads=[pltpu.make_async_copy(r.at[:,:,c],S.at[:,:,pl.ds(q,k)],ls.at[j]) for j,(r,q,k) in enumerate(srcs)]
    cores=[(None,rc(r.at[:,:,1-c],B.at[:,:,pl.ds(q,k)],cs,j,other)) for j,(r,q,k) in enumerate(srcs)]
    def plus(a,b): return (a.astype(F32)+b.astype(F32)).astype(BF)
    def begin():
        for m in loads: m.start()
    add(tc,(0,),begin)
    start(tc,(1,),cores)
    def merge():
        for m in loads: m.wait()
        for _,m in cores: m.wait_recv()
        def body(k,_):
            lev=lax.div(k,2*Q); r=lax.rem(k,2*Q); xx=lax.div(r,Q); q=lax.rem(r,Q)
            S[lev,xx,q]=plus(S[lev,xx,q],B[lev,xx,q])
            return 0
        lax.fori_loop(0,2*Z*Q,body,0)
    add(ta,(2,),merge)
    def levels(d): return [(z,None)] if d==0 else [(z-d,z-d>=0),(z+d,z+d<Z)]
    for i,d in enumerate(range(Z-1,-1,-1)):
        L=levels(d)
        ysend=[(ok,rc(S.at[l,1-x,:,:,half(1-rep)],YB.at[l],ys,l,above)) for l,ok in L]
        xsend=[(ok,rc(S.at[l,1-x,:,:,half(rep)],XB.at[l],xs,l,across)) for l,ok in L]
        start(ty[i],(3,i),ysend)
        def ytake(L=L,ysend=ysend):
            for (l,ok),(_,m) in zip(L,ysend):
                def go(l=l,m=m):
                    m.wait_recv()
                    def body(q,_):
                        S[l,1-x,q,:,half(rep)]=plus(S[l,1-x,q,:,half(rep)],YB[l,q])
                        return 0
                    lax.fori_loop(0,Q,body,0)
                when(ok,go)
        add(tx[i],(4,i,0),ytake)
        start(tx[i],(4,i,1),xsend)
        def xtake(L=L,xsend=xsend):
            for (l,ok),(_,m) in zip(L,xsend):
                def go(l=l,m=m):
                    m.wait_recv()
                    def body(q,_):
                        S[l,x,q,:,half(rep)]=plus(S[l,x,q,:,half(rep)],XB[l,q])
                        return 0
                    lax.fori_loop(0,Q,body,0)
                when(ok,go)
        add(tz[i],(5,i,0),xtake)
        if d<=Z-2:
            def ztake(d=d):
                for dr,(l,ok) in enumerate([(z-d,both(z+1<Z,z-d>=0)),(z+d,both(z>0,z+d<Z))]):
                    def go(dr=dr,l=l):
                        rc(ZB.at[dr,d],ZB.at[dr,d],zs,2*d+dr,other).wait_recv()
                        def body(q,_):
                            S[l,x,q]=plus(S[l,x,q],ZB[dr,d,q])
                            return 0
                        lax.fori_loop(0,Q,body,0)
                    pl.when(ok)(go)
            add(tz[i],(5,i,1),ztake)
        if d>=1:
            start(tz[i],(5,i,2),[(z-d>=0,rc(S.at[z-d,x],ZB.at[0,d-1],zs,2*(d-1),{"shard":p.at(z-1,x,c)})),
                (z+d<Z,rc(S.at[z+d,x],ZB.at[1,d-1],zs,2*(d-1)+1,{"shard":p.at(z+1,x,c)}))])
    final=[(None,rc(S.at[z,x],FB,fs,0,above))]
    start(tz[-1],(6,),final)
    def finish():
        final[0][1].wait_recv()
        for q in range(Q): store(q,S[z,x,q].astype(F32)+FB[q].astype(F32))
    add(tend,(7,),finish)
    def done():
        for ok,m in sends: when(ok,m.wait_send)
    add(tend,(8,),done)
    return ev

def greet_all(place):
    bar=pltpu.get_barrier_semaphore()
    n,R=place.n,place.R
    def hello(d,_):
        pl.semaphore_signal(bar,inc=1,device_id={"shard":lax.rem(place.me+d,n)},device_id_type=pl.DeviceIdType.MESH)
        return 0
    lax.fori_loop(1,n,hello,0)
    for d in range(1,R):
        pl.semaphore_signal(bar,inc=1,device_id={"rep":lax.rem(place.rep+d,R)},device_id_type=pl.DeviceIdType.MESH)
    return lambda: pl.semaphore_wait(bar,n+R-2)

STRIDE=32
def tables(length,width):
    half=width//2; count=2*length//STRIDE
    rates=np.exp(np.arange(half)*(-2.0*math.log(10000.0)/width))
    def pack(angles):
        full=np.concatenate([np.sin(angles),np.cos(angles)],axis=1).astype(np.float32)
        hi=full.astype(jnp.bfloat16); lo=(full-hi.astype(np.float32)).astype(jnp.bfloat16)
        return np.concatenate([hi,lo],axis=0)
    coarse=(np.arange(count)*STRIDE-length)[:,None]*rates[None]
    fine=np.arange(STRIDE)[:,None]*rates[None]
    return pack(coarse),pack(fine)

def front_kernel(n,R,wq_ref,wk_ref,wv_ref,wp_ref,small_ref,kinds_ref,buckets_ref,ta_ref,tb_ref,
        g_ref,vec_ref,bi_ref,em_ref,oh_ref,all_s,mine,own,ssem,*sems):
    place=Place(n,R); me=place.me
    ws=(wq_ref,wk_ref,wv_ref,wp_ref)
    owns=[pltpu.make_async_copy(w,mine.at[j],own.at[j]) for j,w in enumerate(ws)]
    keep=pltpu.make_async_copy(mine,g_ref.at[me],own.at[4])
    for m in owns: m.start()
    bar=pltpu.get_barrier_semaphore()
    def hello(d,_):
        pl.semaphore_signal(bar,inc=1,device_id={"shard":lax.rem(me+d,n)},device_id_type=pl.DeviceIdType.MESH)
        return 0
    lax.fori_loop(1,n,hello,0)
    for d in range(1,R):
        pl.semaphore_signal(bar,inc=1,device_id={"rep":lax.rem(place.rep+d,R)},device_id_type=pl.DeviceIdType.MESH)
    all_s[me]=small_ref[...]
    for m in owns: m.wait()
    keep.start()
    pl.semaphore_wait(bar,n+R-2)
    keep.wait()
    def send(d):
        return pltpu.make_async_remote_copy(src_ref=all_s.at[me],dst_ref=all_s.at[me],send_sem=ssem.at[d,0],recv_sem=ssem.at[d,1],
            device_id={"shard":lax.rem(me+d,n)},device_id_type=pl.DeviceIdType.MESH)
    def arrive(d):
        w=lax.rem(me-d+n,n)
        return pltpu.make_async_remote_copy(src_ref=all_s.at[w],dst_ref=all_s.at[w],send_sem=ssem.at[d,0],recv_sem=ssem.at[d,1],
            device_id={"shard":lax.rem(me+d,n)},device_id_type=pl.DeviceIdType.MESH)
    def prepare():
        def go(d,_):
            send(d).start()
            return 0
        lax.fori_loop(1,n,go,0)
        L2=buckets_ref.shape[1]; L=L2//2
        count=L2//STRIDE
        def body(j,_):
            rows=pl.ds(pl.multiple_of(j*256,256),256)
            b=buckets_ref[:,rows]
            hot=lambda v,m: jnp.where(v==lax.rem(lax.broadcasted_iota(jnp.int32,(2*m,256),0),m),1.0,0.0).astype(BF)
            A=dot(hot(lax.div(b,STRIDE),count),ta_ref[...],TN)
            B=dot(hot(lax.rem(b,STRIDE),STRIDE),tb_ref[...],TN)
            h=A.shape[1]//2
            sa,ca,sb,cb=A[:,:h],A[:,h:],B[:,:h],B[:,h:]
            em_ref[rows,:]=jnp.concatenate([sa*cb+ca*sb,ca*cb-sa*sb],axis=1).astype(BF)
            return 0
        lax.fori_loop(0,L2//256,body,0)
        for j in range(L//256):
            kinds=kinds_ref[:,j*256:(j+1)*256]
            lane=lax.rem(lax.broadcasted_iota(jnp.int32,(128,256),0),64)
            hot=jnp.where((lax.rem(lane,3)==kinds)&(lane<6),1.0,0.0)
            oh_ref[j*256:(j+1)*256,:]=hot.T.astype(BF)
        def come(d,_):
            arrive(d).wait_recv()
            send(d).wait_send()
            return 0
        lax.fori_loop(1,n,come,0)
        s=wq_ref.shape[0]; fs=bi_ref.shape[1]//n
        for w in range(n):
            a=all_s[w].astype(F32)
            vec_ref[:,w*s:(w+1)*s]=a[:,:s]
            bi_ref[:,w*fs:(w+1)*fs]=a[14:15,:fs]
    ev=spread_events(place,g_ref,sems,0,1,1,1,99)
    ev=sorted(ev+[(0,(9,),prepare)],key=lambda e:(e[0],e[1]))
    for e in ev: e[2]()

def front(R,wq,wk,wv,wp,small,kinds,buckets,FF):
    s,D=wq.shape; n=D//s; L=kinds.shape[1]; SL=small.shape[1]
    ta,tb=tables(L,D)
    hbm=pl.BlockSpec(memory_space=pl.ANY); vm=pl.BlockSpec(memory_space=pltpu.VMEM)
    return pl.pallas_call(functools.partial(front_kernel,n,R),
        in_specs=[hbm]*4+[vm]*5,out_specs=[hbm]+[vm]*4,
        out_shape=[jax.ShapeDtypeStruct((n,4,s,D),BF),jax.ShapeDtypeStruct((16,D),F32),jax.ShapeDtypeStruct((1,FF),F32),
            jax.ShapeDtypeStruct((2*L,D),BF),jax.ShapeDtypeStruct((L,128),BF)],
        scratch_shapes=[pltpu.VMEM((n,16,SL),BF),pltpu.VMEM((4,s,D),BF),pltpu.SemaphoreType.DMA((5,)),pltpu.SemaphoreType.DMA((n,2))]+spread_sems(n,R),
        compiler_params=CP(collective_id=0,has_side_effects=True),name="front")(wq,wk,wv,wp,small,kinds,buckets,jnp.asarray(ta),jnp.asarray(tb))

BI=256
ONE=pl.Buffered(1)


def lane_half(rows, lanes):
    lane=lax.broadcasted_iota(jnp.int32,(rows,lanes),1)
    return (lane//64)%2

def split_hi_lo(v):
    hi=v.astype(BF); return hi,(v-hi.astype(F32)).astype(BF)

def queries(q, vec, oh):
    s=0.125*LOG2E
    cq=((q+vec[0:1])*s).astype(BF)
    pq=((q+vec[1:2])*s).astype(BF)
    tq=(q+vec[2:3])*0.125
    return cq,pq,tq

def fwd_kernel(n,R,roll_bf,q_ref,k_ref,v_ref,r_ref,oh_ref,vec_ref,wo_ref,wi_ref,wu_ref,e_ref,att_ref,linv_ref,g_ref,mine,own,*sems):
    bi=q_ref.shape[0]; L=k_ref.shape[0]; W=L+bi
    i=pl.program_id(1); nb=L//bi
    step=pl.program_id(0)*nb+i; steps=6*nb
    place=Place(n,R)
    kk=wu_ref.shape[0]; D=wo_ref.shape[1]
    owns=[pltpu.make_async_copy(wu_ref,mine.at[pl.ds(0,kk)],own.at[0]),pltpu.make_async_copy(wo_ref,mine.at[kk],own.at[1])]
    owns+=[pltpu.make_async_copy(wi_ref.at[:,pl.ds(j*D,D)],mine.at[kk+1+j],own.at[2+j]) for j in range(kk)]
    keep=pltpu.make_async_copy(mine,g_ref.at[place.me],own.at[2+kk])
    def enter():
        for m in owns: m.start()
        for m in owns: m.wait()
        keep.start()
        greet(place)
        keep.wait()
    run_events(step,[(0,(-1,),enter)]+spread_events(place,g_ref,sems,0,7,4,4,steps-1))
    vec=vec_ref[...]
    q=q_ref[...]
    oh_i=oh_ref[pl.ds(pl.multiple_of(i*bi,bi),bi),:]
    cq,pq,tq=queries(q,vec,None)
    rr=lax.broadcasted_iota(jnp.int32,(256,128),0)%128
    cc=lax.broadcasted_iota(jnp.int32,(256,128),1)
    M=jnp.where((rr//64==cc//64)&(cc%64<6),1.0,0.0).astype(BF)
    def tt(te):
        hi,lo=split_hi_lo(tq*(te*LOG2E))
        return dot(jnp.concatenate([hi,lo],axis=1),M)
    t0=tt(vec[3:4]); t1=tt(vec[4:5])
    tv=jnp.where(oh_i>0,t1,t0)
    hi=tv.astype(BF).astype(F32)
    lane=lax.broadcasted_iota(jnp.int32,(bi,128),1)
    tv=jnp.where(lane%64<3,hi,tv-hi).astype(BF)
    half=lane_half(bi,128)
    kext=jnp.concatenate([k_ref[...],oh_ref[...]],axis=1)
    vext=jnp.concatenate([v_ref[...],jnp.ones((L,128),BF)],axis=1)
    w0=pl.multiple_of(L-bi-i*bi,bi)
    rwin=r_ref[pl.ds(w0,W),:]
    z=jnp.zeros((),BF)
    outs=[]
    for h in range(2):
        qx=jnp.concatenate([jnp.where(half==h,cq,z),jnp.where(half==h,tv,z)],axis=1)
        pos=dot(jnp.where(half==h,pq,z),rwin,NT)
        if roll_bf: pos=pos.astype(BF)
        pos=pltpu.roll(pos,W-(bi-1),1,stride=1,stride_axis=0)[:,:L]
        s=dot(qx,kext,NT)+pos.astype(F32)
        m=jnp.max(s,axis=1,keepdims=True)
        e=jnp.exp2(s-m).astype(BF)
        e_ref[h]=e
        o=dot(e,vext)
        li=1.0/o[:,128:]
        outs.append((o[:,:128]*li,li))
    att_ref[...]=jnp.where(half==0,outs[0][0],outs[1][0]).astype(BF)
    linv_ref[...]=jnp.where(half==0,outs[0][1],outs[1][1])

def att_fwd(R,q,k,v,r,oh,vec,wo,wi,wu,bi=BI,roll_bf=False):
    L,D=q.shape; P=D//128; nb=L//bi; s=wo.shape[0]; n=D//s; kk=wu.shape[0]//s
    hbm=pl.BlockSpec(memory_space=pl.ANY)
    return pl.pallas_call(functools.partial(fwd_kernel,n,R,roll_bf),
        grid=(P,nb),
        in_specs=[pl.BlockSpec((bi,128),lambda p,i:(i,p)),
            pl.BlockSpec((L,128),lambda p,i:(0,p)),
            pl.BlockSpec((L,128),lambda p,i:(0,p)),
            pl.BlockSpec((2*L,128),lambda p,i:(0,p)),
            pl.BlockSpec((L,128),lambda p,i:(0,0)),
            pl.BlockSpec((8,128),lambda p,i:(0,p)),hbm,hbm,hbm],
        out_specs=[pl.BlockSpec((2,bi,L),lambda p,i:(p,i,0)),
            pl.BlockSpec((bi,128),lambda p,i:(i,p)),
            pl.BlockSpec((bi,128),lambda p,i:(i,p)),hbm],
        out_shape=[jax.ShapeDtypeStruct((2*P,L,L),BF),jax.ShapeDtypeStruct((L,D),BF),jax.ShapeDtypeStruct((L,D),F32),
            jax.ShapeDtypeStruct((n,2*kk+1,s,D),BF)],
        scratch_shapes=[pltpu.VMEM((2*kk+1,s,D),BF),pltpu.SemaphoreType.DMA((3+kk,))]+spread_sems(n,R),
        compiler_params=pltpu.CompilerParams(vmem_limit_bytes=56*2**20,dimension_semantics=("arbitrary","arbitrary"),collective_id=1,has_side_effects=True),
        name="attend")(q,k,v,r,oh,vec,wo,wi,wu.reshape(kk,s,D))

TIMES_A=(0,2,(2,3,4,6),(4,5,7,8),(6,9,12,15),18)
TIMES_B=(1,4,(5,6,8,10),(7,8,11,12),(11,15,18,21),23)

def bwd_kernel(n,R,roll_bf,q_ref,k_ref,v_ref,r_ref,oh_ref,vec_ref,e_ref,att_ref,linv_ref,datt_ref,*rest):
    bi=q_ref.shape[0]; L=k_ref.shape[0]; W=L+bi
    i=pl.program_id(1); nb=L//bi
    if is_square(n,R):
        gu_ref,gi_ref,go_ref=rest[:3]
        dq_ref,dk_ref,dv_ref,dr_ref,dvec_ref,wu_ref,wi_ref,wo_ref,dk_acc,dv_acc,dr_acc=rest[3:14]
        refs=rest[14:]
        s,D=wo_ref.shape; kk=wu_ref.shape[0]//s
        def store_a(q,v): wu_ref[q*s:(q+1)*s,:]=v
        def store_b(q,v):
            if q<kk: wi_ref[:,q*D:(q+1)*D]=v
            else: wo_ref[...]=v
        place=Place(n,R)
        ev=[(0,(-1,),lambda: greet(place))]
        ev+=sum_events(place,[(gu_ref,0,kk)],refs[:SUM_REFS],TIMES_A,store_a)
        ev+=sum_events(place,[(gi_ref,0,kk),(go_ref,kk,1)],refs[SUM_REFS:],TIMES_B,store_b)
        ev.sort(key=lambda e:(e[0],e[1]))
        run_events(pl.program_id(0)*nb+i,ev)
    else:
        dq_ref,dk_ref,dv_ref,dr_ref,dvec_ref,dk_acc,dv_acc,dr_acc=rest
    vec=vec_ref[...]
    q=q_ref[...]
    oh_i=oh_ref[pl.ds(pl.multiple_of(i*bi,bi),bi),:].astype(F32)
    cq,pq,tq=queries(q,vec,None)
    half=lane_half(bi,128)
    lane=lax.broadcasted_iota(jnp.int32,(bi,128),1)
    @pl.when(i==0)
    def _():
        dk_acc[...]=jnp.zeros_like(dk_acc); dv_acc[...]=jnp.zeros_like(dv_acc); dr_acc[...]=jnp.zeros_like(dr_acc)
        dvec_ref[...]=jnp.zeros_like(dvec_ref)
    P=jnp.where(lax.broadcasted_iota(jnp.int32,(bi,bi),0)+lax.broadcasted_iota(jnp.int32,(bi,bi),1)==bi-1,1.0,0.0).astype(BF)
    pqr=dot(P,pq).astype(BF)
    kext=jnp.concatenate([k_ref[...],oh_ref[...]],axis=1)
    ones2=jnp.where(lax.broadcasted_iota(jnp.int32,(L,128),1)<2,1.0,0.0).astype(BF)
    vext=jnp.concatenate([v_ref[...],ones2],axis=1)
    w0=pl.multiple_of(L-bi-i*bi,bi)
    rwin=r_ref[pl.ds(w0,W),:]
    z=jnp.zeros((),BF)
    dattl=datt_ref[...].astype(F32)*linv_ref[...]
    prod=dattl*att_ref[...].astype(F32)
    dattl=dattl.astype(BF)
    dcs=[];dps=[];dts=[];tes=[]
    dk=None; dv=None; dr=None
    for h in range(2):
        delta=-jnp.sum(jnp.where(half==h,prod,0.0),axis=1,keepdims=True)
        dhi=delta.astype(BF).astype(F32)
        dx=jnp.where(lane==0,dhi,jnp.where(lane==1,delta-dhi,0.0)).astype(BF)
        dm=jnp.where(half==h,dattl,z)
        dpd=dot(jnp.concatenate([dm,dx],axis=1),vext,NT)
        e=e_ref[h]
        ds=(e.astype(F32)*dpd).astype(BF)
        dvh=dot(e,dm,TN)
        dkh=dot(ds,jnp.where(half==h,cq,z),TN)
        dc=dot(ds,kext)
        rev=dot(P,ds)
        if roll_bf: rev=rev.astype(BF)
        rev=jnp.concatenate([rev,jnp.zeros((bi,W-L),rev.dtype)],axis=1)
        dpr=pltpu.roll(rev,0,1,stride=1,stride_axis=0).astype(BF)
        dp=dot(dpr,rwin)
        drh=dot(dpr,jnp.where(half==h,pqr,z),TN)
        dv=dvh if dv is None else dv+dvh
        dk=dkh if dk is None else dk+dkh
        dr=drh if dr is None else dr+drh
        D=jnp.where(lane<3,dc[:,128:],0.0)
        dall=jnp.sum(D,axis=1,keepdims=True)
        d1=jnp.sum(D*oh_i,axis=1,keepdims=True)
        d0=dall-d1
        dcs.append(dc[:,:128]); dps.append(dp)
        dts.append(d0*vec[3:4]+d1*vec[4:5])
        tes.append((d0,d1))
    dv_acc[...]+=dv
    dk_acc[...]+=dk
    dr_acc[pl.ds(w0,W),:]+=dr
    dcq=jnp.where(half==0,dcs[0],dcs[1]).astype(BF).astype(F32)
    dpr=jnp.where(half==0,dps[0],dps[1]).astype(BF)
    dpq=dot(P,dpr)
    dtq=jnp.where(half==0,dts[0],dts[1])
    dq_ref[...]=((dcq+dpq+dtq)*0.125).astype(BF)
    d0=jnp.where(half==0,tes[0][0],tes[1][0]); d1=jnp.where(half==0,tes[0][1],tes[1][1])
    rows=[dcq*0.125,dpq*0.125,dtq*0.125,d0*tq,d1*tq]
    sums=[jnp.sum(v,axis=0,keepdims=True) for v in rows]+[jnp.zeros((3,128),F32)]
    dvec_ref[...]+=jnp.concatenate(sums,axis=0)
    @pl.when(i==nb-1)
    def _():
        dk_ref[...]=(dk_acc[...]*LN2).astype(BF)
        dv_ref[...]=dv_acc[...].astype(BF)
        dr_ref[...]=(dr_acc[...]*LN2).astype(BF)

def att_bwd(R,q,k,v,r,oh,vec,e,att,linv,datt,dwu,dwi,dwo,bi=BI,roll_bf=False):
    L,D=q.shape; P=D//128; nb=L//bi; n,kk,s,_=dwu.shape
    col=pl.BlockSpec((L,128),lambda p,i:(0,p)); tile=pl.BlockSpec((bi,128),lambda p,i:(i,p))
    in_specs=[tile,col,col,pl.BlockSpec((2*L,128),lambda p,i:(0,p)),pl.BlockSpec((L,128),lambda p,i:(0,0)),
        pl.BlockSpec((8,128),lambda p,i:(0,p)),pl.BlockSpec((2,bi,L),lambda p,i:(p,i,0)),tile,tile,tile]
    out_specs=[tile,col,col,pl.BlockSpec((2*L,128),lambda p,i:(0,p)),pl.BlockSpec((8,128),lambda p,i:(0,p))]
    out_shape=[jax.ShapeDtypeStruct((L,D),BF),jax.ShapeDtypeStruct((L,D),BF),jax.ShapeDtypeStruct((L,D),BF),
        jax.ShapeDtypeStruct((2*L,D),BF),jax.ShapeDtypeStruct((8,D),F32)]
    scratch=[pltpu.VMEM((L,128),F32),pltpu.VMEM((L,128),F32),pltpu.VMEM((2*L,128),F32)]
    args=[q,k,v,r,oh,vec,e,att,linv,datt]
    params=dict(vmem_limit_bytes=60*2**20,dimension_semantics=("arbitrary","arbitrary"))
    if is_square(n,R):
        Z,X=shape_of(n)
        in_specs+=[pl.BlockSpec(memory_space=pl.ANY)]*3
        for sh in ((kk*s,D),(s,kk*D),(s,D)):
            out_specs.append(pl.BlockSpec(sh,lambda p,i:(0,0),pipeline_mode=ONE)); out_shape.append(jax.ShapeDtypeStruct(sh,F32))
        scratch+=sum_scratch(n,kk,s,D,1)+sum_scratch(n,kk+1,s,D,2)
        args+=[dwu.reshape(Z,X,2,kk,s,D),dwi.reshape(Z,X,2,kk,s,D),dwo.reshape(Z,X,2,1,s,D)]
        params.update(collective_id=2,has_side_effects=True)
    return pl.pallas_call(functools.partial(bwd_kernel,n,R,roll_bf),grid=(P,nb),in_specs=in_specs,out_specs=out_specs,out_shape=out_shape,
        scratch_shapes=scratch,compiler_params=pltpu.CompilerParams(**params),
        name="attend_back")(*args)

CP=lambda **k: pltpu.CompilerParams(vmem_limit_bytes=60*2**20,**k)
C0=math.sqrt(2.0/math.pi); C1=0.044715
EPS=1e-6

def whole(ref):
    a=ref[...]
    return a.reshape(-1,a.shape[-1])

def proj_kernel(x_ref,em_ref,wq_ref,wk_ref,wv_ref,wp_ref,vec_ref,q_ref,k_ref,v_ref,r_ref):
    x=x_ref[...]
    q_ref[...]=dot(x,whole(wq_ref))
    k_ref[...]=dot(x,whole(wk_ref)).astype(BF)
    v_ref[...]=(dot(x,whole(wv_ref))+vec_ref[5:6,:]).astype(BF)
    r_ref[...]=dot(em_ref[...],whole(wp_ref)).astype(BF)

def project(x,em,g,vec,bi=256):
    L,D=x.shape; nb=L//bi; n,_,s,_=g.shape
    w=[pl.BlockSpec((n,1,s,D),lambda i,j=j:(0,j,0,0),pipeline_mode=ONE) for j in range(4)]
    row=pl.BlockSpec((bi,D),lambda i:(i,0)); row2=pl.BlockSpec((2*bi,D),lambda i:(i,0))
    return pl.pallas_call(proj_kernel,grid=(nb,),
        in_specs=[row,row2]+w+[pl.BlockSpec((8,D),lambda i:(0,0))],
        out_specs=[row,row,row,row2],
        out_shape=[jax.ShapeDtypeStruct((L,D),F32),jax.ShapeDtypeStruct((L,D),BF),jax.ShapeDtypeStruct((L,D),BF),jax.ShapeDtypeStruct((2*L,D),BF)],
        compiler_params=CP(),name="project")(x,em,g,g,g,g,vec)

def ln_stats(z):
    n=z.shape[1]
    mu=jnp.sum(z,axis=1,keepdims=True)*(1.0/n)
    c=z-mu
    var=jnp.sum(c*c,axis=1,keepdims=True)*(1.0/n)
    r=lax.rsqrt(var+EPS)
    return c*r,r

def ln_back(g,zhat,r):
    n=g.shape[1]
    a=jnp.sum(g,axis=1,keepdims=True)*(1.0/n)
    b=jnp.sum(g*zhat,axis=1,keepdims=True)*(1.0/n)
    return r*(g-a-zhat*b)

def rowsum(v): return jnp.sum(v,axis=0,keepdims=True)

def mid_kernel(nb,bi,nc,x_ref,att_ref,cot_ref,wo_ref,wu_ref,*rest):
    wi_refs=rest[:nc]
    (vec_ref,bi_ref,out_ref,dz1_ref,datt_ref,dwo_ref,dwi_ref,dwu_ref,dvec_ref,dbi_ref,
        mid_s,att_s,dffn_s,dattn_s,hid_s,din_s,acc_s)=rest[nc:]
    t=pl.program_id(0)
    D=x_ref.shape[1]; fc=D
    n=wu_ref.shape[0]; per=n//nc
    wu=lambda c: wu_ref[c*per:(c+1)*per].reshape(fc,D)
    wi=lambda c: whole(wi_refs[c])
    @pl.when(t==0)
    def _():
        dvec_ref[...]=jnp.zeros_like(dvec_ref); dbi_ref[...]=jnp.zeros_like(dbi_ref)
    @pl.when(t<nb)
    def _():
        rows=pl.ds(pl.multiple_of(t*bi,bi),bi)
        b_out,ga,sa,b_outer,gf,sf=[vec_ref[k:k+1,:] for k in range(6)]
        att=att_ref[...]
        att_s[rows,:]=att
        z1=x_ref[...].astype(F32)+dot(att,whole(wo_ref))+b_out
        zh1,r1=ln_stats(z1)
        middle=zh1*ga+sa
        mid=middle.astype(BF)
        mid_s[rows,:]=mid
        acc_s[...]=middle+b_outer
        for c in range(nc):
            cs=slice(c*fc,(c+1)*fc)
            v=dot(mid,wi(c))+bi_ref[:,cs]
            u=v*v
            th=jnp.tanh(v*(C0+(C0*C1)*u))
            hv=0.5*v
            hid=(hv+hv*th).astype(BF)
            dg=0.5+0.5*th+hv*(1.0-th*th)*(C0+(3*C0*C1)*u)
            hid_s[rows,cs]=hid
            din_s[rows,cs]=dg.astype(BF)
            acc_s[...]+=dot(hid,wu(c))
        zh2,r2=ln_stats(acc_s[...])
        out_ref[...]=(zh2*gf+sf).astype(BF)
        g=cot_ref[...].astype(F32)
        dz2=ln_back(g*gf,zh2,r2)
        dffn=dz2.astype(BF)
        dffn_s[rows,:]=dffn
        acc_s[...]=dz2
        dbs=[]
        for c in range(nc):
            cs=slice(c*fc,(c+1)*fc)
            dh=dot(dffn,wu(c),NT)
            din=(dh*din_s[rows,cs].astype(F32)).astype(BF)
            din_s[rows,cs]=din
            dbi_ref[:,cs]+=rowsum(din.astype(F32))
            acc_s[...]+=dot(din,wi(c),NT)
        dm=acc_s[...]
        dz1=ln_back(dm*ga,zh1,r1)
        dz1_ref[...]=dz1
        dattn=dz1.astype(BF)
        dattn_s[rows,:]=dattn
        datt_ref[...]=dot(dattn,whole(wo_ref),NT).astype(BF)
        dvec_ref[...]+=jnp.concatenate([rowsum(dz1),rowsum(dm*zh1),rowsum(dm),rowsum(dz2),rowsum(g*zh2),rowsum(g),jnp.zeros((2,D),F32)],axis=0)
    @pl.when(t==nb)
    def _():
        dwo_ref[...]=dot(att_s[...],dattn_s[...],TN).astype(BF).reshape(dwo_ref.shape)
    for c in range(nc):
        cs=slice(c*fc,(c+1)*fc)
        @pl.when(t==nb+c)
        def _():
            dwi_ref[...]=dot(mid_s[...],din_s[:,cs],TN).astype(BF).reshape(dwi_ref.shape)
            dwu_ref[...]=dot(hid_s[:,cs],dffn_s[...],TN).astype(BF).reshape(dwu_ref.shape)

def middle(x,att,cot,g,vec,b_inner,bi=256):
    L,D=x.shape; n,parts,s,_=g.shape; nc=(parts-1)//2; FF=nc*D; nb=L//bi; per=n//nc
    row=pl.BlockSpec((bi,D),lambda t:(jnp.minimum(t,nb-1),0))
    cc=lambda t: jnp.clip(t-nb,0,nc-1)
    w=lambda j: pl.BlockSpec((n,1,s,D),lambda t:(0,j,0,0),pipeline_mode=ONE)
    return pl.pallas_call(functools.partial(mid_kernel,nb,bi,nc),grid=(nb+nc,),
        in_specs=[row,row,row,w(nc),pl.BlockSpec((n,nc,s,D),lambda t:(0,0,0,0),pipeline_mode=ONE)]+[w(nc+1+j) for j in range(nc)]
            +[pl.BlockSpec((8,D),lambda t:(1,0)),pl.BlockSpec((1,FF),lambda t:(0,0))],
        out_specs=[row,row,row,pl.BlockSpec((n,s,D),lambda t:(0,0,0)),pl.BlockSpec((n,1,s,D),lambda t:(0,cc(t),0,0)),
            pl.BlockSpec((per,nc,s,D),lambda t:(cc(t),0,0,0)),
            pl.BlockSpec((8,D),lambda t:(0,0)),pl.BlockSpec((1,FF),lambda t:(0,0))],
        out_shape=[jax.ShapeDtypeStruct((L,D),BF),jax.ShapeDtypeStruct((L,D),F32),jax.ShapeDtypeStruct((L,D),BF),
            jax.ShapeDtypeStruct((n,s,D),BF),jax.ShapeDtypeStruct((n,nc,s,D),BF),jax.ShapeDtypeStruct((n,nc,s,D),BF),
            jax.ShapeDtypeStruct((8,D),F32),jax.ShapeDtypeStruct((1,FF),F32)],
        scratch_shapes=[pltpu.VMEM((L,D),BF)]*4+[pltpu.VMEM((L,FF),BF)]*2+[pltpu.VMEM((bi,D),F32)],
        compiler_params=CP(),name="middle")(x,att,cot,*([g]*(2+nc)),vec,b_inner)

TIMES_C=(2,3,(4,4,5,5),(5,6,6,7),(7,8,9,10),11)
TIMES_D=(4,5,(6,6,7,7),(7,8,8,9),(9,10,11,12),13)

def last_kernel(n,R,nb,bi,x_ref,dq_ref,dk_ref,dv_ref,dz_ref,em_ref,dr_ref,wq_ref,wk_ref,wv_ref,va_ref,vb_ref,vi_ref,*rest):
    t=pl.program_id(0)
    if is_square(n,R):
        gi_ref,dwq_ref,dwk_ref,dwv_ref,dwp_ref,vec_ref,pq,kv,piece,came,total,theirs,ss,ts=rest[:14]
        refs=rest[14:]
        place=Place(n,R); Z,X=place.Z,place.X; me=place.me
        s,D=dwq_ref.shape
        blocks=lambda v: v.astype(BF).reshape(Z,X,2,s,D)
        def store_c(q,v): (dwp_ref if q==0 else dwq_ref)[...]=v
        def store_d(q,v): (dwk_ref if q==0 else dwv_ref)[...]=v
        def arrive(d):
            w=lax.rem(me-d+n,n)
            return pltpu.make_async_remote_copy(src_ref=piece.at[w],dst_ref=came.at[w],send_sem=ss.at[d,0],recv_sem=ss.at[d,1],
                device_id={"shard":w},device_id_type=pl.DeviceIdType.MESH)
        def send(d):
            w=lax.rem(me+d,n)
            return pltpu.make_async_remote_copy(src_ref=piece.at[w],dst_ref=came.at[me],send_sem=ss.at[d,0],recv_sem=ss.at[d,1],
                device_id={"shard":w},device_id_type=pl.DeviceIdType.MESH)
        swap=pltpu.make_async_remote_copy(src_ref=total,dst_ref=theirs,send_sem=ts.at[0],recv_sem=ts.at[1],
            device_id={"rep":1-place.rep},device_id_type=pl.DeviceIdType.MESH)
        def first():
            pq[:,:,:,0]=blocks(dot(em_ref[...],dr_ref[...],TN))
            greet_all(place)()
        def second(): pq[:,:,:,1]=blocks(dot(x_ref[...],dq_ref[...],TN))
        def third(): kv[:,:,:,0]=blocks(dot(x_ref[...],dk_ref[...],TN))
        def fourth():
            kv[:,:,:,1]=blocks(dot(x_ref[...],dv_ref[...],TN))
            fs=vi_ref.shape[1]//n
            dbv=rowsum(dv_ref[...].astype(F32))
            rows=jnp.concatenate([va_ref[0:5,:],dbv,jnp.zeros((2,D),F32),vb_ref[...]],axis=0)
            for w in range(n):
                piece[w,:,:s]=rows[:,w*s:(w+1)*s]
                piece[w,14:15,:fs]=vi_ref[:,w*fs:(w+1)*fs]
            came[me]=piece[me]
            def go(d,_):
                send(d).start()
                return 0
            lax.fori_loop(1,n,go,0)
        def collect():
            def go(d,_):
                arrive(d).wait_recv()
                return 0
            lax.fori_loop(1,n,go,0)
            acc=came[0]
            for w in range(1,n): acc=acc+came[w]
            total[...]=acc
            swap.start()
        def sent():
            swap.wait_recv()
            vec_ref[...]=total[...]+theirs[...]
            swap.wait_send()
            def go(d,_):
                send(d).wait_send()
                return 0
            lax.fori_loop(1,n,go,0)
        ev=[(0,(-1,),first),(1,(-1,),second),(2,(-2,),third),(3,(-1,),fourth),(5,(-1,),collect),(8,(-1,),sent)]
        ev+=sum_events(place,[(pq,0,2)],refs[:SUM_REFS],TIMES_C,store_c)
        ev+=sum_events(place,[(kv,0,2)],refs[SUM_REFS:],TIMES_D,store_d)
        ev.sort(key=lambda e:(e[0],e[1]))
        run_events(t,ev)
        first_row=4
    else:
        gi_ref,dwq_ref,dwk_ref,dwv_ref,dwp_ref,dbv_ref=rest
        first_row=0
        @pl.when(t==nb)
        def _(): dwq_ref[...]=dot(x_ref[...],dq_ref[...],TN).astype(BF)
        @pl.when(t==nb+1)
        def _(): dwk_ref[...]=dot(x_ref[...],dk_ref[...],TN).astype(BF)
        @pl.when(t==nb+2)
        def _():
            dwv_ref[...]=dot(x_ref[...],dv_ref[...],TN).astype(BF)
            dbv_ref[...]=rowsum(dv_ref[...].astype(F32))
        @pl.when(t==nb+3)
        def _(): dwp_ref[...]=dot(em_ref[...],dr_ref[...],TN).astype(BF)
    @pl.when((t>=first_row)&(t<first_row+nb))
    def _():
        rows=pl.ds(pl.multiple_of((t-first_row)*bi,bi),bi)
        gi_ref[...]=dz_ref[...]+dot(dq_ref[rows,:],whole(wq_ref),NT)+dot(dk_ref[rows,:],whole(wk_ref),NT)+dot(dv_ref[rows,:],whole(wv_ref),NT)

def last(R,x,dq,dk,dv,dz1,em,dr,g,va,vb,vi,bi=256):
    L,D=x.shape; nb=L//bi; n,_,s,_=g.shape; FF=vi.shape[1]
    w=[pl.BlockSpec((n,1,s,D),lambda t,j=j:(0,j,0,0),pipeline_mode=ONE) for j in range(3)]
    sq=is_square(n,R)
    row=pl.BlockSpec((bi,D),lambda t:(jnp.clip(t-(4 if sq else 0),0,nb-1),0))
    full=lambda sh: pl.BlockSpec(sh,lambda t:(0,)*len(sh),pipeline_mode=ONE)
    in_specs=[full((L,D))]*4+[row,full((2*L,D)),full((2*L,D))]+w+[full((8,D)),full((8,D)),full((1,FF))]
    SL=-(-max(s,FF//n)//128)*128
    dma=pltpu.SemaphoreType.DMA
    if sq:
        Z,X=shape_of(n)
        grid=14; outs=[(s,D)]*4+[(16,SL)]; kinds=[F32]*5
        scratch=[pltpu.VMEM((Z,X,2,2,s,D),BF)]*2+[pltpu.VMEM((n,16,SL),F32)]*2+[pltpu.VMEM((16,SL),F32)]*2+[dma((n,2)),dma((2,))]
        scratch+=sum_scratch(n,2,s,D,1)*2
        params=dict(collective_id=3,has_side_effects=True)
    else:
        grid=nb+4; outs=[(D,D)]*4+[(1,D)]; kinds=[BF]*4+[F32]
        scratch=[]; params={}
    return pl.pallas_call(functools.partial(last_kernel,n,R,nb,bi),grid=(grid,),in_specs=in_specs,
        out_specs=[row]+[full(o) for o in outs],out_shape=[jax.ShapeDtypeStruct((L,D),F32)]+[jax.ShapeDtypeStruct(o,k) for o,k in zip(outs,kinds)],
        scratch_shapes=scratch,compiler_params=CP(**params),name="last")(x,dq,dk,dv,dz1,em,dr,g,g,g,va,vb,vi)

def local(R,inputs,token_types,buckets,wq,wk,wv,bv,wp,bc,bp,bt,te,wo,bo,ga,sa,wi,b_i,wu,bu,gf,sf,cot):
    s,D=wq.shape; n=D//s; FF=wi.shape[1]; fs=FF//n; kk=FF//D
    SL=-(-max(s,fs)//128)*128
    z=jnp.zeros((s,),BF)
    wide=lambda a: jnp.pad(a,((0,0),(0,SL-a.shape[1])))
    small=jnp.concatenate([wide(jnp.stack([bc,bp,bt,te[0],te[1],bv,z,z,bo,ga,sa,bu,gf,sf])),wide(b_i[None]),jnp.zeros((1,SL),BF)])
    x=inputs[0]
    bk=jnp.pad(buckets,(0,1))[None]
    g1,vec,fb,em,oh=front(R,wq,wk,wv,wp,small,token_types,bk,FF)
    q,k,v,r=project(x,em,g1,vec)
    e,att,linv,g2=att_fwd(R,q,k,v,r,oh,vec,wo,wi,wu)
    out,dz1,datt,dwo,dwi,dwu,dvec2,dbi=middle(x,att,cot[0],g2,vec,fb)
    res=att_bwd(R,q,k,v,r,oh,vec,e,att,linv,datt,dwu,dwi,dwo)
    dq,dk,dv,dr,dvec=res[:5]
    gin,dwq,dwk,dwv,dwp,sv=last(R,x,dq,dk,dv,dz1,em,dr,g1,dvec,dvec2,dbi)
    if is_square(n,R):
        wu_,wi_,wo_=res[5:]
        c=lambda j: sv[j,:s]
        return (out[None],gin[None],dwq,dwk,dwv,c(5),dwp,c(0),c(1),c(2),sv[3:5,:s],wo_,c(8),c(9),c(10),wi_,sv[14,:fs],wu_,c(11),c(12),c(13))
    dbv=sv
    blk=lambda a: a.reshape(n,-1,D)
    r1=jnp.concatenate([blk(dwo),blk(dwi),blk(dwu)],axis=1)
    sv=jnp.concatenate([dbv,dvec[:5],dvec2[:6]]).reshape(12,n,s).transpose(1,0,2).reshape(n,12*s)
    pad=-(12*s+fs)%D
    sv=jnp.concatenate([sv,dbi.reshape(n,fs),jnp.zeros((n,pad),F32)],axis=1).astype(BF).reshape(n,-1,D)
    r2=jnp.concatenate([blk(dwq),blk(dwk),blk(dwv),blk(dwp),sv],axis=1)
    t1=lax.psum_scatter(r1,"shard",scatter_dimension=0,tiled=False).astype(F32)
    t1=lax.psum(t1,"rep")
    t2=lax.psum_scatter(r2,"shard",scatter_dimension=0,tiled=False).astype(F32)
    t2=lax.psum(t2,"rep")
    tv=t2[4*s:].reshape(-1)
    c=lambda j: tv[j*s:(j+1)*s]
    return (out[None],gin[None],t2[:s],t2[s:2*s],t2[2*s:3*s],c(0),t2[3*s:4*s],c(1),c(2),c(3),jnp.stack([c(4),c(5)]),
        t1[:s],c(6),c(7),c(8),jnp.concatenate([t1[(1+j)*s:(2+j)*s] for j in range(kk)],axis=1),tv[12*s:12*s+fs],t1[(1+kk)*s:],c(9),c(10),c(11))

def solution(mesh):
    both=("rep","shard")
    v=P("shard"); w=P("shard",None); a3=P(both,None,None)
    in_specs=(a3,P(both,None),P(),w,w,w,v,w,v,v,v,P(None,"shard"),w,v,v,v,w,v,w,v,v,v,a3)
    out_specs=(a3,a3,w,w,w,v,w,v,v,v,P(None,"shard"),w,v,v,v,w,v,w,v,v,v)
    return jax.shard_map(functools.partial(local,mesh.shape["rep"]),mesh=mesh,in_specs=in_specs,out_specs=out_specs,check_vma=False)
```

```python
import functools, math
import jax, jax.numpy as jnp
from jax import lax
from jax.experimental import pallas as pl
from jax.experimental.pallas import tpu as pltpu
from jax.sharding import PartitionSpec as P
import numpy as np
F32=jnp.float32; BF=jnp.bfloat16
LOG2E=math.log2(math.e); LN2=math.log(2.0)
NT=(((1,),(1,)),((),())); NN=(((1,),(0,)),((),())); TN=(((0,),(0,)),((),()))
def dot(a,b,dims=NN): return lax.dot_general(a,b,dims,preferred_element_type=F32)

def shape_of(n):
    Z=4 if n%8==0 else 1
    return Z,n//(2*Z)

class Place:
    def __init__(self,n,R):
        self.n=n; self.R=R; self.rep=lax.axis_index("rep"); self.Z,self.X=shape_of(n)
        me=lax.axis_index("shard")
        self.me=me; self.c=lax.rem(me,2); q=lax.div(me,2)
        self.x=lax.rem(q,self.X); self.z=lax.div(q,self.X)
    def at(self,z,x,c): return (z*self.X+x)*2+c
    def neighbours(self):
        z,x,c=self.z,self.x,self.c
        out=[(None,self.at(z,x,1-c))]
        if self.Z>1: out+=[(z>0,self.at(z-1,x,c)),(z<self.Z-1,self.at(z+1,x,c))]
        if self.X>1: out+=[(x>0,self.at(z,x-1,c)),(x<self.X-1,self.at(z,x+1,c))]
        return out

def when(cond,fn):
    if cond is None: fn()
    else: pl.when(cond)(fn)

def both(*conds):
    out=None
    for k in conds:
        if k is not None: out=k if out is None else jnp.logical_and(out,k)
    return out

def greet(place):
    bar=pltpu.get_barrier_semaphore()
    total=jnp.int32(0)
    for ok,idx in place.neighbours():
        when(ok,lambda idx=idx: pl.semaphore_signal(bar,inc=1,device_id={"shard":idx},device_id_type=pl.DeviceIdType.MESH))
        total=total+(1 if ok is None else ok.astype(jnp.int32))
    for d in range(1,place.R):
        pl.semaphore_signal(bar,inc=1,device_id={"rep":lax.rem(place.rep+d,place.R)},device_id_type=pl.DeviceIdType.MESH)
    total=total+(place.R-1)
    pl.semaphore_wait(bar,total)

def gather_sems(n):
    Z,X=shape_of(n); A=1+2*(Z-1); J=1+2*(X-1)
    return [pltpu.SemaphoreType.DMA((max(1,2*(Z-1)),2)),pltpu.SemaphoreType.DMA((max(1,A*2*(X-1)),2)),pltpu.SemaphoreType.DMA((A*J,2))]

def gather_events(place,G,sems,t0,dz,dx,last,direct=False):
    p=place; Z,X=p.Z,p.X; zs,xs,cs=sems
    z,x,c=p.z,p.x,p.c
    def copy(idx,sem,k,to):
        return pltpu.make_async_remote_copy(src_ref=G.at[idx],dst_ref=G.at[idx],send_sem=sem.at[k,0],recv_sem=sem.at[k,1],
            device_id={"shard":to},device_id_type=pl.DeviceIdType.MESH)
    ev=[]; sends=[]
    A=1+2*(Z-1); J=1+2*(X-1)
    def slot(a):
        if a==0: return z,None
        s=(a-1)//2
        return (z-1-s,z-1-s>=0) if a%2 else (z+1+s,z+1+s<Z)
    def col(j):
        if j==0: return x,None
        k=(j-1)//2
        return (x-1-k,x-1-k>=0) if j%2 else (x+1+k,x+1+k<X)
    def zmsg(d,s):
        lev=z-s if d==0 else z+s
        ok=both(z+1<Z,z-s>=0) if d==0 else both(z>0,z+s<Z)
        return ok,copy(p.at(lev,x,c),zs,2*s+d,p.at(z+1 if d==0 else z-1,x,c))
    def zarr(d,s):
        lev,ok=slot(1+2*s+d)
        return ok,copy(p.at(lev,x,c),zs,2*s+d,p.at(z,x,1-c))
    def zfar(d,s):
        to=z+1+s if d==0 else z-1-s
        return (to<Z if d==0 else to>=0),copy(p.at(z,x,c),zs,2*s+d,p.at(to,x,c))
    def xmsg(a,d,k):
        lev,va=slot(a)
        cx=x-k if d==0 else x+k
        ok=both(va,x+1<X,x-k>=0) if d==0 else both(va,x>0,x+k<X)
        return ok,copy(p.at(lev,cx,c),xs,(a*(X-1)+k)*2+d,p.at(lev*0+z,x+1 if d==0 else x-1,c))
    def xarr(a,d,k):
        lev,va=slot(a); cx,vc=col(1+2*k+d)
        return both(va,vc),copy(p.at(lev,cx,c),xs,(a*(X-1)+k)*2+d,p.at(z,x,1-c))
    def cmsg(a,j):
        lev,va=slot(a); cx,vc=col(j)
        return both(va,vc),copy(p.at(lev,cx,c),cs,a*J+j,p.at(z,x,1-c))
    def carr(a,j):
        lev,va=slot(a); cx,vc=col(j)
        return both(va,vc),copy(p.at(lev,cx,1-c),cs,a*J+j,p.at(z,x,1-c))
    def add(t,order,fn): ev.append((min(t,last),order,fn))
    def starter(ms):
        def fn():
            for ok,m in ms: when(ok,m.start)
        return fn
    def waiter(ms):
        def fn():
            for ok,m in ms: when(ok,m.wait_recv)
        return fn
    for s in range(Z):
        t=t0+s*dz
        if s>0: add(t,(0,s,0),waiter([zarr(d,s-1) for d in range(2)]))
        if s<Z-1:
            ms=[(zfar if direct else zmsg)(d,s) for d in range(2)]; sends+=ms
            if direct: add(t0,(-0.5,s),starter(ms))
            else: add(t,(0,s,1),starter(ms))
    for a in range(A):
        ra=(a+1)//2; ta=t0+ra*dz
        for k in range(X):
            t=ta+k*dx
            if k>0: add(t,(1,k,a,0),waiter([xarr(a,d,k-1) for d in range(2)]))
            if k<X-1:
                ms=[xmsg(a,d,k) for d in range(2)]; sends+=ms
                add(t,(1,k,a,1),starter(ms))
            ms=[cmsg(a,j) for j in range(J) if (j+1)//2==k]; sends+=ms
            add(t,(1,k,a,2),starter(ms))
    add(last,(2,),waiter([carr(a,j) for a in range(A) for j in range(J)]))
    def done():
        for ok,m in sends: when(ok,m.wait_send)
    add(last,(3,),done)
    ev.sort(key=lambda e:(e[0],e[1]))
    return ev

def square_sems(n):
    Z,X=shape_of(n); A=1+2*(Z-1)
    return [pltpu.SemaphoreType.DMA((2*(Z-1),2)),pltpu.SemaphoreType.DMA((A,2)),pltpu.SemaphoreType.DMA((A,2)),pltpu.SemaphoreType.DMA((3*A,2))]

def square_events(place,G,sems,t0,dz,dx,dy,last,parts=None):
    p=place; Z=p.Z; zs,xs,ys,cs=sems
    z,x,c,rep=p.z,p.x,p.c,p.rep
    lo,parts=parts or (0,G.shape[1]); cut=(parts+1)//2
    halves=((lo,cut),(lo+cut,parts-cut))
    A=1+2*(Z-1)
    def copy(idx,part,sem,k,to):
        ref=G.at[idx,pl.ds(*((lo,parts) if part is None else halves[part]))]
        return pltpu.make_async_remote_copy(src_ref=ref,dst_ref=ref,send_sem=sem.at[k,0],recv_sem=sem.at[k,1],
            device_id=to,device_id_type=pl.DeviceIdType.MESH)
    def slot(a):
        if a==0: return z,None
        s=(a-1)//2
        return (z-1-s,z-1-s>=0) if a%2 else (z+1+s,z+1+s<Z)
    other={"shard":p.at(z,x,1-c)}; across={"shard":p.at(z,1-x,c)}; above={"rep":1-rep}
    def zmsg(d,s):
        lev=z-s if d==0 else z+s
        ok=both(z+1<Z,z-s>=0) if d==0 else both(z>0,z+s<Z)
        return ok,copy(p.at(lev,x,c),None,zs,2*s+d,{"shard":p.at(z+1 if d==0 else z-1,x,c)})
    def zarr(d,s):
        lev,ok=slot(1+2*s+d)
        return ok,copy(p.at(lev,x,c),None,zs,2*s+d,other)
    def xmsg(a,h):
        lev,va=slot(a)
        return both(va,rep==h),copy(p.at(lev,x,c),h,xs,a,across)
    def xarr(a,h):
        lev,va=slot(a)
        return both(va,rep==h),copy(p.at(lev,1-x,c),h,xs,a,across)
    def ymsg(a,h):
        lev,va=slot(a)
        return both(va,rep==h),copy(p.at(lev,1-x,c),h,ys,a,above)
    def yarr(a,h):
        lev,va=slot(a)
        return both(va,rep==1-h),copy(p.at(lev,1-x,c),h,ys,a,above)
    def cmsg(a,h,core):
        lev,va=slot(a); cc=c if core==0 else 1-c
        if h is None: return [(va,copy(p.at(lev,x,cc),None,cs,3*a,other))]
        return [(both(va,rep==(g if h==0 else 1-g)),copy(p.at(lev,1-x,cc),g,cs,3*a+1+h,other)) for g in range(2)]
    ev=[]; sends=[]
    def add(t,order,fn): ev.append((min(t,last),order,fn))
    def start(t,order,ms):
        sends.extend(ms)
        def fn():
            for ok,m in ms: when(ok,m.start)
        add(t,order,fn)
    def await_(t,order,ms):
        def fn():
            for ok,m in ms: when(ok,m.wait_recv)
        add(t,order,fn)
    for s in range(Z):
        t=t0+(dz[s] if isinstance(dz,tuple) else s*dz)
        if s>0: await_(t,(0,s,0),[zarr(d,s-1) for d in range(2)])
        if s<Z-1: start(t,(0,s,1),[zmsg(d,s) for d in range(2)])
        for a in ([0] if s==0 else [2*s-1,2*s]):
            start(t,(1,s,a),[xmsg(a,h) for h in range(2)]+cmsg(a,None,0))
            await_(t+dx,(2,s,a,0),[xarr(a,h) for h in range(2)])
            start(t+dx,(2,s,a,1),[ymsg(a,h) for h in range(2)]+cmsg(a,0,0))
            await_(t+dx+dy,(3,s,a,0),[yarr(a,h) for h in range(2)])
            start(t+dx+dy,(3,s,a,1),cmsg(a,1,0))
    await_(last,(4,),[m for a in range(A) for h in (None,0,1) for m in cmsg(a,h,1)])
    def done():
        for ok,m in sends: when(ok,m.wait_send)
    add(last,(5,),done)
    ev.sort(key=lambda e:(e[0],e[1]))
    return ev

def is_square(n,R): return R==2 and shape_of(n)==(4,2)
def spread_sems(n,R): return square_sems(n) if is_square(n,R) else gather_sems(n)
def spread_events(place,G,sems,t0,dz,dx,dy,last,parts=None):
    if is_square(place.n,place.R): return square_events(place,G,sems,t0,dz,dx,dy,last,parts)
    return gather_events(place,G,sems,t0,dz,dx,last)

def run_events(step,events,after=False):
    picked=[e for e in events if (e[0]-int(e[0])>=0.5)==after]
    for t in sorted({int(e[0]) for e in picked}):
        fns=[e[2] for e in picked if int(e[0])==t]
        def fire(fns=fns):
            for f in fns: f()
        pl.when(step==t)(fire)

def sum_scratch(n,Q,s,D,parts):
    Z,X=shape_of(n); dma=pltpu.SemaphoreType.DMA
    V=lambda *sh: pltpu.VMEM(sh,BF)
    return [V(Z,X,Q,s,D),V(Z,X,Q,s,D),V(Z,Q,s,D//2),V(Z,Q,s,D//2),V(2,Z-1,Q,s,D),V(Q,s,D),
        dma((parts,)),dma((parts,2)),dma((Z,2)),dma((Z,2)),dma((2*(Z-1),2)),dma((1,2))]
SUM_REFS=12

def sum_events(place,srcs,refs,times,store):
    p=place; Z=p.Z
    z,x,c,rep=p.z,p.x,p.c,p.rep
    S,B,YB,XB,ZB,FB,ls,cs,ys,xs,zs,fs=refs
    Q=S.shape[2]; H=S.shape[4]//2
    tc,ta,ty,tx,tz,tend=times
    half=lambda r: pl.ds(pl.multiple_of(r*H,128),H)
    other={"shard":p.at(z,x,1-c)}; across={"shard":p.at(z,1-x,c)}; above={"rep":1-rep}
    def rc(src,dst,sem,k,to):
        return pltpu.make_async_remote_copy(src_ref=src,dst_ref=dst,send_sem=sem.at[k,0],recv_sem=sem.at[k,1],device_id=to,device_id_type=pl.DeviceIdType.MESH)
    ev=[]; sends=[]
    def add(t,order,fn): ev.append((t,order,fn))
    def start(t,order,ms):
        sends.extend(ms)
        def fn():
            for ok,m in ms: when(ok,m.start)
        add(t,order,fn)
    loads=[pltpu.make_async_copy(r.at[:,:,c],S.at[:,:,pl.ds(q,k)],ls.at[j]) for j,(r,q,k) in enumerate(srcs)]
    cores=[(None,rc(r.at[:,:,1-c],B.at[:,:,pl.ds(q,k)],cs,j,other)) for j,(r,q,k) in enumerate(srcs)]
    def plus(a,b): return (a.astype(F32)+b.astype(F32)).astype(BF)
    def begin():
        for m in loads: m.start()
    add(tc,(0,),begin)
    start(tc,(1,),cores)
    def merge():
        for m in loads: m.wait()
        for _,m in cores: m.wait_recv()
        def body(k,_):
            lev=lax.div(k,2*Q); r=lax.rem(k,2*Q); xx=lax.div(r,Q); q=lax.rem(r,Q)
            S[lev,xx,q]=plus(S[lev,xx,q],B[lev,xx,q])
            return 0
        lax.fori_loop(0,2*Z*Q,body,0)
    add(ta,(2,),merge)
    def levels(d): return [(z,None)] if d==0 else [(z-d,z-d>=0),(z+d,z+d<Z)]
    for i,d in enumerate(range(Z-1,-1,-1)):
        L=levels(d)
        ysend=[(ok,rc(S.at[l,1-x,:,:,half(1-rep)],YB.at[l],ys,l,above)) for l,ok in L]
        xsend=[(ok,rc(S.at[l,1-x,:,:,half(rep)],XB.at[l],xs,l,across)) for l,ok in L]
        start(ty[i],(3,i),ysend)
        def ytake(L=L,ysend=ysend):
            for (l,ok),(_,m) in zip(L,ysend):
                def go(l=l,m=m):
                    m.wait_recv()
                    def body(q,_):
                        S[l,1-x,q,:,half(rep)]=plus(S[l,1-x,q,:,half(rep)],YB[l,q])
                        return 0
                    lax.fori_loop(0,Q,body,0)
                when(ok,go)
        add(tx[i],(4,i,0),ytake)
        start(tx[i],(4,i,1),xsend)
        def xtake(L=L,xsend=xsend):
            for (l,ok),(_,m) in zip(L,xsend):
                def go(l=l,m=m):
                    m.wait_recv()
                    def body(q,_):
                        S[l,x,q,:,half(rep)]=plus(S[l,x,q,:,half(rep)],XB[l,q])
                        return 0
                    lax.fori_loop(0,Q,body,0)
                when(ok,go)
        add(tz[i],(5,i,0),xtake)
        if d<=Z-2:
            def ztake(d=d):
                for dr,(l,ok) in enumerate([(z-d,both(z+1<Z,z-d>=0)),(z+d,both(z>0,z+d<Z))]):
                    def go(dr=dr,l=l):
                        rc(ZB.at[dr,d],ZB.at[dr,d],zs,2*d+dr,other).wait_recv()
                        def body(q,_):
                            S[l,x,q]=plus(S[l,x,q],ZB[dr,d,q])
                            return 0
                        lax.fori_loop(0,Q,body,0)
                    pl.when(ok)(go)
            add(tz[i],(5,i,1),ztake)
        if d>=1:
            start(tz[i],(5,i,2),[(z-d>=0,rc(S.at[z-d,x],ZB.at[0,d-1],zs,2*(d-1),{"shard":p.at(z-1,x,c)})),
                (z+d<Z,rc(S.at[z+d,x],ZB.at[1,d-1],zs,2*(d-1)+1,{"shard":p.at(z+1,x,c)}))])
    final=[(None,rc(S.at[z,x],FB,fs,0,above))]
    start(tz[-1],(6,),final)
    def finish():
        final[0][1].wait_recv()
        for q in range(Q): store(q,S[z,x,q].astype(F32)+FB[q].astype(F32))
    add(tend,(7,),finish)
    def done():
        for ok,m in sends: when(ok,m.wait_send)
    add(tend,(8,),done)
    return ev

def greet_all(place):
    bar=pltpu.get_barrier_semaphore()
    n,R=place.n,place.R
    def hello(d,_):
        pl.semaphore_signal(bar,inc=1,device_id={"shard":lax.rem(place.me+d,n)},device_id_type=pl.DeviceIdType.MESH)
        return 0
    lax.fori_loop(1,n,hello,0)
    for d in range(1,R):
        pl.semaphore_signal(bar,inc=1,device_id={"rep":lax.rem(place.rep+d,R)},device_id_type=pl.DeviceIdType.MESH)
    return lambda: pl.semaphore_wait(bar,n+R-2)

STRIDE=32
def tables(length,width):
    half=width//2; count=2*length//STRIDE
    rates=np.exp(np.arange(half)*(-2.0*math.log(10000.0)/width))
    def pack(angles):
        full=np.concatenate([np.sin(angles),np.cos(angles)],axis=1).astype(np.float32)
        hi=full.astype(jnp.bfloat16); lo=(full-hi.astype(np.float32)).astype(jnp.bfloat16)
        return np.concatenate([hi,lo],axis=0)
    coarse=(np.arange(count)*STRIDE-length)[:,None]*rates[None]
    fine=np.arange(STRIDE)[:,None]*rates[None]
    return pack(coarse),pack(fine)

BI=256
ONE=pl.Buffered(1)


def lane_half(rows, lanes):
    lane=lax.broadcasted_iota(jnp.int32,(rows,lanes),1)
    return (lane//64)%2

def split_hi_lo(v):
    hi=v.astype(BF); return hi,(v-hi.astype(F32)).astype(BF)

def queries(q, vec, oh):
    s=0.125*LOG2E
    cq=((q+vec[0:1])*s).astype(BF)
    pq=((q+vec[1:2])*s).astype(BF)
    tq=(q+vec[2:3])*0.125
    return cq,pq,tq

GL=256

def fore_kernel(n,R,x_ref,wq_ref,wk_ref,wv_ref,wp_ref,wo_ref,wi_ref,wu_ref,small_ref,kinds_ref,buckets_ref,ta_ref,tb_ref,
        e_ref,att_ref,linv_ref,q_ref,k_ref,v_ref,r_ref,g_ref,w0_ref,w1_ref,w2_ref,vec_ref,bi_ref,oh_ref,xt_ref,et_ref,
        em,wg,all_s,mine,own,own2,ssem,*sems):
    bi=att_ref.shape[0]; L=x_ref.shape[0]; W=L+bi
    pair=pl.program_id(0); i=pl.program_id(1); nb=L//bi
    step=pair*nb+i; steps=6*nb
    place=Place(n,R); me=place.me
    kk=wu_ref.shape[0]; D=wo_ref.shape[1]
    groups=D//GL; per=len(spread_sems(n,R)); square=is_square(n,R); gs=len(gather_sems(n))
    ws=(wq_ref,wk_ref,wv_ref,wp_ref)
    loads=[[pltpu.make_async_copy(w.at[:,pl.ds(g*GL,GL)],wg.at[g,me,j],own2.at[g,j]) for j,w in enumerate(ws)] for g in range(groups)]
    keeps=[pltpu.make_async_copy(wg.at[g],o,own2.at[g,4]) for g,o in enumerate((w0_ref,w1_ref,w2_ref))]
    owns=[pltpu.make_async_copy(wu_ref,mine.at[pl.ds(0,kk)],own.at[0]),pltpu.make_async_copy(wo_ref,mine.at[kk],own.at[1])]
    owns+=[pltpu.make_async_copy(wi_ref.at[:,pl.ds(j*D,D)],mine.at[kk+1+j],own.at[2+j]) for j in range(kk)]
    keep=pltpu.make_async_copy(mine,g_ref.at[me],own.at[2+kk])
    def send(d):
        return pltpu.make_async_remote_copy(src_ref=all_s.at[me],dst_ref=all_s.at[me],send_sem=ssem.at[d,0],recv_sem=ssem.at[d,1],
            device_id={"shard":lax.rem(me+d,n)},device_id_type=pl.DeviceIdType.MESH)
    def arrive(d):
        w=lax.rem(me-d+n,n)
        return pltpu.make_async_remote_copy(src_ref=all_s.at[w],dst_ref=all_s.at[w],send_sem=ssem.at[d,0],recv_sem=ssem.at[d,1],
            device_id={"shard":lax.rem(me+d,n)},device_id_type=pl.DeviceIdType.MESH)
    def enter():
        for g in range(groups):
            for m in loads[g]: m.start()
        for m in owns: m.start()
        met=greet_all(place)
        all_s[me]=small_ref[...]
        for g in range(groups):
            for m in loads[g]: m.wait()
        met()
    def share():
        def go(d,_):
            send(d).start()
            return 0
        lax.fori_loop(1,n,go,0)
    def enter2():
        for m in owns: m.wait()
        keep.start()
    def prepare():
        L2=buckets_ref.shape[1]
        count=L2//STRIDE
        def body(j,_):
            rows=pl.ds(pl.multiple_of(j*256,256),256)
            b=buckets_ref[:,rows]
            hot=lambda v,m: jnp.where(v==lax.rem(lax.broadcasted_iota(jnp.int32,(2*m,256),0),m),1.0,0.0).astype(BF)
            A=dot(hot(lax.div(b,STRIDE),count),ta_ref[...],TN)
            B=dot(hot(lax.rem(b,STRIDE),STRIDE),tb_ref[...],TN)
            h=A.shape[1]//2
            sa,ca,sb,cb=A[:,:h],A[:,h:],B[:,:h],B[:,h:]
            both_=jnp.concatenate([sa*cb+ca*sb,ca*cb-sa*sb],axis=1)
            em[rows,:]=both_.astype(BF)
            et_ref[:,rows]=both_.T.astype(BF)
            return 0
        lax.fori_loop(0,L2//256,body,0)
        def turn(j,_):
            rows=pl.ds(pl.multiple_of(j*256,256),256)
            xt_ref[:,rows]=x_ref[rows,:].astype(F32).T.astype(BF)
            return 0
        lax.fori_loop(0,L//256,turn,0)
        for j in range(L//256):
            kinds=kinds_ref[:,j*256:(j+1)*256]
            lane=lax.rem(lax.broadcasted_iota(jnp.int32,(128,256),0),64)
            hot=jnp.where((lax.rem(lane,3)==kinds)&(lane<6),1.0,0.0)
            oh_ref[j*256:(j+1)*256,:]=hot.T.astype(BF)
    def unpack():
        def come(d,_):
            arrive(d).wait_recv()
            send(d).wait_send()
            return 0
        lax.fori_loop(1,n,come,0)
        s=wq_ref.shape[0]; fs=bi_ref.shape[1]//n
        for w in range(n):
            a=all_s[w].astype(F32)
            vec_ref[:,w*s:(w+1)*s]=a[:,:s]
            bi_ref[:,w*fs:(w+1)*fs]=a[14:15,:fs]
    def project(g):
        col=lambda j: wg[g,:,j].reshape(D,GL)
        def rows_of(j,_):
            rows=pl.ds(pl.multiple_of(j*256,256),256)
            x=x_ref[rows,:]
            q_ref[rows,:]=dot(x,col(0))
            k_ref[rows,:]=dot(x,col(1)).astype(BF)
            v_ref[rows,:]=(dot(x,col(2))+vec_ref[5:6,g*GL:(g+1)*GL]).astype(BF)
            rows2=pl.ds(pl.multiple_of(j*512,512),512)
            r_ref[rows2,:]=dot(em[rows2,:],col(3)).astype(BF)
            return 0
        lax.fori_loop(0,L//256,rows_of,0)
    ev=[(0,(-2,),enter),(0,(1.5,),share),(0.001,(9,),prepare),(0.1,(9,),unpack),(1,(-1,),enter2),(2,(-1,),keep.wait)]
    for g,(t0,dz,dx,dy,end) in enumerate(FORE_TIMES):
        if g==0: ev+=gather_events(place,wg.at[g],sems[:gs],t0,dz,dx,end,square)
        else: ev+=spread_events(place,wg.at[g],sems[gs+(g-1)*per:gs+g*per],t0,dz,dx,dy,end)
        ev.append((end,(9,),keeps[g].start))
        ev.append((end,(10,),functools.partial(project,g)))
        ev.append((steps-0.5,(9,g),keeps[g].wait))
    rest=sems[gs+(groups-1)*per:]
    if square:
        for k,(lo,cnt) in enumerate(((0,kk),(kk,kk+1))):
            ev+=square_events(place,g_ref,rest[k*per:(k+1)*per],*FORE_REST[k],steps-0.5,(lo,cnt))
    else: ev+=spread_events(place,g_ref,rest[:per],2,6,4,4,steps-0.5)
    ev.sort(key=lambda e:(e[0],e[1]))
    run_events(step,ev)
    side=pl.ds(pl.multiple_of(lax.rem(pair,2)*128,128),128)
    vec=vec_ref[0:8,pl.ds(pl.multiple_of(pair*128,128),128)]
    rows=pl.ds(pl.multiple_of(i*bi,bi),bi)
    q=q_ref[rows,side]
    oh_i=oh_ref[rows,:]
    cq,pq,tq=queries(q,vec,None)
    rr=lax.broadcasted_iota(jnp.int32,(256,128),0)%128
    cc=lax.broadcasted_iota(jnp.int32,(256,128),1)
    M=jnp.where((rr//64==cc//64)&(cc%64<6),1.0,0.0).astype(BF)
    def tt(te):
        hi,lo=split_hi_lo(tq*(te*LOG2E))
        return dot(jnp.concatenate([hi,lo],axis=1),M)
    t0=tt(vec[3:4]); t1=tt(vec[4:5])
    tv=jnp.where(oh_i>0,t1,t0)
    hi=tv.astype(BF).astype(F32)
    lane=lax.broadcasted_iota(jnp.int32,(bi,128),1)
    tv=jnp.where(lane%64<3,hi,tv-hi).astype(BF)
    half=lane_half(bi,128)
    kext=jnp.concatenate([k_ref[:,side],oh_ref[...]],axis=1)
    vext=jnp.concatenate([v_ref[:,side],jnp.ones((L,128),BF)],axis=1)
    w0=pl.multiple_of(L-bi-i*bi,bi)
    rwin=r_ref[pl.ds(w0,W),side]
    z=jnp.zeros((),BF)
    outs=[]
    for h in range(2):
        qx=jnp.concatenate([jnp.where(half==h,cq,z),jnp.where(half==h,tv,z)],axis=1)
        pos=dot(jnp.where(half==h,pq,z),rwin,NT)
        pos=pltpu.roll(pos,W-(bi-1),1,stride=1,stride_axis=0)[:,:L]
        s=dot(qx,kext,NT)+pos
        m=jnp.max(s,axis=1,keepdims=True)
        e=jnp.exp2(s-m).astype(BF)
        e_ref[h]=e
        o=dot(e,vext)
        li=1.0/o[:,128:]
        outs.append((o[:,:128]*li,li))
    att_ref[...]=jnp.where(half==0,outs[0][0],outs[1][0]).astype(BF)
    linv_ref[...]=jnp.where(half==0,outs[0][1],outs[1][1])
    run_events(step,ev,after=True)

FORE_TIMES=((0.0,0.01,0.01,0.01,0.1),(0.2,1,1,1,8.0),(1.2,1,1,1,16.0))
FORE_REST=((4,(0,3,8,13),2,3),(4.01,(0,6,11,16),2,2))

def fore(R,x,wq,wk,wv,wp,wo,wi,wu,small,kinds,buckets,bi=BI):
    L,D=x.shape; P=D//128; nb=L//bi; s=wo.shape[0]; n=D//s; kk=wu.shape[0]//s; FF=wi.shape[1]; SL=small.shape[1]
    ta,tb=tables(L,D)
    hbm=pl.BlockSpec(memory_space=pl.ANY)
    full=lambda a: pl.BlockSpec(a.shape,lambda p,i:(0,)*len(a.shape),pipeline_mode=ONE)
    S=jax.ShapeDtypeStruct
    tile=pl.BlockSpec((bi,128),lambda p,i:(i,p))
    col=lambda k: pl.BlockSpec((k*L,GL),lambda p,i:(0,p//2))
    ta,tb=jnp.asarray(ta),jnp.asarray(tb)
    tails=[S((16,D),F32),S((1,FF),F32),S((L,128),BF),S((D,L),BF),S((D,2*L),BF)]
    dma=pltpu.SemaphoreType.DMA
    return pl.pallas_call(functools.partial(fore_kernel,n,R),grid=(P,nb),
        in_specs=[full(x)]+[hbm]*7+[full(a) for a in (small,kinds,buckets,ta,tb)],
        out_specs=[pl.BlockSpec((2,bi,L),lambda p,i:(p,i,0)),tile,tile,col(1),col(1),col(1),col(2)]+[hbm]*4+[full(t) for t in tails],
        out_shape=[S((2*P,L,L),BF),S((L,D),BF),S((L,D),F32),S((L,D),F32),S((L,D),BF),S((L,D),BF),S((2*L,D),BF),S((n,2*kk+1,s,D),BF)]
            +[S((n,4,s,GL),BF)]*3+tails,
        scratch_shapes=[pltpu.VMEM((2*L,D),BF),pltpu.VMEM((D//GL,n,4,s,GL),BF),pltpu.VMEM((n,16,SL),BF),pltpu.VMEM((2*kk+1,s,D),BF),
            dma((3+kk,)),dma((D//GL,5)),dma((n,2))]+gather_sems(n)+spread_sems(n,R)*(D//GL+1),
        compiler_params=pltpu.CompilerParams(vmem_limit_bytes=60*2**20,dimension_semantics=("arbitrary","arbitrary"),collective_id=1,has_side_effects=True),
        name="fore")(x,wq,wk,wv,wp,wo,wi,wu.reshape(kk,s,D),small,kinds,buckets,ta,tb)

TIMES_A=(0,2,(2,3,4,6),(4,5,7,8),(6,9,12,15),18)
TIMES_B=(1,4,(5,6,8,10),(7,8,11,12),(11,15,18,21),23)
TIMES_G=((8,9,(9,9,10,10),(11,11,12,12),(13,14,15,16),18),
    (16,17,(17,17,18,18),(18,19,19,20),(20,21,22,23),23),
    (23.5,23.5,(23.5,)*4,(23.5,)*4,(23.5,)*4,23.5))

def bwd_kernel(n,R,roll_bf,q_ref,k_ref,v_ref,r_ref,oh_ref,vec_ref,e_ref,att_ref,linv_ref,datt_ref,*rest):
    bi=q_ref.shape[0]; L=k_ref.shape[0]; W=L+bi
    pair=pl.program_id(0); i=pl.program_id(1); nb=L//bi; step=pair*nb+i
    square=is_square(n,R)
    if square:
        gu_ref,gi_ref,go_ref,xt_ref,et_ref,vb_ref,vi_ref=rest[:7]
        dq_ref,dk_ref,dv_ref,wu_ref,wi_ref,wo_ref,g0_ref,g1_ref,g2_ref,sv_ref=rest[7:17]
        dk_acc,dv_acc,dr_acc,dvec_ref,dq2,dk2,dv2,dr2,vec_s,src0,src1,src2,piece,came,total,theirs,ss,ts=rest[17:35]
        refs=rest[35:]
        s,D=wo_ref.shape; kk=wu_ref.shape[0]//s
        def store_a(q,v): wu_ref[q*s:(q+1)*s,:]=v
        def store_b(q,v):
            if q<kk: wi_ref[:,q*D:(q+1)*D]=v
            else: wo_ref[...]=v
        place=Place(n,R); Z,X=place.Z,place.X; me=place.me
        ev=[(0,(-1,),lambda: greet_all(place)())]
        ev+=sum_events(place,[(gu_ref,0,kk)],refs[:SUM_REFS],TIMES_A,store_a)
        ev+=sum_events(place,[(gi_ref,0,kk),(go_ref,kk,1)],refs[SUM_REFS:2*SUM_REFS],TIMES_B,store_b)
        for g,(src,out) in enumerate(((src0,g0_ref),(src1,g1_ref),(src2,g2_ref))):
            def store_g(q,v,out=out): out[q]=v
            ev+=sum_events(place,[(src,0,4)],refs[(2+g)*SUM_REFS:(3+g)*SUM_REFS],TIMES_G[g],store_g)
            def weights(src=src):
                for j,(l,r) in enumerate(((xt_ref,dq2),(xt_ref,dk2),(xt_ref,dv2),(et_ref,dr2))):
                    src[:,:,:,j]=dot(l[...],r[...]).astype(BF).reshape(Z,X,2,s,GL)
            ev.append(((2*g+2)*nb-0.5,(-1,),weights))
        def send(d):
            w=lax.rem(me+d,n)
            return pltpu.make_async_remote_copy(src_ref=piece.at[w],dst_ref=came.at[me],send_sem=ss.at[d,0],recv_sem=ss.at[d,1],
                device_id={"shard":w},device_id_type=pl.DeviceIdType.MESH)
        def arrive(d):
            w=lax.rem(me-d+n,n)
            return pltpu.make_async_remote_copy(src_ref=piece.at[w],dst_ref=came.at[w],send_sem=ss.at[d,0],recv_sem=ss.at[d,1],
                device_id={"shard":w},device_id_type=pl.DeviceIdType.MESH)
        swap=pltpu.make_async_remote_copy(src_ref=total,dst_ref=theirs,send_sem=ts.at[0],recv_sem=ts.at[1],
            device_id={"rep":1-place.rep},device_id_type=pl.DeviceIdType.MESH)
        def give():
            fs=vi_ref.shape[1]//n
            rows=jnp.concatenate([vec_s[...],vb_ref[...]],axis=0)
            for w in range(n):
                piece[w,:,:s]=rows[:,w*s:(w+1)*s]
                piece[w,14:15,:fs]=vi_ref[:,w*fs:(w+1)*fs]
            came[me]=piece[me]
            def go(d,_):
                send(d).start()
                return 0
            lax.fori_loop(1,n,go,0)
        def collect():
            def go(d,_):
                arrive(d).wait_recv()
                return 0
            lax.fori_loop(1,n,go,0)
            acc=came[0]
            for w in range(1,n): acc=acc+came[w]
            total[...]=acc
            swap.start()
        def close():
            swap.wait_recv()
            sv_ref[...]=total[...]+theirs[...]
            swap.wait_send()
            def go(d,_):
                send(d).wait_send()
                return 0
            lax.fori_loop(1,n,go,0)
        end=6*nb-0.5
        ev+=[(end,(1.5,),give),(end,(4.5,),collect),(end,(6.5,),close)]
        ev.sort(key=lambda e:(e[0],e[1]))
        run_events(step,ev)
    else:
        dq_ref,dk_ref,dv_ref,dr_ref,dvec_ref,dk_acc,dv_acc,dr_acc=rest
    vec=vec_ref[...]
    q=q_ref[...]
    oh_i=oh_ref[pl.ds(pl.multiple_of(i*bi,bi),bi),:].astype(F32)
    cq,pq,tq=queries(q,vec,None)
    half=lane_half(bi,128)
    lane=lax.broadcasted_iota(jnp.int32,(bi,128),1)
    @pl.when(i==0)
    def _():
        dk_acc[...]=jnp.zeros_like(dk_acc); dv_acc[...]=jnp.zeros_like(dv_acc); dr_acc[...]=jnp.zeros_like(dr_acc)
        dvec_ref[...]=jnp.zeros_like(dvec_ref)
    P=jnp.where(lax.broadcasted_iota(jnp.int32,(bi,bi),0)+lax.broadcasted_iota(jnp.int32,(bi,bi),1)==bi-1,1.0,0.0).astype(BF)
    pqr=dot(P,pq).astype(BF)
    kext=jnp.concatenate([k_ref[...],oh_ref[...]],axis=1)
    ones2=jnp.where(lax.broadcasted_iota(jnp.int32,(L,128),1)<2,1.0,0.0).astype(BF)
    vext=jnp.concatenate([v_ref[...],ones2],axis=1)
    w0=pl.multiple_of(L-bi-i*bi,bi)
    rwin=r_ref[pl.ds(w0,W),:]
    z=jnp.zeros((),BF)
    dattl=datt_ref[...].astype(F32)*linv_ref[...]
    prod=dattl*att_ref[...].astype(F32)
    dattl=dattl.astype(BF)
    dcs=[];dps=[];dts=[];tes=[]
    dk=None; dv=None; dr=None
    for h in range(2):
        delta=-jnp.sum(jnp.where(half==h,prod,0.0),axis=1,keepdims=True)
        dhi=delta.astype(BF).astype(F32)
        dx=jnp.where(lane==0,dhi,jnp.where(lane==1,delta-dhi,0.0)).astype(BF)
        dm=jnp.where(half==h,dattl,z)
        dpd=dot(jnp.concatenate([dm,dx],axis=1),vext,NT)
        e=e_ref[h]
        ds=(e.astype(F32)*dpd).astype(BF)
        dvh=dot(e,dm,TN)
        dkh=dot(ds,jnp.where(half==h,cq,z),TN)
        dc=dot(ds,kext)
        rev=dot(P,ds)
        if roll_bf: rev=rev.astype(BF)
        rev=jnp.concatenate([rev,jnp.zeros((bi,W-L),rev.dtype)],axis=1)
        dpr=pltpu.roll(rev,0,1,stride=1,stride_axis=0).astype(BF)
        dp=dot(dpr,rwin)
        drh=dot(dpr,jnp.where(half==h,pqr,z),TN)
        dv=dvh if dv is None else dv+dvh
        dk=dkh if dk is None else dk+dkh
        dr=drh if dr is None else dr+drh
        D=jnp.where(lane<3,dc[:,128:],0.0)
        dall=jnp.sum(D,axis=1,keepdims=True)
        d1=jnp.sum(D*oh_i,axis=1,keepdims=True)
        d0=dall-d1
        dcs.append(dc[:,:128]); dps.append(dp)
        dts.append(d0*vec[3:4]+d1*vec[4:5])
        tes.append((d0,d1))
    dv_acc[...]+=dv
    dk_acc[...]+=dk
    dr_acc[pl.ds(w0,W),:]+=dr
    dcq=jnp.where(half==0,dcs[0],dcs[1]).astype(BF).astype(F32)
    dpr=jnp.where(half==0,dps[0],dps[1]).astype(BF)
    dpq=dot(P,dpr)
    dtq=jnp.where(half==0,dts[0],dts[1])
    dq=((dcq+dpq+dtq)*0.125).astype(BF)
    dq_ref[...]=dq
    d0=jnp.where(half==0,tes[0][0],tes[1][0]); d1=jnp.where(half==0,tes[0][1],tes[1][1])
    rows=[dcq*0.125,dpq*0.125,dtq*0.125,d0*tq,d1*tq]
    sums=[jnp.sum(v,axis=0,keepdims=True) for v in rows]+[jnp.zeros((3,128),F32)]
    dvec_ref[...]+=jnp.concatenate(sums,axis=0)
    @pl.when(i==nb-1)
    def _():
        dk=(dk_acc[...]*LN2).astype(BF); dv=dv_acc[...].astype(BF); dr=(dr_acc[...]*LN2).astype(BF)
        dk_ref[...]=dk
        dv_ref[...]=dv
        if square:
            side=pl.ds(pl.multiple_of(lax.rem(pair,2)*128,128),128)
            dk2[:,side]=dk; dv2[:,side]=dv; dr2[:,side]=dr
            cols=pl.ds(pl.multiple_of(pair*128,128),128)
            vec_s[0:5,cols]=dvec_ref[0:5,:]
            vec_s[5:6,cols]=rowsum(dv.astype(F32))
            vec_s[6:8,cols]=jnp.zeros((2,128),F32)
        else: dr_ref[...]=dr
    if square:
        dq2[pl.ds(pl.multiple_of(i*bi,bi),bi),pl.ds(pl.multiple_of(lax.rem(pair,2)*128,128),128)]=dq
        run_events(step,ev,after=True)

def att_bwd(R,q,k,v,r,oh,vec,e,att,linv,datt,dwu,dwi,dwo,xt,et,vb,vi,bi=BI,roll_bf=False):
    L,D=q.shape; P=D//128; nb=L//bi; n,kk,s,_=dwu.shape
    col=pl.BlockSpec((L,128),lambda p,i:(0,p)); tile=pl.BlockSpec((bi,128),lambda p,i:(i,p))
    full=lambda sh: pl.BlockSpec(sh,lambda p,i:(0,)*len(sh),pipeline_mode=ONE)
    in_specs=[tile,col,col,pl.BlockSpec((2*L,128),lambda p,i:(0,p)),pl.BlockSpec((L,128),lambda p,i:(0,0)),
        pl.BlockSpec((8,128),lambda p,i:(0,p)),pl.BlockSpec((2,bi,L),lambda p,i:(p,i,0)),tile,tile,tile]
    out_specs=[tile,col,col]
    out_shape=[jax.ShapeDtypeStruct((L,D),BF)]*3
    scratch=[pltpu.VMEM((L,128),F32),pltpu.VMEM((L,128),F32),pltpu.VMEM((2*L,128),F32)]
    args=[q,k,v,r,oh,vec,e,att,linv,datt]
    params=dict(vmem_limit_bytes=62*2**20,dimension_semantics=("arbitrary","arbitrary"))
    if is_square(n,R):
        Z,X=shape_of(n); FF=vi.shape[1]; SL=-(-max(s,FF//n)//128)*128
        in_specs+=[pl.BlockSpec(memory_space=pl.ANY)]*3+[full((D,L)),full((D,2*L)),full((8,D)),full((1,FF))]
        for sh in ((kk*s,D),(s,kk*D),(s,D),(4,s,GL),(4,s,GL),(4,s,GL),(16,SL)):
            out_specs.append(full(sh)); out_shape.append(jax.ShapeDtypeStruct(sh,F32))
        dma=pltpu.SemaphoreType.DMA
        scratch+=[pltpu.VMEM((8,128),F32)]+[pltpu.VMEM((L,GL),BF)]*3+[pltpu.VMEM((2*L,GL),BF),pltpu.VMEM((8,D),F32)]
        scratch+=[pltpu.VMEM((Z,X,2,4,s,GL),BF)]*3+[pltpu.VMEM((n,16,SL),F32)]*2+[pltpu.VMEM((16,SL),F32)]*2+[dma((n,2)),dma((2,))]
        scratch+=sum_scratch(n,kk,s,D,1)+sum_scratch(n,kk+1,s,D,2)+sum_scratch(n,4,s,GL,1)*3
        args+=[dwu.reshape(Z,X,2,kk,s,D),dwi.reshape(Z,X,2,kk,s,D),dwo.reshape(Z,X,2,1,s,D),xt,et,vb,vi]
        params.update(collective_id=2,has_side_effects=True)
    else:
        out_specs+=[pl.BlockSpec((2*L,128),lambda p,i:(0,p)),pl.BlockSpec((8,128),lambda p,i:(0,p))]
        out_shape+=[jax.ShapeDtypeStruct((2*L,D),BF),jax.ShapeDtypeStruct((8,D),F32)]
    return pl.pallas_call(functools.partial(bwd_kernel,n,R,roll_bf),grid=(P,nb),in_specs=in_specs,out_specs=out_specs,out_shape=out_shape,
        scratch_shapes=scratch,compiler_params=pltpu.CompilerParams(**params),
        name="attend_back")(*args)

CP=lambda **k: pltpu.CompilerParams(vmem_limit_bytes=60*2**20,**k)
C0=math.sqrt(2.0/math.pi); C1=0.044715
EPS=1e-6

def whole(ref):
    a=ref[...]
    return a.reshape(-1,a.shape[-1])

def ln_stats(z):
    n=z.shape[1]
    mu=jnp.sum(z,axis=1,keepdims=True)*(1.0/n)
    c=z-mu
    var=jnp.sum(c*c,axis=1,keepdims=True)*(1.0/n)
    r=lax.rsqrt(var+EPS)
    return c*r,r

def ln_back(g,zhat,r):
    n=g.shape[1]
    a=jnp.sum(g,axis=1,keepdims=True)*(1.0/n)
    b=jnp.sum(g*zhat,axis=1,keepdims=True)*(1.0/n)
    return r*(g-a-zhat*b)

def rowsum(v): return jnp.sum(v,axis=0,keepdims=True)

def mid_kernel(nb,bi,nc,x_ref,att_ref,cot_ref,wo_ref,wu_ref,*rest):
    wi_refs=rest[:nc]
    (vec_ref,bi_ref,out_ref,dz1_ref,datt_ref,dwo_ref,dwi_ref,dwu_ref,dvec_ref,dbi_ref,
        mid_s,att_s,dffn_s,dattn_s,hid_s,din_s,acc_s)=rest[nc:]
    t=pl.program_id(0)
    D=x_ref.shape[1]; fc=D
    n=wu_ref.shape[0]; per=n//nc
    wu=lambda c: wu_ref[c*per:(c+1)*per].reshape(fc,D)
    wi=lambda c: whole(wi_refs[c])
    @pl.when(t==0)
    def _():
        dvec_ref[...]=jnp.zeros_like(dvec_ref); dbi_ref[...]=jnp.zeros_like(dbi_ref)
    @pl.when(t<nb)
    def _():
        rows=pl.ds(pl.multiple_of(t*bi,bi),bi)
        b_out,ga,sa,b_outer,gf,sf=[vec_ref[k:k+1,:] for k in range(6)]
        att=att_ref[...]
        att_s[rows,:]=att
        z1=x_ref[...].astype(F32)+dot(att,whole(wo_ref))+b_out
        zh1,r1=ln_stats(z1)
        middle=zh1*ga+sa
        mid=middle.astype(BF)
        mid_s[rows,:]=mid
        acc_s[...]=middle+b_outer
        for c in range(nc):
            cs=slice(c*fc,(c+1)*fc)
            v=dot(mid,wi(c))+bi_ref[:,cs]
            u=v*v
            th=jnp.tanh(v*(C0+(C0*C1)*u))
            hv=0.5*v
            hid=(hv+hv*th).astype(BF)
            dg=0.5+0.5*th+hv*(1.0-th*th)*(C0+(3*C0*C1)*u)
            hid_s[rows,cs]=hid
            din_s[rows,cs]=dg.astype(BF)
            acc_s[...]+=dot(hid,wu(c))
        zh2,r2=ln_stats(acc_s[...])
        out_ref[...]=(zh2*gf+sf).astype(BF)
        g=cot_ref[...].astype(F32)
        dz2=ln_back(g*gf,zh2,r2)
        dffn=dz2.astype(BF)
        dffn_s[rows,:]=dffn
        acc_s[...]=dz2
        dbs=[]
        for c in range(nc):
            cs=slice(c*fc,(c+1)*fc)
            dh=dot(dffn,wu(c),NT)
            din=(dh*din_s[rows,cs].astype(F32)).astype(BF)
            din_s[rows,cs]=din
            dbi_ref[:,cs]+=rowsum(din.astype(F32))
            acc_s[...]+=dot(din,wi(c),NT)
        dm=acc_s[...]
        dz1=ln_back(dm*ga,zh1,r1)
        dz1_ref[...]=dz1
        dattn=dz1.astype(BF)
        dattn_s[rows,:]=dattn
        datt_ref[...]=dot(dattn,whole(wo_ref),NT).astype(BF)
        dvec_ref[...]+=jnp.concatenate([rowsum(dz1),rowsum(dm*zh1),rowsum(dm),rowsum(dz2),rowsum(g*zh2),rowsum(g),jnp.zeros((2,D),F32)],axis=0)
    @pl.when(t==nb)
    def _():
        dwo_ref[...]=dot(att_s[...],dattn_s[...],TN).astype(BF).reshape(dwo_ref.shape)
    for c in range(nc):
        cs=slice(c*fc,(c+1)*fc)
        @pl.when(t==nb+c)
        def _():
            dwi_ref[...]=dot(mid_s[...],din_s[:,cs],TN).astype(BF).reshape(dwi_ref.shape)
            dwu_ref[...]=dot(hid_s[:,cs],dffn_s[...],TN).astype(BF).reshape(dwu_ref.shape)

def middle(x,att,cot,g,vec,b_inner,bi=256):
    L,D=x.shape; n,parts,s,_=g.shape; nc=(parts-1)//2; FF=nc*D; nb=L//bi; per=n//nc
    row=pl.BlockSpec((bi,D),lambda t:(jnp.minimum(t,nb-1),0))
    cc=lambda t: jnp.clip(t-nb,0,nc-1)
    w=lambda j: pl.BlockSpec((n,1,s,D),lambda t:(0,j,0,0),pipeline_mode=ONE)
    return pl.pallas_call(functools.partial(mid_kernel,nb,bi,nc),grid=(nb+nc,),
        in_specs=[row,row,row,w(nc),pl.BlockSpec((n,nc,s,D),lambda t:(0,0,0,0),pipeline_mode=ONE)]+[w(nc+1+j) for j in range(nc)]
            +[pl.BlockSpec((8,D),lambda t:(1,0)),pl.BlockSpec((1,FF),lambda t:(0,0))],
        out_specs=[row,row,row,pl.BlockSpec((n,s,D),lambda t:(0,0,0)),pl.BlockSpec((n,1,s,D),lambda t:(0,cc(t),0,0)),
            pl.BlockSpec((per,nc,s,D),lambda t:(cc(t),0,0,0)),
            pl.BlockSpec((8,D),lambda t:(0,0)),pl.BlockSpec((1,FF),lambda t:(0,0))],
        out_shape=[jax.ShapeDtypeStruct((L,D),BF),jax.ShapeDtypeStruct((L,D),F32),jax.ShapeDtypeStruct((L,D),BF),
            jax.ShapeDtypeStruct((n,s,D),BF),jax.ShapeDtypeStruct((n,nc,s,D),BF),jax.ShapeDtypeStruct((n,nc,s,D),BF),
            jax.ShapeDtypeStruct((8,D),F32),jax.ShapeDtypeStruct((1,FF),F32)],
        scratch_shapes=[pltpu.VMEM((L,D),BF)]*4+[pltpu.VMEM((L,FF),BF)]*2+[pltpu.VMEM((bi,D),F32)],
        compiler_params=CP(),name="middle")(x,att,cot,*([g]*(2+nc)),vec,b_inner)

def pulled(ds,ws):
    out=None
    for g in range(len(ws)//3):
        for j,d in enumerate(ds):
            t=dot(d[:,g*GL:(g+1)*GL],whole(ws[3*g+j]),NT)
            out=t if out is None else out+t
    return out

def last_kernel(nb,bi,x_ref,dq_ref,dk_ref,dv_ref,dz_ref,em_ref,dr_ref,*rest):
    ws=rest[:-6]
    gi_ref,dwq_ref,dwk_ref,dwv_ref,dwp_ref,dbv_ref=rest[-6:]
    t=pl.program_id(0)
    @pl.when(t<nb)
    def _():
        rows=pl.ds(pl.multiple_of(t*bi,bi),bi)
        gi_ref[...]=dz_ref[...]+pulled([r[rows,:] for r in (dq_ref,dk_ref,dv_ref)],ws)
    @pl.when(t==nb)
    def _(): dwq_ref[...]=dot(x_ref[...],dq_ref[...],TN).astype(BF)
    @pl.when(t==nb+1)
    def _(): dwk_ref[...]=dot(x_ref[...],dk_ref[...],TN).astype(BF)
    @pl.when(t==nb+2)
    def _():
        dwv_ref[...]=dot(x_ref[...],dv_ref[...],TN).astype(BF)
        dbv_ref[...]=rowsum(dv_ref[...].astype(F32))
    @pl.when(t==nb+3)
    def _(): dwp_ref[...]=dot(em_ref[...],dr_ref[...],TN).astype(BF)

def last(x,dq,dk,dv,dz1,em,dr,gs,bi=256):
    L,D=x.shape; nb=L//bi; n,_,s,_=gs[0].shape
    w=[pl.BlockSpec((n,1,s,GL),lambda t,j=j:(0,j,0,0),pipeline_mode=ONE) for _ in gs for j in range(3)]
    row=pl.BlockSpec((bi,D),lambda t:(jnp.minimum(t,nb-1),0))
    full=lambda sh: pl.BlockSpec(sh,lambda t:(0,0),pipeline_mode=ONE)
    o=pl.BlockSpec((D,D),lambda t:(0,0))
    W=jax.ShapeDtypeStruct((D,D),BF)
    return pl.pallas_call(functools.partial(last_kernel,nb,bi),grid=(nb+4,),
        in_specs=[full((L,D))]*4+[row,full((2*L,D)),full((2*L,D))]+w,
        out_specs=[row,o,o,o,o,pl.BlockSpec((1,D),lambda t:(0,0))],
        out_shape=[jax.ShapeDtypeStruct((L,D),F32),W,W,W,W,jax.ShapeDtypeStruct((1,D),F32)],
        compiler_params=CP(),name="last")(x,dq,dk,dv,dz1,em,dr,*[g for g in gs for _ in range(3)])

VECTORS=(5,0,1,2,3,8,9,10,14,11,12,13)

def finish_kernel(dz_ref,dq_ref,dk_ref,dv_ref,*rest):
    ws=rest[:9]
    (wu_ref,wi_ref,wo_ref,g0_ref,g1_ref,g2_ref,sv_ref,
        gi_ref,owq_ref,owk_ref,owv_ref,owp_ref,owu_ref,owi_ref,owo_ref)=rest[9:24]
    vecs=rest[24:]
    gi_ref[...]=dz_ref[...]+pulled([r[...] for r in (dq_ref,dk_ref,dv_ref)],ws)
    @pl.when(pl.program_id(0)==0)
    def _():
        for j,o in enumerate((owq_ref,owk_ref,owv_ref,owp_ref)):
            for g,r in enumerate((g0_ref,g1_ref,g2_ref)): o[:,g*GL:(g+1)*GL]=r[j]
        owu_ref[...]=wu_ref[...]; owi_ref[...]=wi_ref[...]; owo_ref[...]=wo_ref[...]
        for r,o in zip(VECTORS,vecs): o[...]=sv_ref[r:r+o.shape[0],:o.shape[1]]

def finish(dq,dk,dv,dz1,gs,wu,wi,wo,groups,sv,bi=256):
    L,D=dq.shape; nb=L//bi; n,_,s,_=gs[0].shape; fs=wu.shape[0]
    w=[pl.BlockSpec((n,1,s,GL),lambda t,j=j:(0,j,0,0),pipeline_mode=ONE) for _ in gs for j in range(3)]
    row=pl.BlockSpec((bi,D),lambda t:(t,0))
    full=lambda sh: pl.BlockSpec(sh,lambda t:(0,)*len(sh),pipeline_mode=ONE)
    outs=[(s,D)]*4+[wu.shape,wi.shape,wo.shape]+[(2,s) if r==3 else (1,fs) if r==14 else (1,s) for r in VECTORS]
    return pl.pallas_call(finish_kernel,grid=(nb,),
        in_specs=[row]*4+w+[full(wu.shape),full(wi.shape),full(wo.shape)]+[full(g_.shape) for g_ in groups]+[full(sv.shape)],
        out_specs=[row]+[full(o) for o in outs],
        out_shape=[jax.ShapeDtypeStruct((L,D),F32)]+[jax.ShapeDtypeStruct(o,F32) for o in outs],
        compiler_params=CP(),name="finish")(dz1,dq,dk,dv,*[g for g in gs for _ in range(3)],wu,wi,wo,*groups,sv)

def local(R,inputs,token_types,buckets,wq,wk,wv,bv,wp,bc,bp,bt,te,wo,bo,ga,sa,wi,b_i,wu,bu,gf,sf,cot):
    s,D=wq.shape; n=D//s; FF=wi.shape[1]; fs=FF//n; kk=FF//D
    SL=-(-max(s,fs)//128)*128
    z=jnp.zeros((s,),BF)
    wide=lambda a: jnp.pad(a,((0,0),(0,SL-a.shape[1])))
    small=jnp.concatenate([wide(jnp.stack([bc,bp,bt,te[0],te[1],bv,z,z,bo,ga,sa,bu,gf,sf])),wide(b_i[None]),jnp.zeros((1,SL),BF)])
    x=inputs[0]
    bk=jnp.pad(buckets,(0,1))[None]
    e,att,linv,q,k,v,r,g2,ga_,gb_,gc_,vec,fb,oh,xt,et=fore(R,x,wq,wk,wv,wp,wo,wi,wu,small,token_types,bk)
    g1=(ga_,gb_,gc_)
    out,dz1,datt,dwo,dwi,dwu,dvec2,dbi=middle(x,att,cot[0],g2,vec,fb)
    res=att_bwd(R,q,k,v,r,oh,vec,e,att,linv,datt,dwu,dwi,dwo,xt,et,dvec2,dbi)
    dq,dk,dv=res[:3]
    if is_square(n,R):
        wu_,wi_,wo_,*gr,sv=res[3:]
        o=finish(dq,dk,dv,dz1,g1,wu_,wi_,wo_,gr,sv)
        gin,dwq,dwk,dwv,dwp,dwu,dwi,dwo=o[:8]
        c=[a[0] for a in o[8:]]
        return (out[None],gin[None],dwq,dwk,dwv,c[0],dwp,c[1],c[2],c[3],o[12],dwo,c[5],c[6],c[7],dwi,c[8],dwu,c[9],c[10],c[11])
    dr,dvec=res[3:]
    gin,dwq,dwk,dwv,dwp,dbv=last(x,dq,dk,dv,dz1,et.T,dr,g1)
    blk=lambda a: a.reshape(n,-1,D)
    r1=jnp.concatenate([blk(dwo),blk(dwi),blk(dwu)],axis=1)
    sv=jnp.concatenate([dbv,dvec[:5],dvec2[:6]]).reshape(12,n,s).transpose(1,0,2).reshape(n,12*s)
    pad=-(12*s+fs)%D
    sv=jnp.concatenate([sv,dbi.reshape(n,fs),jnp.zeros((n,pad),F32)],axis=1).astype(BF).reshape(n,-1,D)
    r2=jnp.concatenate([blk(dwq),blk(dwk),blk(dwv),blk(dwp),sv],axis=1)
    t1=lax.psum_scatter(r1,"shard",scatter_dimension=0,tiled=False).astype(F32)
    t1=lax.psum(t1,"rep")
    t2=lax.psum_scatter(r2,"shard",scatter_dimension=0,tiled=False).astype(F32)
    t2=lax.psum(t2,"rep")
    tv=t2[4*s:].reshape(-1)
    c=lambda j: tv[j*s:(j+1)*s]
    return (out[None],gin[None],t2[:s],t2[s:2*s],t2[2*s:3*s],c(0),t2[3*s:4*s],c(1),c(2),c(3),jnp.stack([c(4),c(5)]),
        t1[:s],c(6),c(7),c(8),jnp.concatenate([t1[(1+j)*s:(2+j)*s] for j in range(kk)],axis=1),tv[12*s:12*s+fs],t1[(1+kk)*s:],c(9),c(10),c(11))

def solution(mesh):
    both=("rep","shard")
    v=P("shard"); w=P("shard",None); a3=P(both,None,None)
    in_specs=(a3,P(both,None),P(),w,w,w,v,w,v,v,v,P(None,"shard"),w,v,v,v,w,v,w,v,v,v,a3)
    out_specs=(a3,a3,w,w,w,v,w,v,v,v,P(None,"shard"),w,v,v,v,w,v,w,v,v,v)
    return jax.shard_map(functools.partial(local,mesh.shape["rep"]),mesh=mesh,in_specs=in_specs,out_specs=out_specs,check_vma=False)
```

```python
import functools, math
import jax, jax.numpy as jnp
from jax import lax
from jax.experimental import pallas as pl
from jax.experimental.pallas import tpu as pltpu
from jax.sharding import PartitionSpec as P
import numpy as np
F32=jnp.float32; BF=jnp.bfloat16
LOG2E=math.log2(math.e); LN2=math.log(2.0)
NT=(((1,),(1,)),((),())); NN=(((1,),(0,)),((),())); TN=(((0,),(0,)),((),()))
def dot(a,b,dims=NN): return lax.dot_general(a,b,dims,preferred_element_type=F32)

def shape_of(n):
    Z=4 if n%8==0 else 1
    return Z,n//(2*Z)

class Place:
    def __init__(self,n,R):
        self.n=n; self.R=R; self.rep=lax.axis_index("rep"); self.Z,self.X=shape_of(n)
        me=lax.axis_index("shard")
        self.me=me; self.c=lax.rem(me,2); q=lax.div(me,2)
        self.x=lax.rem(q,self.X); self.z=lax.div(q,self.X)
    def at(self,z,x,c): return (z*self.X+x)*2+c
    def neighbours(self):
        z,x,c=self.z,self.x,self.c
        out=[(None,self.at(z,x,1-c))]
        if self.Z>1: out+=[(z>0,self.at(z-1,x,c)),(z<self.Z-1,self.at(z+1,x,c))]
        if self.X>1: out+=[(x>0,self.at(z,x-1,c)),(x<self.X-1,self.at(z,x+1,c))]
        return out

def when(cond,fn):
    if cond is None: fn()
    else: pl.when(cond)(fn)

def both(*conds):
    out=None
    for k in conds:
        if k is not None: out=k if out is None else jnp.logical_and(out,k)
    return out

def greet(place):
    bar=pltpu.get_barrier_semaphore()
    total=jnp.int32(0)
    for ok,idx in place.neighbours():
        when(ok,lambda idx=idx: pl.semaphore_signal(bar,inc=1,device_id={"shard":idx},device_id_type=pl.DeviceIdType.MESH))
        total=total+(1 if ok is None else ok.astype(jnp.int32))
    for d in range(1,place.R):
        pl.semaphore_signal(bar,inc=1,device_id={"rep":lax.rem(place.rep+d,place.R)},device_id_type=pl.DeviceIdType.MESH)
    total=total+(place.R-1)
    pl.semaphore_wait(bar,total)

def gather_sems(n):
    Z,X=shape_of(n); A=1+2*(Z-1); J=1+2*(X-1)
    return [pltpu.SemaphoreType.DMA((max(1,2*(Z-1)),2)),pltpu.SemaphoreType.DMA((max(1,A*2*(X-1)),2)),pltpu.SemaphoreType.DMA((A*J,2))]

def gather_events(place,G,sems,t0,dz,dx,last,direct=False):
    p=place; Z,X=p.Z,p.X; zs,xs,cs=sems
    z,x,c=p.z,p.x,p.c
    def copy(idx,sem,k,to):
        return pltpu.make_async_remote_copy(src_ref=G.at[idx],dst_ref=G.at[idx],send_sem=sem.at[k,0],recv_sem=sem.at[k,1],
            device_id={"shard":to},device_id_type=pl.DeviceIdType.MESH)
    ev=[]; sends=[]
    A=1+2*(Z-1); J=1+2*(X-1)
    def slot(a):
        if a==0: return z,None
        s=(a-1)//2
        return (z-1-s,z-1-s>=0) if a%2 else (z+1+s,z+1+s<Z)
    def col(j):
        if j==0: return x,None
        k=(j-1)//2
        return (x-1-k,x-1-k>=0) if j%2 else (x+1+k,x+1+k<X)
    def zmsg(d,s):
        lev=z-s if d==0 else z+s
        ok=both(z+1<Z,z-s>=0) if d==0 else both(z>0,z+s<Z)
        return ok,copy(p.at(lev,x,c),zs,2*s+d,p.at(z+1 if d==0 else z-1,x,c))
    def zarr(d,s):
        lev,ok=slot(1+2*s+d)
        return ok,copy(p.at(lev,x,c),zs,2*s+d,p.at(z,x,1-c))
    def zfar(d,s):
        to=z+1+s if d==0 else z-1-s
        return (to<Z if d==0 else to>=0),copy(p.at(z,x,c),zs,2*s+d,p.at(to,x,c))
    def xmsg(a,d,k):
        lev,va=slot(a)
        cx=x-k if d==0 else x+k
        ok=both(va,x+1<X,x-k>=0) if d==0 else both(va,x>0,x+k<X)
        return ok,copy(p.at(lev,cx,c),xs,(a*(X-1)+k)*2+d,p.at(lev*0+z,x+1 if d==0 else x-1,c))
    def xarr(a,d,k):
        lev,va=slot(a); cx,vc=col(1+2*k+d)
        return both(va,vc),copy(p.at(lev,cx,c),xs,(a*(X-1)+k)*2+d,p.at(z,x,1-c))
    def cmsg(a,j):
        lev,va=slot(a); cx,vc=col(j)
        return both(va,vc),copy(p.at(lev,cx,c),cs,a*J+j,p.at(z,x,1-c))
    def carr(a,j):
        lev,va=slot(a); cx,vc=col(j)
        return both(va,vc),copy(p.at(lev,cx,1-c),cs,a*J+j,p.at(z,x,1-c))
    def add(t,order,fn): ev.append((min(t,last),order,fn))
    def starter(ms):
        def fn():
            for ok,m in ms: when(ok,m.start)
        return fn
    def waiter(ms):
        def fn():
            for ok,m in ms: when(ok,m.wait_recv)
        return fn
    for s in range(Z):
        t=t0+s*dz
        if s>0: add(t,(0,s,0),waiter([zarr(d,s-1) for d in range(2)]))
        if s<Z-1:
            ms=[(zfar if direct else zmsg)(d,s) for d in range(2)]; sends+=ms
            if direct: add(t0,(-0.5,s),starter(ms))
            else: add(t,(0,s,1),starter(ms))
    for a in range(A):
        ra=(a+1)//2; ta=t0+ra*dz
        for k in range(X):
            t=ta+k*dx
            if k>0: add(t,(1,k,a,0),waiter([xarr(a,d,k-1) for d in range(2)]))
            if k<X-1:
                ms=[xmsg(a,d,k) for d in range(2)]; sends+=ms
                add(t,(1,k,a,1),starter(ms))
            ms=[cmsg(a,j) for j in range(J) if (j+1)//2==k]; sends+=ms
            add(t,(1,k,a,2),starter(ms))
    add(last,(2,),waiter([carr(a,j) for a in range(A) for j in range(J)]))
    def done():
        for ok,m in sends: when(ok,m.wait_send)
    add(last,(3,),done)
    ev.sort(key=lambda e:(e[0],e[1]))
    return ev

def square_sems(n):
    Z,X=shape_of(n); A=1+2*(Z-1)
    return [pltpu.SemaphoreType.DMA((2*(Z-1),2)),pltpu.SemaphoreType.DMA((A,2)),pltpu.SemaphoreType.DMA((A,2)),pltpu.SemaphoreType.DMA((3*A,2))]

def square_events(place,G,sems,t0,dz,dx,dy,last,parts=None):
    p=place; Z=p.Z; zs,xs,ys,cs=sems
    z,x,c,rep=p.z,p.x,p.c,p.rep
    lo,parts=parts or (0,G.shape[1]); cut=(parts+1)//2
    halves=((lo,cut),(lo+cut,parts-cut))
    A=1+2*(Z-1)
    def copy(idx,part,sem,k,to):
        ref=G.at[idx,pl.ds(*((lo,parts) if part is None else halves[part]))]
        return pltpu.make_async_remote_copy(src_ref=ref,dst_ref=ref,send_sem=sem.at[k,0],recv_sem=sem.at[k,1],
            device_id=to,device_id_type=pl.DeviceIdType.MESH)
    def slot(a):
        if a==0: return z,None
        s=(a-1)//2
        return (z-1-s,z-1-s>=0) if a%2 else (z+1+s,z+1+s<Z)
    other={"shard":p.at(z,x,1-c)}; across={"shard":p.at(z,1-x,c)}; above={"rep":1-rep}
    def zmsg(d,s):
        lev=z-s if d==0 else z+s
        ok=both(z+1<Z,z-s>=0) if d==0 else both(z>0,z+s<Z)
        return ok,copy(p.at(lev,x,c),None,zs,2*s+d,{"shard":p.at(z+1 if d==0 else z-1,x,c)})
    def zarr(d,s):
        lev,ok=slot(1+2*s+d)
        return ok,copy(p.at(lev,x,c),None,zs,2*s+d,other)
    def xmsg(a,h):
        lev,va=slot(a)
        return both(va,rep==h),copy(p.at(lev,x,c),h,xs,a,across)
    def xarr(a,h):
        lev,va=slot(a)
        return both(va,rep==h),copy(p.at(lev,1-x,c),h,xs,a,across)
    def ymsg(a,h):
        lev,va=slot(a)
        return both(va,rep==h),copy(p.at(lev,1-x,c),h,ys,a,above)
    def yarr(a,h):
        lev,va=slot(a)
        return both(va,rep==1-h),copy(p.at(lev,1-x,c),h,ys,a,above)
    def cmsg(a,h,core):
        lev,va=slot(a); cc=c if core==0 else 1-c
        if h is None: return [(va,copy(p.at(lev,x,cc),None,cs,3*a,other))]
        return [(both(va,rep==(g if h==0 else 1-g)),copy(p.at(lev,1-x,cc),g,cs,3*a+1+h,other)) for g in range(2)]
    ev=[]; sends=[]
    def add(t,order,fn): ev.append((min(t,last),order,fn))
    def start(t,order,ms):
        sends.extend(ms)
        def fn():
            for ok,m in ms: when(ok,m.start)
        add(t,order,fn)
    def await_(t,order,ms):
        def fn():
            for ok,m in ms: when(ok,m.wait_recv)
        add(t,order,fn)
    for s in range(Z):
        t=t0+(dz[s] if isinstance(dz,tuple) else s*dz)
        if s>0: await_(t,(0,s,0),[zarr(d,s-1) for d in range(2)])
        if s<Z-1: start(t,(0,s,1),[zmsg(d,s) for d in range(2)])
        for a in ([0] if s==0 else [2*s-1,2*s]):
            start(t,(1,s,a),[xmsg(a,h) for h in range(2)]+cmsg(a,None,0))
            await_(t+dx,(2,s,a,0),[xarr(a,h) for h in range(2)])
            start(t+dx,(2,s,a,1),[ymsg(a,h) for h in range(2)]+cmsg(a,0,0))
            await_(t+dx+dy,(3,s,a,0),[yarr(a,h) for h in range(2)])
            start(t+dx+dy,(3,s,a,1),cmsg(a,1,0))
    await_(last,(4,),[m for a in range(A) for h in (None,0,1) for m in cmsg(a,h,1)])
    def done():
        for ok,m in sends: when(ok,m.wait_send)
    add(last,(5,),done)
    ev.sort(key=lambda e:(e[0],e[1]))
    return ev

def is_square(n,R): return R==2 and shape_of(n)==(4,2)
def spread_sems(n,R): return square_sems(n) if is_square(n,R) else gather_sems(n)
def spread_events(place,G,sems,t0,dz,dx,dy,last,parts=None):
    if is_square(place.n,place.R): return square_events(place,G,sems,t0,dz,dx,dy,last,parts)
    return gather_events(place,G,sems,t0,dz,dx,last)

def run_events(step,events,after=False):
    picked=[e for e in events if (e[0]-int(e[0])>=0.5)==after]
    for t in sorted({int(e[0]) for e in picked}):
        fns=[e[2] for e in picked if int(e[0])==t]
        def fire(fns=fns):
            for f in fns: f()
        pl.when(step==t)(fire)

def sum_scratch(n,Q,s,D,parts):
    Z,X=shape_of(n); dma=pltpu.SemaphoreType.DMA
    V=lambda *sh: pltpu.VMEM(sh,BF)
    return [V(Z,X,Q,s,D),V(Z,X,Q,s,D),V(Z,Q,s,D//2),V(Z,Q,s,D//2),V(2,Z-1,Q,s,D),V(Q,s,D),
        dma((parts,)),dma((parts,2)),dma((Z,2)),dma((Z,2)),dma((2*(Z-1),2)),dma((1,2))]
SUM_REFS=12

def sum_events(place,srcs,refs,times,store):
    p=place; Z=p.Z
    z,x,c,rep=p.z,p.x,p.c,p.rep
    S,B,YB,XB,ZB,FB,ls,cs,ys,xs,zs,fs=refs
    Q=S.shape[2]; H=S.shape[4]//2
    tc,ta,ty,tx,tz,tend=times
    half=lambda r: pl.ds(pl.multiple_of(r*H,128),H)
    other={"shard":p.at(z,x,1-c)}; across={"shard":p.at(z,1-x,c)}; above={"rep":1-rep}
    def rc(src,dst,sem,k,to):
        return pltpu.make_async_remote_copy(src_ref=src,dst_ref=dst,send_sem=sem.at[k,0],recv_sem=sem.at[k,1],device_id=to,device_id_type=pl.DeviceIdType.MESH)
    ev=[]; sends=[]
    def add(t,order,fn): ev.append((t,order,fn))
    def start(t,order,ms):
        sends.extend(ms)
        def fn():
            for ok,m in ms: when(ok,m.start)
        add(t,order,fn)
    loads=[pltpu.make_async_copy(r.at[:,:,c],S.at[:,:,pl.ds(q,k)],ls.at[j]) for j,(r,q,k) in enumerate(srcs)]
    cores=[(None,rc(r.at[:,:,1-c],B.at[:,:,pl.ds(q,k)],cs,j,other)) for j,(r,q,k) in enumerate(srcs)]
    def plus(a,b): return (a.astype(F32)+b.astype(F32)).astype(BF)
    def begin():
        for m in loads: m.start()
    add(tc,(0,),begin)
    start(tc,(1,),cores)
    def merge():
        for m in loads: m.wait()
        for _,m in cores: m.wait_recv()
        def body(k,_):
            lev=lax.div(k,2*Q); r=lax.rem(k,2*Q); xx=lax.div(r,Q); q=lax.rem(r,Q)
            S[lev,xx,q]=plus(S[lev,xx,q],B[lev,xx,q])
            return 0
        lax.fori_loop(0,2*Z*Q,body,0)
    add(ta,(2,),merge)
    def levels(d): return [(z,None)] if d==0 else [(z-d,z-d>=0),(z+d,z+d<Z)]
    for i,d in enumerate(range(Z-1,-1,-1)):
        L=levels(d)
        ysend=[(ok,rc(S.at[l,1-x,:,:,half(1-rep)],YB.at[l],ys,l,above)) for l,ok in L]
        xsend=[(ok,rc(S.at[l,1-x,:,:,half(rep)],XB.at[l],xs,l,across)) for l,ok in L]
        start(ty[i],(3,i),ysend)
        def ytake(L=L,ysend=ysend):
            for (l,ok),(_,m) in zip(L,ysend):
                def go(l=l,m=m):
                    m.wait_recv()
                    def body(q,_):
                        S[l,1-x,q,:,half(rep)]=plus(S[l,1-x,q,:,half(rep)],YB[l,q])
                        return 0
                    lax.fori_loop(0,Q,body,0)
                when(ok,go)
        add(tx[i],(4,i,0),ytake)
        start(tx[i],(4,i,1),xsend)
        def xtake(L=L,xsend=xsend):
            for (l,ok),(_,m) in zip(L,xsend):
                def go(l=l,m=m):
                    m.wait_recv()
                    def body(q,_):
                        S[l,x,q,:,half(rep)]=plus(S[l,x,q,:,half(rep)],XB[l,q])
                        return 0
                    lax.fori_loop(0,Q,body,0)
                when(ok,go)
        add(tz[i],(5,i,0),xtake)
        if d<=Z-2:
            def ztake(d=d):
                for dr,(l,ok) in enumerate([(z-d,both(z+1<Z,z-d>=0)),(z+d,both(z>0,z+d<Z))]):
                    def go(dr=dr,l=l):
                        rc(ZB.at[dr,d],ZB.at[dr,d],zs,2*d+dr,other).wait_recv()
                        def body(q,_):
                            S[l,x,q]=plus(S[l,x,q],ZB[dr,d,q])
                            return 0
                        lax.fori_loop(0,Q,body,0)
                    pl.when(ok)(go)
            add(tz[i],(5,i,1),ztake)
        if d>=1:
            start(tz[i],(5,i,2),[(z-d>=0,rc(S.at[z-d,x],ZB.at[0,d-1],zs,2*(d-1),{"shard":p.at(z-1,x,c)})),
                (z+d<Z,rc(S.at[z+d,x],ZB.at[1,d-1],zs,2*(d-1)+1,{"shard":p.at(z+1,x,c)}))])
    final=[(None,rc(S.at[z,x],FB,fs,0,above))]
    start(tz[-1],(6,),final)
    def finish():
        final[0][1].wait_recv()
        for q in range(Q): store(q,S[z,x,q].astype(F32)+FB[q].astype(F32))
    add(tend,(7,),finish)
    def done():
        for ok,m in sends: when(ok,m.wait_send)
    add(tend,(8,),done)
    return ev

def greet_all(place):
    bar=pltpu.get_barrier_semaphore()
    n,R=place.n,place.R
    def hello(d,_):
        pl.semaphore_signal(bar,inc=1,device_id={"shard":lax.rem(place.me+d,n)},device_id_type=pl.DeviceIdType.MESH)
        return 0
    lax.fori_loop(1,n,hello,0)
    for d in range(1,R):
        pl.semaphore_signal(bar,inc=1,device_id={"rep":lax.rem(place.rep+d,R)},device_id_type=pl.DeviceIdType.MESH)
    return lambda: pl.semaphore_wait(bar,n+R-2)

STRIDE=32
def tables(length,width):
    half=width//2; count=2*length//STRIDE
    rates=np.exp(np.arange(half)*(-2.0*math.log(10000.0)/width))
    def pack(angles):
        full=np.concatenate([np.sin(angles),np.cos(angles)],axis=1).astype(np.float32)
        hi=full.astype(jnp.bfloat16); lo=(full-hi.astype(np.float32)).astype(jnp.bfloat16)
        return np.concatenate([hi,lo],axis=0)
    coarse=(np.arange(count)*STRIDE-length)[:,None]*rates[None]
    fine=np.arange(STRIDE)[:,None]*rates[None]
    return pack(coarse),pack(fine)

BI=256
ONE=pl.Buffered(1)


def lane_half(rows, lanes):
    lane=lax.broadcasted_iota(jnp.int32,(rows,lanes),1)
    return (lane//64)%2

def split_hi_lo(v):
    hi=v.astype(BF); return hi,(v-hi.astype(F32)).astype(BF)

def queries(q, vec, oh):
    s=0.125*LOG2E
    cq=((q+vec[0:1])*s).astype(BF)
    pq=((q+vec[1:2])*s).astype(BF)
    tq=(q+vec[2:3])*0.125
    return cq,pq,tq

GL=256

def fore_kernel(n,R,x_ref,wq_ref,wk_ref,wv_ref,wp_ref,wo_ref,wi_ref,wu_ref,small_ref,kinds_ref,buckets_ref,ta_ref,tb_ref,
        e_ref,att_ref,linv_ref,q_ref,k_ref,v_ref,r_ref,g_ref,w0_ref,w1_ref,w2_ref,vec_ref,bi_ref,oh_ref,xt_ref,et_ref,
        em,wg,all_s,mine,own,own2,ssem,*sems):
    bi=att_ref.shape[0]; L=x_ref.shape[0]; W=L+bi
    pair=pl.program_id(0); i=pl.program_id(1); nb=L//bi
    step=pair*nb+i; steps=6*nb
    place=Place(n,R); me=place.me
    kk=wu_ref.shape[0]; D=wo_ref.shape[1]
    groups=D//GL; per=len(spread_sems(n,R)); square=is_square(n,R); gs=len(gather_sems(n))
    ws=(wq_ref,wk_ref,wv_ref,wp_ref)
    loads=[[pltpu.make_async_copy(w.at[:,pl.ds(g*GL,GL)],wg.at[g,me,j],own2.at[g,j]) for j,w in enumerate(ws)] for g in range(groups)]
    keeps=[pltpu.make_async_copy(wg.at[g],o,own2.at[g,4]) for g,o in enumerate((w0_ref,w1_ref,w2_ref))]
    owns=[pltpu.make_async_copy(wu_ref,mine.at[pl.ds(0,kk)],own.at[0]),pltpu.make_async_copy(wo_ref,mine.at[kk],own.at[1])]
    owns+=[pltpu.make_async_copy(wi_ref.at[:,pl.ds(j*D,D)],mine.at[kk+1+j],own.at[2+j]) for j in range(kk)]
    keep=pltpu.make_async_copy(mine,g_ref.at[me],own.at[2+kk])
    def send(d):
        return pltpu.make_async_remote_copy(src_ref=all_s.at[me],dst_ref=all_s.at[me],send_sem=ssem.at[d,0],recv_sem=ssem.at[d,1],
            device_id={"shard":lax.rem(me+d,n)},device_id_type=pl.DeviceIdType.MESH)
    def arrive(d):
        w=lax.rem(me-d+n,n)
        return pltpu.make_async_remote_copy(src_ref=all_s.at[w],dst_ref=all_s.at[w],send_sem=ssem.at[d,0],recv_sem=ssem.at[d,1],
            device_id={"shard":lax.rem(me+d,n)},device_id_type=pl.DeviceIdType.MESH)
    def enter():
        for g in range(groups):
            for m in loads[g]: m.start()
        for m in owns: m.start()
        met=greet_all(place)
        all_s[me]=small_ref[...]
        for g in range(groups):
            for m in loads[g]: m.wait()
        met()
    def share():
        def go(d,_):
            send(d).start()
            return 0
        lax.fori_loop(1,n,go,0)
    def enter2():
        for m in owns: m.wait()
        keep.start()
    def prepare():
        L2=buckets_ref.shape[1]
        count=L2//STRIDE
        def body(j,_):
            rows=pl.ds(pl.multiple_of(j*256,256),256)
            b=buckets_ref[:,rows]
            hot=lambda v,m: jnp.where(v==lax.rem(lax.broadcasted_iota(jnp.int32,(2*m,256),0),m),1.0,0.0).astype(BF)
            A=dot(hot(lax.div(b,STRIDE),count),ta_ref[...],TN)
            B=dot(hot(lax.rem(b,STRIDE),STRIDE),tb_ref[...],TN)
            h=A.shape[1]//2
            sa,ca,sb,cb=A[:,:h],A[:,h:],B[:,:h],B[:,h:]
            both_=jnp.concatenate([sa*cb+ca*sb,ca*cb-sa*sb],axis=1)
            em[rows,:]=both_.astype(BF)
            et_ref[:,rows]=both_.T.astype(BF)
            return 0
        lax.fori_loop(0,L2//256,body,0)
        def turn(j,_):
            rows=pl.ds(pl.multiple_of(j*256,256),256)
            xt_ref[:,rows]=x_ref[rows,:].astype(F32).T.astype(BF)
            return 0
        lax.fori_loop(0,L//256,turn,0)
        for j in range(L//256):
            kinds=kinds_ref[:,j*256:(j+1)*256]
            lane=lax.rem(lax.broadcasted_iota(jnp.int32,(128,256),0),64)
            hot=jnp.where((lax.rem(lane,3)==kinds)&(lane<6),1.0,0.0)
            oh_ref[j*256:(j+1)*256,:]=hot.T.astype(BF)
    def unpack():
        def come(d,_):
            arrive(d).wait_recv()
            send(d).wait_send()
            return 0
        lax.fori_loop(1,n,come,0)
        s=wq_ref.shape[0]; fs=bi_ref.shape[1]//n
        for w in range(n):
            a=all_s[w].astype(F32)
            vec_ref[:,w*s:(w+1)*s]=a[:,:s]
            bi_ref[:,w*fs:(w+1)*fs]=a[14:15,:fs]
    def project(g):
        col=lambda j: wg[g,:,j].reshape(D,GL)
        def rows_of(j,_):
            rows=pl.ds(pl.multiple_of(j*256,256),256)
            x=x_ref[rows,:]
            q_ref[rows,:]=dot(x,col(0))
            k_ref[rows,:]=dot(x,col(1)).astype(BF)
            v_ref[rows,:]=(dot(x,col(2))+vec_ref[5:6,g*GL:(g+1)*GL]).astype(BF)
            rows2=pl.ds(pl.multiple_of(j*512,512),512)
            r_ref[rows2,:]=dot(em[rows2,:],col(3)).astype(BF)
            return 0
        lax.fori_loop(0,L//256,rows_of,0)
    ev=[(0,(-2,),enter),(0,(1.5,),share),(0.001,(9,),prepare),(0.1,(9,),unpack),(1,(-1,),enter2),(2,(-1,),keep.wait)]
    for g,(t0,dz,dx,dy,end) in enumerate(FORE_TIMES):
        if g==0: ev+=gather_events(place,wg.at[g],sems[:gs],t0,dz,dx,end,square)
        else: ev+=spread_events(place,wg.at[g],sems[gs+(g-1)*per:gs+g*per],t0,dz,dx,dy,end)
        ev.append((end,(9,),keeps[g].start))
        ev.append((end,(10,),functools.partial(project,g)))
        ev.append((steps-0.5,(9,g),keeps[g].wait))
    rest=sems[gs+(groups-1)*per:]
    if square:
        for k,(lo,cnt) in enumerate(((0,kk),(kk,kk+1))):
            ev+=square_events(place,g_ref,rest[k*per:(k+1)*per],*FORE_REST[k],steps-0.5,(lo,cnt))
    else: ev+=spread_events(place,g_ref,rest[:per],2,6,4,4,steps-0.5)
    ev.sort(key=lambda e:(e[0],e[1]))
    run_events(step,ev)
    side=pl.ds(pl.multiple_of(lax.rem(pair,2)*128,128),128)
    vec=vec_ref[0:8,pl.ds(pl.multiple_of(pair*128,128),128)]
    rows=pl.ds(pl.multiple_of(i*bi,bi),bi)
    q=q_ref[rows,side]
    oh_i=oh_ref[rows,:]
    cq,pq,tq=queries(q,vec,None)
    rr=lax.broadcasted_iota(jnp.int32,(256,128),0)%128
    cc=lax.broadcasted_iota(jnp.int32,(256,128),1)
    M=jnp.where((rr//64==cc//64)&(cc%64<6),1.0,0.0).astype(BF)
    def tt(te):
        hi,lo=split_hi_lo(tq*(te*LOG2E))
        return dot(jnp.concatenate([hi,lo],axis=1),M)
    t0=tt(vec[3:4]); t1=tt(vec[4:5])
    tv=jnp.where(oh_i>0,t1,t0)
    hi=tv.astype(BF).astype(F32)
    lane=lax.broadcasted_iota(jnp.int32,(bi,128),1)
    tv=jnp.where(lane%64<3,hi,tv-hi).astype(BF)
    half=lane_half(bi,128)
    kext=jnp.concatenate([k_ref[:,side],oh_ref[...]],axis=1)
    vext=jnp.concatenate([v_ref[:,side],jnp.ones((L,128),BF)],axis=1)
    w0=pl.multiple_of(L-bi-i*bi,bi)
    rwin=r_ref[pl.ds(w0,W),side]
    z=jnp.zeros((),BF)
    outs=[]
    for h in range(2):
        qx=jnp.concatenate([jnp.where(half==h,cq,z),jnp.where(half==h,tv,z)],axis=1)
        pos=dot(jnp.where(half==h,pq,z),rwin,NT)
        pos=pltpu.roll(pos,W-(bi-1),1,stride=1,stride_axis=0)[:,:L]
        s=dot(qx,kext,NT)+pos
        m=jnp.max(s,axis=1,keepdims=True)
        e=jnp.exp2(s-m).astype(BF)
        e_ref[h]=e
        o=dot(e,vext)
        li=1.0/o[:,128:]
        outs.append((o[:,:128]*li,li))
    att_ref[...]=jnp.where(half==0,outs[0][0],outs[1][0]).astype(BF)
    linv_ref[...]=jnp.where(half==0,outs[0][1],outs[1][1])
    run_events(step,ev,after=True)

FORE_TIMES=((0.0,0.01,0.01,0.01,0.1),(0.2,1,1,1,8.0),(1.2,1,1,1,16.0))
FORE_REST=((4,(0,3,8,13),2,3),(4.01,(0,6,11,16),2,2))

def fore(R,x,wq,wk,wv,wp,wo,wi,wu,small,kinds,buckets,bi=BI):
    L,D=x.shape; P=D//128; nb=L//bi; s=wo.shape[0]; n=D//s; kk=wu.shape[0]//s; FF=wi.shape[1]; SL=small.shape[1]
    ta,tb=tables(L,D)
    hbm=pl.BlockSpec(memory_space=pl.ANY)
    full=lambda a: pl.BlockSpec(a.shape,lambda p,i:(0,)*len(a.shape),pipeline_mode=ONE)
    S=jax.ShapeDtypeStruct
    tile=pl.BlockSpec((bi,128),lambda p,i:(i,p))
    col=lambda k: pl.BlockSpec((k*L,GL),lambda p,i:(0,p//2))
    ta,tb=jnp.asarray(ta),jnp.asarray(tb)
    tails=[S((16,D),F32),S((1,FF),F32),S((L,128),BF),S((D,L),BF),S((D,2*L),BF)]
    dma=pltpu.SemaphoreType.DMA
    return pl.pallas_call(functools.partial(fore_kernel,n,R),grid=(P,nb),
        in_specs=[full(x)]+[hbm]*7+[full(a) for a in (small,kinds,buckets,ta,tb)],
        out_specs=[pl.BlockSpec((2,bi,L),lambda p,i:(p,i,0)),tile,tile,col(1),col(1),col(1),col(2)]+[hbm]*4+[full(t) for t in tails],
        out_shape=[S((2*P,L,L),BF),S((L,D),BF),S((L,D),F32),S((L,D),F32),S((L,D),BF),S((L,D),BF),S((2*L,D),BF),S((n,2*kk+1,s,D),BF)]
            +[S((n,4,s,GL),BF)]*3+tails,
        scratch_shapes=[pltpu.VMEM((2*L,D),BF),pltpu.VMEM((D//GL,n,4,s,GL),BF),pltpu.VMEM((n,16,SL),BF),pltpu.VMEM((2*kk+1,s,D),BF),
            dma((3+kk,)),dma((D//GL,5)),dma((n,2))]+gather_sems(n)+spread_sems(n,R)*(D//GL+1),
        compiler_params=pltpu.CompilerParams(vmem_limit_bytes=60*2**20,dimension_semantics=("arbitrary","arbitrary"),collective_id=1,has_side_effects=True),
        name="fore")(x,wq,wk,wv,wp,wo,wi,wu.reshape(kk,s,D),small,kinds,buckets,ta,tb)

TIMES_A=(0,2,(2,3,4,6),(4,5,7,8),(6,9,12,15),18)
TIMES_B=(1,4,(5,6,8,10),(7,8,11,12),(11,15,18,21),23)
TIMES_G=((8,10,(10,10,11,11),(13,13,14,14),(16,18,20,22),23),
    (16,18,(18,18,19,19),(21,21,22,22),(23,23.5,23.5,23.5),23.5),
    (23.5,23.5,(23.5,)*4,(23.5,)*4,(23.5,)*4,23.5))

def bwd_kernel(n,R,roll_bf,q_ref,k_ref,v_ref,r_ref,oh_ref,vec_ref,e_ref,att_ref,linv_ref,datt_ref,*rest):
    bi=q_ref.shape[0]; L=k_ref.shape[0]; W=L+bi
    pair=pl.program_id(0); i=pl.program_id(1); nb=L//bi; step=pair*nb+i
    square=is_square(n,R)
    if square:
        gu_ref,gi_ref,go_ref,xt_ref,et_ref,vb_ref,vi_ref=rest[:7]
        dq_ref,dk_ref,dv_ref,wu_ref,wi_ref,wo_ref,g0_ref,g1_ref,g2_ref,sv_ref=rest[7:17]
        dk_acc,dv_acc,dr_acc,dvec_ref,dq2,dk2,dv2,dr2,vec_s,src0,src1,src2=rest[17:29]
        refs=rest[29:]
        s,D=wo_ref.shape; kk=wu_ref.shape[0]//s
        def store_a(q,v): wu_ref[q*s:(q+1)*s,:]=v
        def store_b(q,v):
            if q<kk: wi_ref[:,q*D:(q+1)*D]=v
            else: wo_ref[...]=v
        place=Place(n,R); Z,X=place.Z,place.X; me=place.me
        ev=[(0,(-1,),lambda: greet(place))]
        ev+=sum_events(place,[(gu_ref,0,kk)],refs[:SUM_REFS],TIMES_A,store_a)
        ev+=sum_events(place,[(gi_ref,0,kk),(go_ref,kk,1)],refs[SUM_REFS:2*SUM_REFS],TIMES_B,store_b)
        for g,(src,out) in enumerate(((src0,g0_ref),(src1,g1_ref),(src2,g2_ref))):
            def store_g(q,v,out=out):
                if q<4: out[q]=v
                else: sv_ref[...]=v[:16,:]
            ev+=sum_events(place,[(src,0,src.shape[3])],refs[(2+g)*SUM_REFS:(3+g)*SUM_REFS],TIMES_G[g],store_g)
            def weights(src=src):
                for j,(l,r) in enumerate(((xt_ref,dq2),(xt_ref,dk2),(xt_ref,dv2),(et_ref,dr2))):
                    src[:,:,:,j]=dot(l[...],r[...]).astype(BF).reshape(Z,X,2,s,GL)
            ev.append(((2*g+2)*nb-0.5,(-1,),weights))
        def vectors():
            fs=vi_ref.shape[1]//n
            rows=jnp.concatenate([vec_s[...],vb_ref[...]],axis=0)
            row=lax.broadcasted_iota(jnp.int32,(16,GL),0)
            wide=lambda a: jnp.concatenate([a,jnp.zeros((a.shape[0],GL-a.shape[1]),F32)],axis=1)
            for w in range(n):
                v=jnp.where(row==14,wide(vi_ref[:,w*fs:(w+1)*fs]),wide(rows[:,w*s:(w+1)*s]))
                src2[w//(2*X),w//2%X,w%2,4]=jnp.concatenate([v,jnp.zeros((s-16,GL),F32)],axis=0).astype(BF)
        ev.append((6*nb-0.5,(-1.5,),vectors))
        ev.sort(key=lambda e:(e[0],e[1]))
        run_events(step,ev)
    else:
        dq_ref,dk_ref,dv_ref,dr_ref,dvec_ref,dk_acc,dv_acc,dr_acc=rest
    vec=vec_ref[...]
    q=q_ref[...]
    oh_i=oh_ref[pl.ds(pl.multiple_of(i*bi,bi),bi),:].astype(F32)
    cq,pq,tq=queries(q,vec,None)
    half=lane_half(bi,128)
    lane=lax.broadcasted_iota(jnp.int32,(bi,128),1)
    @pl.when(i==0)
    def _():
        dk_acc[...]=jnp.zeros_like(dk_acc); dv_acc[...]=jnp.zeros_like(dv_acc); dr_acc[...]=jnp.zeros_like(dr_acc)
        dvec_ref[...]=jnp.zeros_like(dvec_ref)
    P=jnp.where(lax.broadcasted_iota(jnp.int32,(bi,bi),0)+lax.broadcasted_iota(jnp.int32,(bi,bi),1)==bi-1,1.0,0.0).astype(BF)
    pqr=dot(P,pq).astype(BF)
    kext=jnp.concatenate([k_ref[...],oh_ref[...]],axis=1)
    ones2=jnp.where(lax.broadcasted_iota(jnp.int32,(L,128),1)<2,1.0,0.0).astype(BF)
    vext=jnp.concatenate([v_ref[...],ones2],axis=1)
    w0=pl.multiple_of(L-bi-i*bi,bi)
    rwin=r_ref[pl.ds(w0,W),:]
    z=jnp.zeros((),BF)
    dattl=datt_ref[...].astype(F32)*linv_ref[...]
    prod=dattl*att_ref[...].astype(F32)
    dattl=dattl.astype(BF)
    dcs=[];dps=[];dts=[];tes=[]
    dk=None; dv=None; dr=None
    for h in range(2):
        delta=-jnp.sum(jnp.where(half==h,prod,0.0),axis=1,keepdims=True)
        dhi=delta.astype(BF).astype(F32)
        dx=jnp.where(lane==0,dhi,jnp.where(lane==1,delta-dhi,0.0)).astype(BF)
        dm=jnp.where(half==h,dattl,z)
        dpd=dot(jnp.concatenate([dm,dx],axis=1),vext,NT)
        e=e_ref[h]
        ds=(e.astype(F32)*dpd).astype(BF)
        dvh=dot(e,dm,TN)
        dkh=dot(ds,jnp.where(half==h,cq,z),TN)
        dc=dot(ds,kext)
        rev=dot(P,ds)
        if roll_bf: rev=rev.astype(BF)
        rev=jnp.concatenate([rev,jnp.zeros((bi,W-L),rev.dtype)],axis=1)
        dpr=pltpu.roll(rev,0,1,stride=1,stride_axis=0).astype(BF)
        dp=dot(dpr,rwin)
        drh=dot(dpr,jnp.where(half==h,pqr,z),TN)
        dv=dvh if dv is None else dv+dvh
        dk=dkh if dk is None else dk+dkh
        dr=drh if dr is None else dr+drh
        D=jnp.where(lane<3,dc[:,128:],0.0)
        dall=jnp.sum(D,axis=1,keepdims=True)
        d1=jnp.sum(D*oh_i,axis=1,keepdims=True)
        d0=dall-d1
        dcs.append(dc[:,:128]); dps.append(dp)
        dts.append(d0*vec[3:4]+d1*vec[4:5])
        tes.append((d0,d1))
    dv_acc[...]+=dv
    dk_acc[...]+=dk
    dr_acc[pl.ds(w0,W),:]+=dr
    dcq=jnp.where(half==0,dcs[0],dcs[1]).astype(BF).astype(F32)
    dpr=jnp.where(half==0,dps[0],dps[1]).astype(BF)
    dpq=dot(P,dpr)
    dtq=jnp.where(half==0,dts[0],dts[1])
    dq=((dcq+dpq+dtq)*0.125).astype(BF)
    dq_ref[...]=dq
    d0=jnp.where(half==0,tes[0][0],tes[1][0]); d1=jnp.where(half==0,tes[0][1],tes[1][1])
    rows=[dcq*0.125,dpq*0.125,dtq*0.125,d0*tq,d1*tq]
    sums=[jnp.sum(v,axis=0,keepdims=True) for v in rows]+[jnp.zeros((3,128),F32)]
    dvec_ref[...]+=jnp.concatenate(sums,axis=0)
    @pl.when(i==nb-1)
    def _():
        dk=(dk_acc[...]*LN2).astype(BF); dv=dv_acc[...].astype(BF); dr=(dr_acc[...]*LN2).astype(BF)
        dk_ref[...]=dk
        dv_ref[...]=dv
        if square:
            side=pl.ds(pl.multiple_of(lax.rem(pair,2)*128,128),128)
            dk2[:,side]=dk; dv2[:,side]=dv; dr2[:,side]=dr
            cols=pl.ds(pl.multiple_of(pair*128,128),128)
            vec_s[0:5,cols]=dvec_ref[0:5,:]
            vec_s[5:6,cols]=rowsum(dv.astype(F32))
            vec_s[6:8,cols]=jnp.zeros((2,128),F32)
        else: dr_ref[...]=dr
    if square:
        dq2[pl.ds(pl.multiple_of(i*bi,bi),bi),pl.ds(pl.multiple_of(lax.rem(pair,2)*128,128),128)]=dq
        run_events(step,ev,after=True)

def att_bwd(R,q,k,v,r,oh,vec,e,att,linv,datt,dwu,dwi,dwo,xt,et,vb,vi,bi=BI,roll_bf=False):
    L,D=q.shape; P=D//128; nb=L//bi; n,kk,s,_=dwu.shape
    col=pl.BlockSpec((L,128),lambda p,i:(0,p)); tile=pl.BlockSpec((bi,128),lambda p,i:(i,p))
    full=lambda sh: pl.BlockSpec(sh,lambda p,i:(0,)*len(sh),pipeline_mode=ONE)
    in_specs=[tile,col,col,pl.BlockSpec((2*L,128),lambda p,i:(0,p)),pl.BlockSpec((L,128),lambda p,i:(0,0)),
        pl.BlockSpec((8,128),lambda p,i:(0,p)),pl.BlockSpec((2,bi,L),lambda p,i:(p,i,0)),tile,tile,tile]
    out_specs=[tile,col,col]
    out_shape=[jax.ShapeDtypeStruct((L,D),BF)]*3
    scratch=[pltpu.VMEM((L,128),F32),pltpu.VMEM((L,128),F32),pltpu.VMEM((2*L,128),F32)]
    args=[q,k,v,r,oh,vec,e,att,linv,datt]
    params=dict(vmem_limit_bytes=62*2**20,dimension_semantics=("arbitrary","arbitrary"))
    if is_square(n,R):
        Z,X=shape_of(n); FF=vi.shape[1]; SL=-(-max(s,FF//n)//128)*128
        in_specs+=[pl.BlockSpec(memory_space=pl.ANY)]*3+[full((D,L)),full((D,2*L)),full((8,D)),full((1,FF))]
        for sh in ((kk*s,D),(s,kk*D),(s,D),(4,s,GL),(4,s,GL),(4,s,GL),(16,GL)):
            out_specs.append(full(sh)); out_shape.append(jax.ShapeDtypeStruct(sh,F32))
        scratch+=[pltpu.VMEM((8,128),F32)]+[pltpu.VMEM((L,GL),BF)]*3+[pltpu.VMEM((2*L,GL),BF),pltpu.VMEM((8,D),F32)]
        scratch+=[pltpu.VMEM((Z,X,2,q,s,GL),BF) for q in (4,4,5)]
        scratch+=sum_scratch(n,kk,s,D,1)+sum_scratch(n,kk+1,s,D,2)+sum_scratch(n,4,s,GL,1)*2+sum_scratch(n,5,s,GL,1)
        args+=[dwu.reshape(Z,X,2,kk,s,D),dwi.reshape(Z,X,2,kk,s,D),dwo.reshape(Z,X,2,1,s,D),xt,et,vb,vi]
        params.update(collective_id=2,has_side_effects=True)
    else:
        out_specs+=[pl.BlockSpec((2*L,128),lambda p,i:(0,p)),pl.BlockSpec((8,128),lambda p,i:(0,p))]
        out_shape+=[jax.ShapeDtypeStruct((2*L,D),BF),jax.ShapeDtypeStruct((8,D),F32)]
    return pl.pallas_call(functools.partial(bwd_kernel,n,R,roll_bf),grid=(P,nb),in_specs=in_specs,out_specs=out_specs,out_shape=out_shape,
        scratch_shapes=scratch,compiler_params=pltpu.CompilerParams(**params),
        name="attend_back")(*args)

CP=lambda **k: pltpu.CompilerParams(vmem_limit_bytes=60*2**20,**k)
C0=math.sqrt(2.0/math.pi); C1=0.044715
EPS=1e-6

def whole(ref):
    a=ref[...]
    return a.reshape(-1,a.shape[-1])

def ln_stats(z):
    n=z.shape[1]
    mu=jnp.sum(z,axis=1,keepdims=True)*(1.0/n)
    c=z-mu
    var=jnp.sum(c*c,axis=1,keepdims=True)*(1.0/n)
    r=lax.rsqrt(var+EPS)
    return c*r,r

def ln_back(g,zhat,r):
    n=g.shape[1]
    a=jnp.sum(g,axis=1,keepdims=True)*(1.0/n)
    b=jnp.sum(g*zhat,axis=1,keepdims=True)*(1.0/n)
    return r*(g-a-zhat*b)

def rowsum(v): return jnp.sum(v,axis=0,keepdims=True)

def mid_kernel(nb,bi,nc,x_ref,att_ref,cot_ref,wo_ref,wu_ref,*rest):
    wi_refs=rest[:nc]
    (vec_ref,bi_ref,out_ref,dz1_ref,datt_ref,dwo_ref,dwi_ref,dwu_ref,dvec_ref,dbi_ref,
        mid_s,att_s,dffn_s,dattn_s,hid_s,din_s,acc_s)=rest[nc:]
    t=pl.program_id(0)
    D=x_ref.shape[1]; fc=D
    n=wu_ref.shape[0]; per=n//nc
    wu=lambda c: wu_ref[c*per:(c+1)*per].reshape(fc,D)
    wi=lambda c: whole(wi_refs[c])
    @pl.when(t==0)
    def _():
        dvec_ref[...]=jnp.zeros_like(dvec_ref); dbi_ref[...]=jnp.zeros_like(dbi_ref)
    @pl.when(t<nb)
    def _():
        rows=pl.ds(pl.multiple_of(t*bi,bi),bi)
        b_out,ga,sa,b_outer,gf,sf=[vec_ref[k:k+1,:] for k in range(6)]
        att=att_ref[...]
        att_s[rows,:]=att
        z1=x_ref[...].astype(F32)+dot(att,whole(wo_ref))+b_out
        zh1,r1=ln_stats(z1)
        middle=zh1*ga+sa
        mid=middle.astype(BF)
        mid_s[rows,:]=mid
        acc_s[...]=middle+b_outer
        for c in range(nc):
            cs=slice(c*fc,(c+1)*fc)
            v=dot(mid,wi(c))+bi_ref[:,cs]
            u=v*v
            th=jnp.tanh(v*(C0+(C0*C1)*u))
            hv=0.5*v
            hid=(hv+hv*th).astype(BF)
            dg=0.5+0.5*th+hv*(1.0-th*th)*(C0+(3*C0*C1)*u)
            hid_s[rows,cs]=hid
            din_s[rows,cs]=dg.astype(BF)
            acc_s[...]+=dot(hid,wu(c))
        zh2,r2=ln_stats(acc_s[...])
        out_ref[...]=(zh2*gf+sf).astype(BF)
        g=cot_ref[...].astype(F32)
        dz2=ln_back(g*gf,zh2,r2)
        dffn=dz2.astype(BF)
        dffn_s[rows,:]=dffn
        acc_s[...]=dz2
        dbs=[]
        for c in range(nc):
            cs=slice(c*fc,(c+1)*fc)
            dh=dot(dffn,wu(c),NT)
            din=(dh*din_s[rows,cs].astype(F32)).astype(BF)
            din_s[rows,cs]=din
            dbi_ref[:,cs]+=rowsum(din.astype(F32))
            acc_s[...]+=dot(din,wi(c),NT)
        dm=acc_s[...]
        dz1=ln_back(dm*ga,zh1,r1)
        dz1_ref[...]=dz1
        dattn=dz1.astype(BF)
        dattn_s[rows,:]=dattn
        datt_ref[...]=dot(dattn,whole(wo_ref),NT).astype(BF)
        dvec_ref[...]+=jnp.concatenate([rowsum(dz1),rowsum(dm*zh1),rowsum(dm),rowsum(dz2),rowsum(g*zh2),rowsum(g),jnp.zeros((2,D),F32)],axis=0)
    @pl.when(t==nb)
    def _():
        dwo_ref[...]=dot(att_s[...],dattn_s[...],TN).astype(BF).reshape(dwo_ref.shape)
    for c in range(nc):
        cs=slice(c*fc,(c+1)*fc)
        @pl.when(t==nb+c)
        def _():
            dwi_ref[...]=dot(mid_s[...],din_s[:,cs],TN).astype(BF).reshape(dwi_ref.shape)
            dwu_ref[...]=dot(hid_s[:,cs],dffn_s[...],TN).astype(BF).reshape(dwu_ref.shape)

def middle(x,att,cot,g,vec,b_inner,bi=256):
    L,D=x.shape; n,parts,s,_=g.shape; nc=(parts-1)//2; FF=nc*D; nb=L//bi; per=n//nc
    row=pl.BlockSpec((bi,D),lambda t:(jnp.minimum(t,nb-1),0))
    cc=lambda t: jnp.clip(t-nb,0,nc-1)
    w=lambda j: pl.BlockSpec((n,1,s,D),lambda t:(0,j,0,0),pipeline_mode=ONE)
    return pl.pallas_call(functools.partial(mid_kernel,nb,bi,nc),grid=(nb+nc,),
        in_specs=[row,row,row,w(nc),pl.BlockSpec((n,nc,s,D),lambda t:(0,0,0,0),pipeline_mode=ONE)]+[w(nc+1+j) for j in range(nc)]
            +[pl.BlockSpec((8,D),lambda t:(1,0)),pl.BlockSpec((1,FF),lambda t:(0,0))],
        out_specs=[row,row,row,pl.BlockSpec((n,s,D),lambda t:(0,0,0)),pl.BlockSpec((n,1,s,D),lambda t:(0,cc(t),0,0)),
            pl.BlockSpec((per,nc,s,D),lambda t:(cc(t),0,0,0)),
            pl.BlockSpec((8,D),lambda t:(0,0)),pl.BlockSpec((1,FF),lambda t:(0,0))],
        out_shape=[jax.ShapeDtypeStruct((L,D),BF),jax.ShapeDtypeStruct((L,D),F32),jax.ShapeDtypeStruct((L,D),BF),
            jax.ShapeDtypeStruct((n,s,D),BF),jax.ShapeDtypeStruct((n,nc,s,D),BF),jax.ShapeDtypeStruct((n,nc,s,D),BF),
            jax.ShapeDtypeStruct((8,D),F32),jax.ShapeDtypeStruct((1,FF),F32)],
        scratch_shapes=[pltpu.VMEM((L,D),BF)]*4+[pltpu.VMEM((L,FF),BF)]*2+[pltpu.VMEM((bi,D),F32)],
        compiler_params=CP(),name="middle")(x,att,cot,*([g]*(2+nc)),vec,b_inner)

def pulled(ds,ws):
    out=None
    for g in range(len(ws)//3):
        for j,d in enumerate(ds):
            t=dot(d[:,g*GL:(g+1)*GL],whole(ws[3*g+j]),NT)
            out=t if out is None else out+t
    return out

def last_kernel(nb,bi,x_ref,dq_ref,dk_ref,dv_ref,dz_ref,em_ref,dr_ref,*rest):
    ws=rest[:-6]
    gi_ref,dwq_ref,dwk_ref,dwv_ref,dwp_ref,dbv_ref=rest[-6:]
    t=pl.program_id(0)
    @pl.when(t<nb)
    def _():
        rows=pl.ds(pl.multiple_of(t*bi,bi),bi)
        gi_ref[...]=dz_ref[...]+pulled([r[rows,:] for r in (dq_ref,dk_ref,dv_ref)],ws)
    @pl.when(t==nb)
    def _(): dwq_ref[...]=dot(x_ref[...],dq_ref[...],TN).astype(BF)
    @pl.when(t==nb+1)
    def _(): dwk_ref[...]=dot(x_ref[...],dk_ref[...],TN).astype(BF)
    @pl.when(t==nb+2)
    def _():
        dwv_ref[...]=dot(x_ref[...],dv_ref[...],TN).astype(BF)
        dbv_ref[...]=rowsum(dv_ref[...].astype(F32))
    @pl.when(t==nb+3)
    def _(): dwp_ref[...]=dot(em_ref[...],dr_ref[...],TN).astype(BF)

def last(x,dq,dk,dv,dz1,em,dr,gs,bi=256):
    L,D=x.shape; nb=L//bi; n,_,s,_=gs[0].shape
    w=[pl.BlockSpec((n,1,s,GL),lambda t,j=j:(0,j,0,0),pipeline_mode=ONE) for _ in gs for j in range(3)]
    row=pl.BlockSpec((bi,D),lambda t:(jnp.minimum(t,nb-1),0))
    full=lambda sh: pl.BlockSpec(sh,lambda t:(0,0),pipeline_mode=ONE)
    o=pl.BlockSpec((D,D),lambda t:(0,0))
    W=jax.ShapeDtypeStruct((D,D),BF)
    return pl.pallas_call(functools.partial(last_kernel,nb,bi),grid=(nb+4,),
        in_specs=[full((L,D))]*4+[row,full((2*L,D)),full((2*L,D))]+w,
        out_specs=[row,o,o,o,o,pl.BlockSpec((1,D),lambda t:(0,0))],
        out_shape=[jax.ShapeDtypeStruct((L,D),F32),W,W,W,W,jax.ShapeDtypeStruct((1,D),F32)],
        compiler_params=CP(),name="last")(x,dq,dk,dv,dz1,em,dr,*[g for g in gs for _ in range(3)])

VECTORS=(5,0,1,2,3,8,9,10,14,11,12,13)

def finish_kernel(dz_ref,dq_ref,dk_ref,dv_ref,*rest):
    ws=rest[:9]
    (wu_ref,wi_ref,wo_ref,g0_ref,g1_ref,g2_ref,sv_ref,
        gi_ref,owq_ref,owk_ref,owv_ref,owp_ref,owu_ref,owi_ref,owo_ref)=rest[9:24]
    vecs=rest[24:]
    gi_ref[...]=dz_ref[...]+pulled([r[...] for r in (dq_ref,dk_ref,dv_ref)],ws)
    @pl.when(pl.program_id(0)==0)
    def _():
        for j,o in enumerate((owq_ref,owk_ref,owv_ref,owp_ref)):
            for g,r in enumerate((g0_ref,g1_ref,g2_ref)): o[:,g*GL:(g+1)*GL]=r[j]
        owu_ref[...]=wu_ref[...]; owi_ref[...]=wi_ref[...]; owo_ref[...]=wo_ref[...]
        for r,o in zip(VECTORS,vecs): o[...]=sv_ref[r:r+o.shape[0],:o.shape[1]]

def finish(dq,dk,dv,dz1,gs,wu,wi,wo,groups,sv,bi=256):
    L,D=dq.shape; nb=L//bi; n,_,s,_=gs[0].shape; fs=wu.shape[0]
    w=[pl.BlockSpec((n,1,s,GL),lambda t,j=j:(0,j,0,0),pipeline_mode=ONE) for _ in gs for j in range(3)]
    row=pl.BlockSpec((bi,D),lambda t:(t,0))
    full=lambda sh: pl.BlockSpec(sh,lambda t:(0,)*len(sh),pipeline_mode=ONE)
    outs=[(s,D)]*4+[wu.shape,wi.shape,wo.shape]+[(2,s) if r==3 else (1,fs) if r==14 else (1,s) for r in VECTORS]
    return pl.pallas_call(finish_kernel,grid=(nb,),
        in_specs=[row]*4+w+[full(wu.shape),full(wi.shape),full(wo.shape)]+[full(g_.shape) for g_ in groups]+[full(sv.shape)],
        out_specs=[row]+[full(o) for o in outs],
        out_shape=[jax.ShapeDtypeStruct((L,D),F32)]+[jax.ShapeDtypeStruct(o,F32) for o in outs],
        compiler_params=CP(),name="finish")(dz1,dq,dk,dv,*[g for g in gs for _ in range(3)],wu,wi,wo,*groups,sv)

def local(R,inputs,token_types,buckets,wq,wk,wv,bv,wp,bc,bp,bt,te,wo,bo,ga,sa,wi,b_i,wu,bu,gf,sf,cot):
    s,D=wq.shape; n=D//s; FF=wi.shape[1]; fs=FF//n; kk=FF//D
    SL=-(-max(s,fs)//128)*128
    z=jnp.zeros((s,),BF)
    wide=lambda a: jnp.pad(a,((0,0),(0,SL-a.shape[1])))
    small=jnp.concatenate([wide(jnp.stack([bc,bp,bt,te[0],te[1],bv,z,z,bo,ga,sa,bu,gf,sf])),wide(b_i[None]),jnp.zeros((1,SL),BF)])
    x=inputs[0]
    bk=jnp.pad(buckets,(0,1))[None]
    e,att,linv,q,k,v,r,g2,ga_,gb_,gc_,vec,fb,oh,xt,et=fore(R,x,wq,wk,wv,wp,wo,wi,wu,small,token_types,bk)
    g1=(ga_,gb_,gc_)
    out,dz1,datt,dwo,dwi,dwu,dvec2,dbi=middle(x,att,cot[0],g2,vec,fb)
    res=att_bwd(R,q,k,v,r,oh,vec,e,att,linv,datt,dwu,dwi,dwo,xt,et,dvec2,dbi)
    dq,dk,dv=res[:3]
    if is_square(n,R):
        wu_,wi_,wo_,*gr,sv=res[3:]
        o=finish(dq,dk,dv,dz1,g1,wu_,wi_,wo_,gr,sv)
        gin,dwq,dwk,dwv,dwp,dwu,dwi,dwo=o[:8]
        c=[a[0] for a in o[8:]]
        return (out[None],gin[None],dwq,dwk,dwv,c[0],dwp,c[1],c[2],c[3],o[12],dwo,c[5],c[6],c[7],dwi,c[8],dwu,c[9],c[10],c[11])
    dr,dvec=res[3:]
    gin,dwq,dwk,dwv,dwp,dbv=last(x,dq,dk,dv,dz1,et.T,dr,g1)
    blk=lambda a: a.reshape(n,-1,D)
    r1=jnp.concatenate([blk(dwo),blk(dwi),blk(dwu)],axis=1)
    sv=jnp.concatenate([dbv,dvec[:5],dvec2[:6]]).reshape(12,n,s).transpose(1,0,2).reshape(n,12*s)
    pad=-(12*s+fs)%D
    sv=jnp.concatenate([sv,dbi.reshape(n,fs),jnp.zeros((n,pad),F32)],axis=1).astype(BF).reshape(n,-1,D)
    r2=jnp.concatenate([blk(dwq),blk(dwk),blk(dwv),blk(dwp),sv],axis=1)
    t1=lax.psum_scatter(r1,"shard",scatter_dimension=0,tiled=False).astype(F32)
    t1=lax.psum(t1,"rep")
    t2=lax.psum_scatter(r2,"shard",scatter_dimension=0,tiled=False).astype(F32)
    t2=lax.psum(t2,"rep")
    tv=t2[4*s:].reshape(-1)
    c=lambda j: tv[j*s:(j+1)*s]
    return (out[None],gin[None],t2[:s],t2[s:2*s],t2[2*s:3*s],c(0),t2[3*s:4*s],c(1),c(2),c(3),jnp.stack([c(4),c(5)]),
        t1[:s],c(6),c(7),c(8),jnp.concatenate([t1[(1+j)*s:(2+j)*s] for j in range(kk)],axis=1),tv[12*s:12*s+fs],t1[(1+kk)*s:],c(9),c(10),c(11))

def solution(mesh):
    both=("rep","shard")
    v=P("shard"); w=P("shard",None); a3=P(both,None,None)
    in_specs=(a3,P(both,None),P(),w,w,w,v,w,v,v,v,P(None,"shard"),w,v,v,v,w,v,w,v,v,v,a3)
    out_specs=(a3,a3,w,w,w,v,w,v,v,v,P(None,"shard"),w,v,v,v,w,v,w,v,v,v)
    return jax.shard_map(functools.partial(local,mesh.shape["rep"]),mesh=mesh,in_specs=in_specs,out_specs=out_specs,check_vma=False)
```

```python
import functools, math
import jax, jax.numpy as jnp
from jax import lax
from jax.experimental import pallas as pl
from jax.experimental.pallas import tpu as pltpu
from jax.sharding import PartitionSpec as P
import numpy as np
F32=jnp.float32; BF=jnp.bfloat16
LOG2E=math.log2(math.e); LN2=math.log(2.0)
NT=(((1,),(1,)),((),())); NN=(((1,),(0,)),((),())); TN=(((0,),(0,)),((),()))
def dot(a,b,dims=NN): return lax.dot_general(a,b,dims,preferred_element_type=F32)

def shape_of(n):
    Z=4 if n%8==0 else 1
    return Z,n//(2*Z)

class Place:
    def __init__(self,n,R):
        self.n=n; self.R=R; self.rep=lax.axis_index("rep"); self.Z,self.X=shape_of(n)
        me=lax.axis_index("shard")
        self.me=me; self.c=lax.rem(me,2); q=lax.div(me,2)
        self.x=lax.rem(q,self.X); self.z=lax.div(q,self.X)
    def at(self,z,x,c): return (z*self.X+x)*2+c
    def neighbours(self):
        z,x,c=self.z,self.x,self.c
        out=[(None,self.at(z,x,1-c))]
        if self.Z>1: out+=[(z>0,self.at(z-1,x,c)),(z<self.Z-1,self.at(z+1,x,c))]
        if self.X>1: out+=[(x>0,self.at(z,x-1,c)),(x<self.X-1,self.at(z,x+1,c))]
        return out

def when(cond,fn):
    if cond is None: fn()
    else: pl.when(cond)(fn)

def both(*conds):
    out=None
    for k in conds:
        if k is not None: out=k if out is None else jnp.logical_and(out,k)
    return out

def greet(place):
    bar=pltpu.get_barrier_semaphore()
    total=jnp.int32(0)
    for ok,idx in place.neighbours():
        when(ok,lambda idx=idx: pl.semaphore_signal(bar,inc=1,device_id={"shard":idx},device_id_type=pl.DeviceIdType.MESH))
        total=total+(1 if ok is None else ok.astype(jnp.int32))
    for d in range(1,place.R):
        pl.semaphore_signal(bar,inc=1,device_id={"rep":lax.rem(place.rep+d,place.R)},device_id_type=pl.DeviceIdType.MESH)
    total=total+(place.R-1)
    pl.semaphore_wait(bar,total)

def gather_sems(n):
    Z,X=shape_of(n); A=1+2*(Z-1); J=1+2*(X-1)
    return [pltpu.SemaphoreType.DMA((max(1,2*(Z-1)),2)),pltpu.SemaphoreType.DMA((max(1,A*2*(X-1)),2)),pltpu.SemaphoreType.DMA((A*J,2))]

def gather_events(place,G,sems,t0,dz,dx,last,direct=False):
    p=place; Z,X=p.Z,p.X; zs,xs,cs=sems
    z,x,c=p.z,p.x,p.c
    def copy(idx,sem,k,to):
        return pltpu.make_async_remote_copy(src_ref=G.at[idx],dst_ref=G.at[idx],send_sem=sem.at[k,0],recv_sem=sem.at[k,1],
            device_id={"shard":to},device_id_type=pl.DeviceIdType.MESH)
    ev=[]; sends=[]
    A=1+2*(Z-1); J=1+2*(X-1)
    def slot(a):
        if a==0: return z,None
        s=(a-1)//2
        return (z-1-s,z-1-s>=0) if a%2 else (z+1+s,z+1+s<Z)
    def col(j):
        if j==0: return x,None
        k=(j-1)//2
        return (x-1-k,x-1-k>=0) if j%2 else (x+1+k,x+1+k<X)
    def zmsg(d,s):
        lev=z-s if d==0 else z+s
        ok=both(z+1<Z,z-s>=0) if d==0 else both(z>0,z+s<Z)
        return ok,copy(p.at(lev,x,c),zs,2*s+d,p.at(z+1 if d==0 else z-1,x,c))
    def zarr(d,s):
        lev,ok=slot(1+2*s+d)
        return ok,copy(p.at(lev,x,c),zs,2*s+d,p.at(z,x,1-c))
    def zfar(d,s):
        to=z+1+s if d==0 else z-1-s
        return (to<Z if d==0 else to>=0),copy(p.at(z,x,c),zs,2*s+d,p.at(to,x,c))
    def xmsg(a,d,k):
        lev,va=slot(a)
        cx=x-k if d==0 else x+k
        ok=both(va,x+1<X,x-k>=0) if d==0 else both(va,x>0,x+k<X)
        return ok,copy(p.at(lev,cx,c),xs,(a*(X-1)+k)*2+d,p.at(lev*0+z,x+1 if d==0 else x-1,c))
    def xarr(a,d,k):
        lev,va=slot(a); cx,vc=col(1+2*k+d)
        return both(va,vc),copy(p.at(lev,cx,c),xs,(a*(X-1)+k)*2+d,p.at(z,x,1-c))
    def cmsg(a,j):
        lev,va=slot(a); cx,vc=col(j)
        return both(va,vc),copy(p.at(lev,cx,c),cs,a*J+j,p.at(z,x,1-c))
    def carr(a,j):
        lev,va=slot(a); cx,vc=col(j)
        return both(va,vc),copy(p.at(lev,cx,1-c),cs,a*J+j,p.at(z,x,1-c))
    def add(t,order,fn): ev.append((min(t,last),order,fn))
    def starter(ms):
        def fn():
            for ok,m in ms: when(ok,m.start)
        return fn
    def waiter(ms):
        def fn():
            for ok,m in ms: when(ok,m.wait_recv)
        return fn
    for s in range(Z):
        t=t0+s*dz
        if s>0: add(t,(0,s,0),waiter([zarr(d,s-1) for d in range(2)]))
        if s<Z-1:
            ms=[(zfar if direct else zmsg)(d,s) for d in range(2)]; sends+=ms
            if direct: add(t0,(-0.5,s),starter(ms))
            else: add(t,(0,s,1),starter(ms))
    for a in range(A):
        ra=(a+1)//2; ta=t0+ra*dz
        for k in range(X):
            t=ta+k*dx
            if k>0: add(t,(1,k,a,0),waiter([xarr(a,d,k-1) for d in range(2)]))
            if k<X-1:
                ms=[xmsg(a,d,k) for d in range(2)]; sends+=ms
                add(t,(1,k,a,1),starter(ms))
            ms=[cmsg(a,j) for j in range(J) if (j+1)//2==k]; sends+=ms
            add(t,(1,k,a,2),starter(ms))
    add(last,(2,),waiter([carr(a,j) for a in range(A) for j in range(J)]))
    def done():
        for ok,m in sends: when(ok,m.wait_send)
    add(last,(3,),done)
    ev.sort(key=lambda e:(e[0],e[1]))
    return ev

def square_sems(n):
    Z,X=shape_of(n); A=1+2*(Z-1)
    return [pltpu.SemaphoreType.DMA((2*(Z-1),2)),pltpu.SemaphoreType.DMA((A,2)),pltpu.SemaphoreType.DMA((A,2)),pltpu.SemaphoreType.DMA((3*A,2))]

def square_events(place,G,sems,t0,dz,dx,dy,last,parts=None):
    p=place; Z=p.Z; zs,xs,ys,cs=sems
    z,x,c,rep=p.z,p.x,p.c,p.rep
    lo,parts=parts or (0,G.shape[1]); cut=(parts+1)//2
    halves=((lo,cut),(lo+cut,parts-cut))
    A=1+2*(Z-1)
    def copy(idx,part,sem,k,to):
        ref=G.at[idx,pl.ds(*((lo,parts) if part is None else halves[part]))]
        return pltpu.make_async_remote_copy(src_ref=ref,dst_ref=ref,send_sem=sem.at[k,0],recv_sem=sem.at[k,1],
            device_id=to,device_id_type=pl.DeviceIdType.MESH)
    def slot(a):
        if a==0: return z,None
        s=(a-1)//2
        return (z-1-s,z-1-s>=0) if a%2 else (z+1+s,z+1+s<Z)
    other={"shard":p.at(z,x,1-c)}; across={"shard":p.at(z,1-x,c)}; above={"rep":1-rep}
    def zmsg(d,s):
        lev=z-s if d==0 else z+s
        ok=both(z+1<Z,z-s>=0) if d==0 else both(z>0,z+s<Z)
        return ok,copy(p.at(lev,x,c),None,zs,2*s+d,{"shard":p.at(z+1 if d==0 else z-1,x,c)})
    def zarr(d,s):
        lev,ok=slot(1+2*s+d)
        return ok,copy(p.at(lev,x,c),None,zs,2*s+d,other)
    def xmsg(a,h):
        lev,va=slot(a)
        return both(va,rep==h),copy(p.at(lev,x,c),h,xs,a,across)
    def xarr(a,h):
        lev,va=slot(a)
        return both(va,rep==h),copy(p.at(lev,1-x,c),h,xs,a,across)
    def ymsg(a,h):
        lev,va=slot(a)
        return both(va,rep==h),copy(p.at(lev,1-x,c),h,ys,a,above)
    def yarr(a,h):
        lev,va=slot(a)
        return both(va,rep==1-h),copy(p.at(lev,1-x,c),h,ys,a,above)
    def cmsg(a,h,core):
        lev,va=slot(a); cc=c if core==0 else 1-c
        if h is None: return [(va,copy(p.at(lev,x,cc),None,cs,3*a,other))]
        return [(both(va,rep==(g if h==0 else 1-g)),copy(p.at(lev,1-x,cc),g,cs,3*a+1+h,other)) for g in range(2)]
    ev=[]; sends=[]
    def add(t,order,fn): ev.append((min(t,last),order,fn))
    def start(t,order,ms):
        sends.extend(ms)
        def fn():
            for ok,m in ms: when(ok,m.start)
        add(t,order,fn)
    def await_(t,order,ms):
        def fn():
            for ok,m in ms: when(ok,m.wait_recv)
        add(t,order,fn)
    for s in range(Z):
        t=t0+(dz[s] if isinstance(dz,tuple) else s*dz)
        if s>0: await_(t,(0,s,0),[zarr(d,s-1) for d in range(2)])
        if s<Z-1: start(t,(0,s,1),[zmsg(d,s) for d in range(2)])
        for a in ([0] if s==0 else [2*s-1,2*s]):
            start(t,(1,s,a),[xmsg(a,h) for h in range(2)]+cmsg(a,None,0))
            await_(t+dx,(2,s,a,0),[xarr(a,h) for h in range(2)])
            start(t+dx,(2,s,a,1),[ymsg(a,h) for h in range(2)]+cmsg(a,0,0))
            await_(t+dx+dy,(3,s,a,0),[yarr(a,h) for h in range(2)])
            start(t+dx+dy,(3,s,a,1),cmsg(a,1,0))
    await_(last,(4,),[m for a in range(A) for h in (None,0,1) for m in cmsg(a,h,1)])
    def done():
        for ok,m in sends: when(ok,m.wait_send)
    add(last,(5,),done)
    ev.sort(key=lambda e:(e[0],e[1]))
    return ev

def is_square(n,R): return R==2 and shape_of(n)==(4,2)
def spread_sems(n,R): return square_sems(n) if is_square(n,R) else gather_sems(n)
def spread_events(place,G,sems,t0,dz,dx,dy,last,parts=None):
    if is_square(place.n,place.R): return square_events(place,G,sems,t0,dz,dx,dy,last,parts)
    return gather_events(place,G,sems,t0,dz,dx,last)

def run_events(step,events,after=False):
    picked=[e for e in events if (e[0]-int(e[0])>=0.5)==after]
    for t in sorted({int(e[0]) for e in picked}):
        fns=[e[2] for e in picked if int(e[0])==t]
        def fire(fns=fns):
            for f in fns: f()
        pl.when(step==t)(fire)

def sum_scratch(n,Q,s,D,parts):
    Z,X=shape_of(n); dma=pltpu.SemaphoreType.DMA
    V=lambda *sh: pltpu.VMEM(sh,BF)
    return [V(Z,X,Q,s,D),V(Z,X,Q,s,D),V(Z,Q,s,D//2),V(Z,Q,s,D//2),V(2,Z-1,Q,s,D),V(Q,s,D),
        dma((parts,)),dma((parts,2)),dma((Z,2)),dma((Z,2)),dma((2*(Z-1),2)),dma((1,2))]
SUM_REFS=12

def sum_events(place,srcs,refs,times,store):
    p=place; Z=p.Z
    z,x,c,rep=p.z,p.x,p.c,p.rep
    S,B,YB,XB,ZB,FB,ls,cs,ys,xs,zs,fs=refs
    Q=S.shape[2]; H=S.shape[4]//2
    tc,ta,ty,tx,tz,tend=times
    half=lambda r: pl.ds(pl.multiple_of(r*H,128),H)
    other={"shard":p.at(z,x,1-c)}; across={"shard":p.at(z,1-x,c)}; above={"rep":1-rep}
    def rc(src,dst,sem,k,to):
        return pltpu.make_async_remote_copy(src_ref=src,dst_ref=dst,send_sem=sem.at[k,0],recv_sem=sem.at[k,1],device_id=to,device_id_type=pl.DeviceIdType.MESH)
    ev=[]; sends=[]
    def add(t,order,fn): ev.append((t,order,fn))
    def start(t,order,ms):
        sends.extend(ms)
        def fn():
            for ok,m in ms: when(ok,m.start)
        add(t,order,fn)
    loads=[pltpu.make_async_copy(r.at[:,:,c],S.at[:,:,pl.ds(q,k)],ls.at[j]) for j,(r,q,k) in enumerate(srcs)]
    cores=[(None,rc(r.at[:,:,1-c],B.at[:,:,pl.ds(q,k)],cs,j,other)) for j,(r,q,k) in enumerate(srcs)]
    def plus(a,b): return (a.astype(F32)+b.astype(F32)).astype(BF)
    def begin():
        for m in loads: m.start()
    add(tc,(0,),begin)
    start(tc,(1,),cores)
    def merge():
        for m in loads: m.wait()
        for _,m in cores: m.wait_recv()
        def body(k,_):
            lev=lax.div(k,2*Q); r=lax.rem(k,2*Q); xx=lax.div(r,Q); q=lax.rem(r,Q)
            S[lev,xx,q]=plus(S[lev,xx,q],B[lev,xx,q])
            return 0
        lax.fori_loop(0,2*Z*Q,body,0)
    add(ta,(2,),merge)
    def levels(d): return [(z,None)] if d==0 else [(z-d,z-d>=0),(z+d,z+d<Z)]
    for i,d in enumerate(range(Z-1,-1,-1)):
        L=levels(d)
        ysend=[(ok,rc(S.at[l,1-x,:,:,half(1-rep)],YB.at[l],ys,l,above)) for l,ok in L]
        xsend=[(ok,rc(S.at[l,1-x,:,:,half(rep)],XB.at[l],xs,l,across)) for l,ok in L]
        start(ty[i],(3,i),ysend)
        def ytake(L=L,ysend=ysend):
            for (l,ok),(_,m) in zip(L,ysend):
                def go(l=l,m=m):
                    m.wait_recv()
                    def body(q,_):
                        S[l,1-x,q,:,half(rep)]=plus(S[l,1-x,q,:,half(rep)],YB[l,q])
                        return 0
                    lax.fori_loop(0,Q,body,0)
                when(ok,go)
        add(tx[i],(4,i,0),ytake)
        start(tx[i],(4,i,1),xsend)
        def xtake(L=L,xsend=xsend):
            for (l,ok),(_,m) in zip(L,xsend):
                def go(l=l,m=m):
                    m.wait_recv()
                    def body(q,_):
                        S[l,x,q,:,half(rep)]=plus(S[l,x,q,:,half(rep)],XB[l,q])
                        return 0
                    lax.fori_loop(0,Q,body,0)
                when(ok,go)
        add(tz[i],(5,i,0),xtake)
        if d<=Z-2:
            def ztake(d=d):
                for dr,(l,ok) in enumerate([(z-d,both(z+1<Z,z-d>=0)),(z+d,both(z>0,z+d<Z))]):
                    def go(dr=dr,l=l):
                        rc(ZB.at[dr,d],ZB.at[dr,d],zs,2*d+dr,other).wait_recv()
                        def body(q,_):
                            S[l,x,q]=plus(S[l,x,q],ZB[dr,d,q])
                            return 0
                        lax.fori_loop(0,Q,body,0)
                    pl.when(ok)(go)
            add(tz[i],(5,i,1),ztake)
        if d>=1:
            start(tz[i],(5,i,2),[(z-d>=0,rc(S.at[z-d,x],ZB.at[0,d-1],zs,2*(d-1),{"shard":p.at(z-1,x,c)})),
                (z+d<Z,rc(S.at[z+d,x],ZB.at[1,d-1],zs,2*(d-1)+1,{"shard":p.at(z+1,x,c)}))])
    final=[(None,rc(S.at[z,x],FB,fs,0,above))]
    start(tz[-1],(6,),final)
    def finish():
        final[0][1].wait_recv()
        for q in range(Q): store(q,S[z,x,q].astype(F32)+FB[q].astype(F32))
    add(tend,(7,),finish)
    def done():
        for ok,m in sends: when(ok,m.wait_send)
    add(tend,(8,),done)
    return ev

def greet_all(place):
    bar=pltpu.get_barrier_semaphore()
    n,R=place.n,place.R
    def hello(d,_):
        pl.semaphore_signal(bar,inc=1,device_id={"shard":lax.rem(place.me+d,n)},device_id_type=pl.DeviceIdType.MESH)
        return 0
    lax.fori_loop(1,n,hello,0)
    for d in range(1,R):
        pl.semaphore_signal(bar,inc=1,device_id={"rep":lax.rem(place.rep+d,R)},device_id_type=pl.DeviceIdType.MESH)
    return lambda: pl.semaphore_wait(bar,n+R-2)

STRIDE=32
def tables(length,width):
    half=width//2; count=2*length//STRIDE
    rates=np.exp(np.arange(half)*(-2.0*math.log(10000.0)/width))
    def pack(angles):
        full=np.concatenate([np.sin(angles),np.cos(angles)],axis=1).astype(np.float32)
        hi=full.astype(jnp.bfloat16); lo=(full-hi.astype(np.float32)).astype(jnp.bfloat16)
        return np.concatenate([hi,lo],axis=0)
    coarse=(np.arange(count)*STRIDE-length)[:,None]*rates[None]
    fine=np.arange(STRIDE)[:,None]*rates[None]
    return pack(coarse),pack(fine)

BI=256
ONE=pl.Buffered(1)


def lane_half(rows, lanes):
    lane=lax.broadcasted_iota(jnp.int32,(rows,lanes),1)
    return (lane//64)%2

def split_hi_lo(v):
    hi=v.astype(BF); return hi,(v-hi.astype(F32)).astype(BF)

def queries(q, vec, oh):
    s=0.125*LOG2E
    cq=((q+vec[0:1])*s).astype(BF)
    pq=((q+vec[1:2])*s).astype(BF)
    tq=(q+vec[2:3])*0.125
    return cq,pq,tq

GL=256

def fore_kernel(n,R,x_ref,wq_ref,wk_ref,wv_ref,wp_ref,wo_ref,wi_ref,wu_ref,small_ref,kinds_ref,buckets_ref,ta_ref,tb_ref,
        e_ref,att_ref,linv_ref,q_ref,k_ref,v_ref,r_ref,g_ref,w0_ref,w1_ref,w2_ref,vec_ref,bi_ref,oh_ref,xt_ref,et_ref,
        em,wg,all_s,mine,own,own2,ssem,*sems):
    bi=att_ref.shape[0]; L=x_ref.shape[0]; W=L+bi
    pair=pl.program_id(0); i=pl.program_id(1); nb=L//bi
    step=pair*nb+i; steps=6*nb
    place=Place(n,R); me=place.me
    kk=wu_ref.shape[0]; D=wo_ref.shape[1]
    groups=D//GL; per=len(spread_sems(n,R)); square=is_square(n,R); gs=len(gather_sems(n))
    ws=(wq_ref,wk_ref,wv_ref,wp_ref)
    loads=[[pltpu.make_async_copy(w.at[:,pl.ds(g*GL,GL)],wg.at[g,me,j],own2.at[g,j]) for j,w in enumerate(ws)] for g in range(groups)]
    keeps=[pltpu.make_async_copy(wg.at[g],o,own2.at[g,4]) for g,o in enumerate((w0_ref,w1_ref,w2_ref))]
    owns=[pltpu.make_async_copy(wu_ref,mine.at[pl.ds(0,kk)],own.at[0]),pltpu.make_async_copy(wo_ref,mine.at[kk],own.at[1])]
    owns+=[pltpu.make_async_copy(wi_ref.at[:,pl.ds(j*D,D)],mine.at[kk+1+j],own.at[2+j]) for j in range(kk)]
    keep=pltpu.make_async_copy(mine,g_ref.at[me],own.at[2+kk])
    def send(d):
        return pltpu.make_async_remote_copy(src_ref=all_s.at[me],dst_ref=all_s.at[me],send_sem=ssem.at[d,0],recv_sem=ssem.at[d,1],
            device_id={"shard":lax.rem(me+d,n)},device_id_type=pl.DeviceIdType.MESH)
    def arrive(d):
        w=lax.rem(me-d+n,n)
        return pltpu.make_async_remote_copy(src_ref=all_s.at[w],dst_ref=all_s.at[w],send_sem=ssem.at[d,0],recv_sem=ssem.at[d,1],
            device_id={"shard":lax.rem(me+d,n)},device_id_type=pl.DeviceIdType.MESH)
    def enter():
        for g in range(groups):
            for m in loads[g]: m.start()
        for m in owns: m.start()
        met=greet_all(place)
        all_s[me]=small_ref[...]
        for g in range(groups):
            for m in loads[g]: m.wait()
        met()
    def share():
        def go(d,_):
            send(d).start()
            return 0
        lax.fori_loop(1,n,go,0)
    def enter2():
        for m in owns: m.wait()
        keep.start()
    def prepare():
        L2=buckets_ref.shape[1]
        count=L2//STRIDE
        def body(j,_):
            rows=pl.ds(pl.multiple_of(j*256,256),256)
            b=buckets_ref[:,rows]
            hot=lambda v,m: jnp.where(v==lax.rem(lax.broadcasted_iota(jnp.int32,(2*m,256),0),m),1.0,0.0).astype(BF)
            A=dot(hot(lax.div(b,STRIDE),count),ta_ref[...],TN)
            B=dot(hot(lax.rem(b,STRIDE),STRIDE),tb_ref[...],TN)
            h=A.shape[1]//2
            sa,ca,sb,cb=A[:,:h],A[:,h:],B[:,:h],B[:,h:]
            both_=jnp.concatenate([sa*cb+ca*sb,ca*cb-sa*sb],axis=1)
            em[rows,:]=both_.astype(BF)
            et_ref[:,rows]=both_.T.astype(BF)
            return 0
        lax.fori_loop(0,L2//256,body,0)
        def turn(j,_):
            rows=pl.ds(pl.multiple_of(j*256,256),256)
            xt_ref[:,rows]=x_ref[rows,:].astype(F32).T.astype(BF)
            return 0
        lax.fori_loop(0,L//256,turn,0)
        for j in range(L//256):
            kinds=kinds_ref[:,j*256:(j+1)*256]
            lane=lax.rem(lax.broadcasted_iota(jnp.int32,(128,256),0),64)
            hot=jnp.where((lax.rem(lane,3)==kinds)&(lane<6),1.0,0.0)
            oh_ref[j*256:(j+1)*256,:]=hot.T.astype(BF)
    def unpack():
        def come(d,_):
            arrive(d).wait_recv()
            send(d).wait_send()
            return 0
        lax.fori_loop(1,n,come,0)
        s=wq_ref.shape[0]; fs=bi_ref.shape[1]//n
        for w in range(n):
            a=all_s[w].astype(F32)
            vec_ref[:,w*s:(w+1)*s]=a[:,:s]
            bi_ref[:,w*fs:(w+1)*fs]=a[14:15,:fs]
    def project(g):
        col=lambda j: wg[g,:,j].reshape(D,GL)
        def rows_of(j,_):
            rows=pl.ds(pl.multiple_of(j*256,256),256)
            x=x_ref[rows,:]
            q_ref[rows,:]=dot(x,col(0))
            k_ref[rows,:]=dot(x,col(1)).astype(BF)
            v_ref[rows,:]=(dot(x,col(2))+vec_ref[5:6,g*GL:(g+1)*GL]).astype(BF)
            rows2=pl.ds(pl.multiple_of(j*512,512),512)
            r_ref[rows2,:]=dot(em[rows2,:],col(3)).astype(BF)
            return 0
        lax.fori_loop(0,L//256,rows_of,0)
    ev=[(0,(-2,),enter),(0,(1.5,),share),(0.001,(9,),prepare),(0.1,(9,),unpack),(1,(-1,),enter2),(2,(-1,),keep.wait)]
    for g,(t0,dz,dx,dy,end) in enumerate(FORE_TIMES):
        if g==0: ev+=gather_events(place,wg.at[g],sems[:gs],t0,dz,dx,end,square)
        else: ev+=spread_events(place,wg.at[g],sems[gs+(g-1)*per:gs+g*per],t0,dz,dx,dy,end)
        ev.append((end,(9,),keeps[g].start))
        ev.append((end,(10,),functools.partial(project,g)))
        ev.append((steps-0.5,(9,g),keeps[g].wait))
    rest=sems[gs+(groups-1)*per:]
    if square:
        for k,(lo,cnt) in enumerate(((0,kk),(kk,kk+1))):
            ev+=square_events(place,g_ref,rest[k*per:(k+1)*per],*FORE_REST[k],steps-0.5,(lo,cnt))
    else: ev+=spread_events(place,g_ref,rest[:per],2,6,4,4,steps-0.5)
    ev.sort(key=lambda e:(e[0],e[1]))
    run_events(step,ev)
    side=pl.ds(pl.multiple_of(lax.rem(pair,2)*128,128),128)
    vec=vec_ref[0:8,pl.ds(pl.multiple_of(pair*128,128),128)]
    rows=pl.ds(pl.multiple_of(i*bi,bi),bi)
    q=q_ref[rows,side]
    oh_i=oh_ref[rows,:]
    cq,pq,tq=queries(q,vec,None)
    rr=lax.broadcasted_iota(jnp.int32,(256,128),0)%128
    cc=lax.broadcasted_iota(jnp.int32,(256,128),1)
    M=jnp.where((rr//64==cc//64)&(cc%64<6),1.0,0.0).astype(BF)
    def tt(te):
        hi,lo=split_hi_lo(tq*(te*LOG2E))
        return dot(jnp.concatenate([hi,lo],axis=1),M)
    t0=tt(vec[3:4]); t1=tt(vec[4:5])
    tv=jnp.where(oh_i>0,t1,t0)
    hi=tv.astype(BF).astype(F32)
    lane=lax.broadcasted_iota(jnp.int32,(bi,128),1)
    tv=jnp.where(lane%64<3,hi,tv-hi).astype(BF)
    half=lane_half(bi,128)
    kext=jnp.concatenate([k_ref[:,side],oh_ref[...]],axis=1)
    vext=jnp.concatenate([v_ref[:,side],jnp.ones((L,128),BF)],axis=1)
    w0=pl.multiple_of(L-bi-i*bi,bi)
    rwin=r_ref[pl.ds(w0,W),side]
    z=jnp.zeros((),BF)
    outs=[]
    for h in range(2):
        qx=jnp.concatenate([jnp.where(half==h,cq,z),jnp.where(half==h,tv,z)],axis=1)
        pos=dot(jnp.where(half==h,pq,z),rwin,NT)
        pos=pltpu.roll(pos,W-(bi-1),1,stride=1,stride_axis=0)[:,:L]
        s=dot(qx,kext,NT)+pos
        m=jnp.max(s,axis=1,keepdims=True)
        e=jnp.exp2(s-m).astype(BF)
        e_ref[h]=e
        o=dot(e,vext)
        li=1.0/o[:,128:]
        outs.append((o[:,:128]*li,li))
    att_ref[...]=jnp.where(half==0,outs[0][0],outs[1][0]).astype(BF)
    linv_ref[...]=jnp.where(half==0,outs[0][1],outs[1][1])
    run_events(step,ev,after=True)

FORE_TIMES=((0.0,0.01,0.01,0.01,0.1),(0.2,1,1,1,8.0),(1.2,1,1,1,16.0))
FORE_REST=((4,(0,3,8,13),2,3),(4.01,(0,6,11,16),2,2))

def fore(R,x,wq,wk,wv,wp,wo,wi,wu,small,kinds,buckets,bi=BI):
    L,D=x.shape; P=D//128; nb=L//bi; s=wo.shape[0]; n=D//s; kk=wu.shape[0]//s; FF=wi.shape[1]; SL=small.shape[1]
    ta,tb=tables(L,D)
    hbm=pl.BlockSpec(memory_space=pl.ANY)
    full=lambda a: pl.BlockSpec(a.shape,lambda p,i:(0,)*len(a.shape),pipeline_mode=ONE)
    S=jax.ShapeDtypeStruct
    tile=pl.BlockSpec((bi,128),lambda p,i:(i,p))
    col=lambda k: pl.BlockSpec((k*L,GL),lambda p,i:(0,p//2))
    ta,tb=jnp.asarray(ta),jnp.asarray(tb)
    tails=[S((16,D),F32),S((1,FF),F32),S((L,128),BF),S((D,L),BF),S((D,2*L),BF)]
    dma=pltpu.SemaphoreType.DMA
    return pl.pallas_call(functools.partial(fore_kernel,n,R),grid=(P,nb),
        in_specs=[full(x)]+[hbm]*7+[full(a) for a in (small,kinds,buckets,ta,tb)],
        out_specs=[pl.BlockSpec((2,bi,L),lambda p,i:(p,i,0)),tile,tile,col(1),col(1),col(1),col(2)]+[hbm]*4+[full(t) for t in tails],
        out_shape=[S((2*P,L,L),BF),S((L,D),BF),S((L,D),F32),S((L,D),F32),S((L,D),BF),S((L,D),BF),S((2*L,D),BF),S((n,2*kk+1,s,D),BF)]
            +[S((n,4,s,GL),BF)]*3+tails,
        scratch_shapes=[pltpu.VMEM((2*L,D),BF),pltpu.VMEM((D//GL,n,4,s,GL),BF),pltpu.VMEM((n,16,SL),BF),pltpu.VMEM((2*kk+1,s,D),BF),
            dma((3+kk,)),dma((D//GL,5)),dma((n,2))]+gather_sems(n)+spread_sems(n,R)*(D//GL+1),
        compiler_params=pltpu.CompilerParams(vmem_limit_bytes=60*2**20,dimension_semantics=("arbitrary","arbitrary"),collective_id=1,has_side_effects=True),
        name="fore")(x,wq,wk,wv,wp,wo,wi,wu.reshape(kk,s,D),small,kinds,buckets,ta,tb)

TIMES_A=(0,2,(2,3,4,6),(4,5,7,8),(6,9,12,15),18)
TIMES_B=(1,4,(5,6,8,10),(7,8,11,12),(11,15,18,21),23)
TIMES_G=((8,10,(10,10,11,11),(13,13,14,14),(16,18,20,22),23),
    (16,18,(18,18,19,19),(21,21,22,22),(23,23.5,23.5,23.5),23.5),
    (23.5,23.5,(23.5,)*4,(23.5,)*4,(23.5,)*4,23.5))

def bwd_kernel(n,R,roll_bf,q_ref,k_ref,v_ref,r_ref,oh_ref,vec_ref,e_ref,att_ref,linv_ref,datt_ref,*rest):
    bi=q_ref.shape[0]; L=k_ref.shape[0]; W=L+bi
    pair=pl.program_id(0); i=pl.program_id(1); nb=L//bi; step=pair*nb+i
    square=is_square(n,R)
    if square:
        gu_ref,gi_ref,go_ref,xt_ref,et_ref,vb_ref,vi_ref=rest[:7]
        dq_ref,dk_ref,dv_ref,wu_ref,wi_ref,wo_ref,g0_ref,g1_ref,g2_ref,sv_ref=rest[7:17]
        dk_acc,dv_acc,dr_acc,dvec_ref,dq2,dk2,dv2,dr2,vec_s,src0,src1,src2=rest[17:29]
        refs=rest[29:]
        s,D=wo_ref.shape; kk=wu_ref.shape[0]//s
        def store_a(q,v): wu_ref[q*s:(q+1)*s,:]=v
        def store_b(q,v):
            if q<kk: wi_ref[:,q*D:(q+1)*D]=v
            else: wo_ref[...]=v
        place=Place(n,R); Z,X=place.Z,place.X; me=place.me
        ev=[(0,(-1,),lambda: greet(place))]
        ev+=sum_events(place,[(gu_ref,0,kk)],refs[:SUM_REFS],TIMES_A,store_a)
        ev+=sum_events(place,[(gi_ref,0,kk),(go_ref,kk,1)],refs[SUM_REFS:2*SUM_REFS],TIMES_B,store_b)
        for g,(src,out) in enumerate(((src0,g0_ref),(src1,g1_ref),(src2,g2_ref))):
            def store_g(q,v,out=out):
                if q<4: out[q]=v
                else: sv_ref[...]=v[:16,:]
            ev+=sum_events(place,[(src,0,src.shape[3])],refs[(2+g)*SUM_REFS:(3+g)*SUM_REFS],TIMES_G[g],store_g)
            def weights(src=src):
                for j,(l,r) in enumerate(((xt_ref,dq2),(xt_ref,dk2),(xt_ref,dv2),(et_ref,dr2))):
                    src[:,:,:,j]=dot(l[...],r[...]).astype(BF).reshape(Z,X,2,s,GL)
            ev.append(((2*g+2)*nb-0.5,(-1,),weights))
        def vectors():
            fs=vi_ref.shape[1]//n
            rows=jnp.concatenate([vec_s[...],vb_ref[...]],axis=0)
            row=lax.broadcasted_iota(jnp.int32,(16,GL),0)
            wide=lambda a: jnp.concatenate([a,jnp.zeros((a.shape[0],GL-a.shape[1]),F32)],axis=1)
            for w in range(n):
                v=jnp.where(row==14,wide(vi_ref[:,w*fs:(w+1)*fs]),wide(rows[:,w*s:(w+1)*s]))
                src2[w//(2*X),w//2%X,w%2,4]=jnp.concatenate([v,jnp.zeros((s-16,GL),F32)],axis=0).astype(BF)
        ev.append((6*nb-0.5,(-1.5,),vectors))
        ev.sort(key=lambda e:(e[0],e[1]))
        run_events(step,ev)
    else:
        dq_ref,dk_ref,dv_ref,dr_ref,dvec_ref,dk_acc,dv_acc,dr_acc=rest
    vec=vec_ref[...]
    q=q_ref[...]
    oh_i=oh_ref[pl.ds(pl.multiple_of(i*bi,bi),bi),:].astype(F32)
    cq,pq,tq=queries(q,vec,None)
    half=lane_half(bi,128)
    lane=lax.broadcasted_iota(jnp.int32,(bi,128),1)
    @pl.when(i==0)
    def _():
        dk_acc[...]=jnp.zeros_like(dk_acc); dv_acc[...]=jnp.zeros_like(dv_acc); dr_acc[...]=jnp.zeros_like(dr_acc)
        dvec_ref[...]=jnp.zeros_like(dvec_ref)
    P=jnp.where(lax.broadcasted_iota(jnp.int32,(bi,bi),0)+lax.broadcasted_iota(jnp.int32,(bi,bi),1)==bi-1,1.0,0.0).astype(BF)
    pqr=dot(P,pq).astype(BF)
    kext=jnp.concatenate([k_ref[...],oh_ref[...]],axis=1)
    ones2=jnp.where(lax.broadcasted_iota(jnp.int32,(L,128),1)<2,1.0,0.0).astype(BF)
    vext=jnp.concatenate([v_ref[...],ones2],axis=1)
    w0=pl.multiple_of(L-bi-i*bi,bi)
    rwin=r_ref[pl.ds(w0,W),:]
    z=jnp.zeros((),BF)
    dattl=datt_ref[...].astype(F32)*linv_ref[...]
    prod=dattl*att_ref[...].astype(F32)
    dattl=dattl.astype(BF)
    dcs=[];dps=[];dts=[];tes=[]
    dk=None; dv=None; dr=None
    for h in range(2):
        delta=-jnp.sum(jnp.where(half==h,prod,0.0),axis=1,keepdims=True)
        dhi=delta.astype(BF).astype(F32)
        dx=jnp.where(lane==0,dhi,jnp.where(lane==1,delta-dhi,0.0)).astype(BF)
        dm=jnp.where(half==h,dattl,z)
        dpd=dot(jnp.concatenate([dm,dx],axis=1),vext,NT)
        e=e_ref[h]
        ds=(e.astype(F32)*dpd).astype(BF)
        dvh=dot(e,dm,TN)
        dkh=dot(ds,jnp.where(half==h,cq,z),TN)
        dc=dot(ds,kext)
        rev=dot(P,ds)
        if roll_bf: rev=rev.astype(BF)
        rev=jnp.concatenate([rev,jnp.zeros((bi,W-L),rev.dtype)],axis=1)
        dpr=pltpu.roll(rev,0,1,stride=1,stride_axis=0).astype(BF)
        dp=dot(dpr,rwin)
        drh=dot(dpr,jnp.where(half==h,pqr,z),TN)
        dv=dvh if dv is None else dv+dvh
        dk=dkh if dk is None else dk+dkh
        dr=drh if dr is None else dr+drh
        D=jnp.where(lane<3,dc[:,128:],0.0)
        dall=jnp.sum(D,axis=1,keepdims=True)
        d1=jnp.sum(D*oh_i,axis=1,keepdims=True)
        d0=dall-d1
        dcs.append(dc[:,:128]); dps.append(dp)
        dts.append(d0*vec[3:4]+d1*vec[4:5])
        tes.append((d0,d1))
    dv_acc[...]+=dv
    dk_acc[...]+=dk
    dr_acc[pl.ds(w0,W),:]+=dr
    dcq=jnp.where(half==0,dcs[0],dcs[1]).astype(BF).astype(F32)
    dpr=jnp.where(half==0,dps[0],dps[1]).astype(BF)
    dpq=dot(P,dpr)
    dtq=jnp.where(half==0,dts[0],dts[1])
    dq=((dcq+dpq+dtq)*0.125).astype(BF)
    dq_ref[...]=dq
    d0=jnp.where(half==0,tes[0][0],tes[1][0]); d1=jnp.where(half==0,tes[0][1],tes[1][1])
    rows=[dcq*0.125,dpq*0.125,dtq*0.125,d0*tq,d1*tq]
    sums=[jnp.sum(v,axis=0,keepdims=True) for v in rows]+[jnp.zeros((3,128),F32)]
    dvec_ref[...]+=jnp.concatenate(sums,axis=0)
    @pl.when(i==nb-1)
    def _():
        dk=(dk_acc[...]*LN2).astype(BF); dv=dv_acc[...].astype(BF); dr=(dr_acc[...]*LN2).astype(BF)
        dk_ref[...]=dk
        dv_ref[...]=dv
        if square:
            side=pl.ds(pl.multiple_of(lax.rem(pair,2)*128,128),128)
            dk2[:,side]=dk; dv2[:,side]=dv; dr2[:,side]=dr
            cols=pl.ds(pl.multiple_of(pair*128,128),128)
            vec_s[0:5,cols]=dvec_ref[0:5,:]
            vec_s[5:6,cols]=rowsum(dv.astype(F32))
            vec_s[6:8,cols]=jnp.zeros((2,128),F32)
        else: dr_ref[...]=dr
    if square:
        dq2[pl.ds(pl.multiple_of(i*bi,bi),bi),pl.ds(pl.multiple_of(lax.rem(pair,2)*128,128),128)]=dq
        run_events(step,ev,after=True)

def att_bwd(R,q,k,v,r,oh,vec,e,att,linv,datt,dwu,dwi,dwo,xt,et,vb,vi,bi=BI,roll_bf=False):
    L,D=q.shape; P=D//128; nb=L//bi; n,kk,s,_=dwu.shape
    col=pl.BlockSpec((L,128),lambda p,i:(0,p)); tile=pl.BlockSpec((bi,128),lambda p,i:(i,p))
    full=lambda sh: pl.BlockSpec(sh,lambda p,i:(0,)*len(sh),pipeline_mode=ONE)
    in_specs=[tile,col,col,pl.BlockSpec((2*L,128),lambda p,i:(0,p)),pl.BlockSpec((L,128),lambda p,i:(0,0)),
        pl.BlockSpec((8,128),lambda p,i:(0,p)),pl.BlockSpec((2,bi,L),lambda p,i:(p,i,0)),tile,tile,tile]
    out_specs=[tile,col,col]
    out_shape=[jax.ShapeDtypeStruct((L,D),BF)]*3
    scratch=[pltpu.VMEM((L,128),F32),pltpu.VMEM((L,128),F32),pltpu.VMEM((2*L,128),F32)]
    args=[q,k,v,r,oh,vec,e,att,linv,datt]
    params=dict(vmem_limit_bytes=52*2**20,dimension_semantics=("arbitrary","arbitrary"))
    if is_square(n,R):
        Z,X=shape_of(n); FF=vi.shape[1]; SL=-(-max(s,FF//n)//128)*128
        in_specs+=[pl.BlockSpec(memory_space=pl.ANY)]*3+[full((D,L)),full((D,2*L)),full((8,D)),full((1,FF))]
        for sh in ((kk*s,D),(s,kk*D),(s,D),(4,s,GL),(4,s,GL),(4,s,GL),(16,GL)):
            out_specs.append(full(sh)); out_shape.append(jax.ShapeDtypeStruct(sh,F32))
        scratch+=[pltpu.VMEM((8,128),F32)]+[pltpu.VMEM((L,GL),BF)]*3+[pltpu.VMEM((2*L,GL),BF),pltpu.VMEM((8,D),F32)]
        scratch+=[pltpu.VMEM((Z,X,2,q,s,GL),BF) for q in (4,4,5)]
        scratch+=sum_scratch(n,kk,s,D,1)+sum_scratch(n,kk+1,s,D,2)+sum_scratch(n,4,s,GL,1)*2+sum_scratch(n,5,s,GL,1)
        args+=[dwu.reshape(Z,X,2,kk,s,D),dwi.reshape(Z,X,2,kk,s,D),dwo.reshape(Z,X,2,1,s,D),xt,et,vb,vi]
        params.update(collective_id=2,has_side_effects=True)
    else:
        out_specs+=[pl.BlockSpec((2*L,128),lambda p,i:(0,p)),pl.BlockSpec((8,128),lambda p,i:(0,p))]
        out_shape+=[jax.ShapeDtypeStruct((2*L,D),BF),jax.ShapeDtypeStruct((8,D),F32)]
    return pl.pallas_call(functools.partial(bwd_kernel,n,R,roll_bf),grid=(P,nb),in_specs=in_specs,out_specs=out_specs,out_shape=out_shape,
        scratch_shapes=scratch,compiler_params=pltpu.CompilerParams(**params),
        name="attend_back")(*args)

CP=lambda **k: pltpu.CompilerParams(vmem_limit_bytes=60*2**20,**k)
C0=math.sqrt(2.0/math.pi); C1=0.044715
EPS=1e-6

def whole(ref):
    a=ref[...]
    return a.reshape(-1,a.shape[-1])

def ln_stats(z):
    n=z.shape[1]
    mu=jnp.sum(z,axis=1,keepdims=True)*(1.0/n)
    c=z-mu
    var=jnp.sum(c*c,axis=1,keepdims=True)*(1.0/n)
    r=lax.rsqrt(var+EPS)
    return c*r,r

def ln_back(g,zhat,r):
    n=g.shape[1]
    a=jnp.sum(g,axis=1,keepdims=True)*(1.0/n)
    b=jnp.sum(g*zhat,axis=1,keepdims=True)*(1.0/n)
    return r*(g-a-zhat*b)

def rowsum(v): return jnp.sum(v,axis=0,keepdims=True)

def mid_kernel(nb,bi,nc,x_ref,att_ref,cot_ref,wo_ref,wu_ref,*rest):
    wi_refs=rest[:nc]
    (vec_ref,bi_ref,out_ref,dz1_ref,datt_ref,dwo_ref,dwi_ref,dwu_ref,dvec_ref,dbi_ref,
        mid_s,att_s,dffn_s,dattn_s,hid_s,din_s,acc_s)=rest[nc:]
    t=pl.program_id(0)
    D=x_ref.shape[1]; fc=D
    n=wu_ref.shape[0]; per=n//nc
    wu=lambda c: wu_ref[c*per:(c+1)*per].reshape(fc,D)
    wi=lambda c: whole(wi_refs[c])
    @pl.when(t==0)
    def _():
        dvec_ref[...]=jnp.zeros_like(dvec_ref); dbi_ref[...]=jnp.zeros_like(dbi_ref)
    @pl.when(t<nb)
    def _():
        rows=pl.ds(pl.multiple_of(t*bi,bi),bi)
        b_out,ga,sa,b_outer,gf,sf=[vec_ref[k:k+1,:] for k in range(6)]
        att=att_ref[...]
        att_s[rows,:]=att
        z1=x_ref[...].astype(F32)+dot(att,whole(wo_ref))+b_out
        zh1,r1=ln_stats(z1)
        middle=zh1*ga+sa
        mid=middle.astype(BF)
        mid_s[rows,:]=mid
        acc_s[...]=middle+b_outer
        for c in range(nc):
            cs=slice(c*fc,(c+1)*fc)
            v=dot(mid,wi(c))+bi_ref[:,cs]
            u=v*v
            th=jnp.tanh(v*(C0+(C0*C1)*u))
            hv=0.5*v
            hid=(hv+hv*th).astype(BF)
            dg=0.5+0.5*th+hv*(1.0-th*th)*(C0+(3*C0*C1)*u)
            hid_s[rows,cs]=hid
            din_s[rows,cs]=dg.astype(BF)
            acc_s[...]+=dot(hid,wu(c))
        zh2,r2=ln_stats(acc_s[...])
        out_ref[...]=(zh2*gf+sf).astype(BF)
        g=cot_ref[...].astype(F32)
        dz2=ln_back(g*gf,zh2,r2)
        dffn=dz2.astype(BF)
        dffn_s[rows,:]=dffn
        acc_s[...]=dz2
        dbs=[]
        for c in range(nc):
            cs=slice(c*fc,(c+1)*fc)
            dh=dot(dffn,wu(c),NT)
            din=(dh*din_s[rows,cs].astype(F32)).astype(BF)
            din_s[rows,cs]=din
            dbi_ref[:,cs]+=rowsum(din.astype(F32))
            acc_s[...]+=dot(din,wi(c),NT)
        dm=acc_s[...]
        dz1=ln_back(dm*ga,zh1,r1)
        dz1_ref[...]=dz1
        dattn=dz1.astype(BF)
        dattn_s[rows,:]=dattn
        datt_ref[...]=dot(dattn,whole(wo_ref),NT).astype(BF)
        dvec_ref[...]+=jnp.concatenate([rowsum(dz1),rowsum(dm*zh1),rowsum(dm),rowsum(dz2),rowsum(g*zh2),rowsum(g),jnp.zeros((2,D),F32)],axis=0)
    @pl.when(t==nb)
    def _():
        dwo_ref[...]=dot(att_s[...],dattn_s[...],TN).astype(BF).reshape(dwo_ref.shape)
    for c in range(nc):
        cs=slice(c*fc,(c+1)*fc)
        @pl.when(t==nb+c)
        def _():
            dwi_ref[...]=dot(mid_s[...],din_s[:,cs],TN).astype(BF).reshape(dwi_ref.shape)
            dwu_ref[...]=dot(hid_s[:,cs],dffn_s[...],TN).astype(BF).reshape(dwu_ref.shape)

def middle(x,att,cot,g,vec,b_inner,bi=256):
    L,D=x.shape; n,parts,s,_=g.shape; nc=(parts-1)//2; FF=nc*D; nb=L//bi; per=n//nc
    row=pl.BlockSpec((bi,D),lambda t:(jnp.minimum(t,nb-1),0))
    cc=lambda t: jnp.clip(t-nb,0,nc-1)
    w=lambda j: pl.BlockSpec((n,1,s,D),lambda t:(0,j,0,0),pipeline_mode=ONE)
    return pl.pallas_call(functools.partial(mid_kernel,nb,bi,nc),grid=(nb+nc,),
        in_specs=[row,row,row,w(nc),pl.BlockSpec((n,nc,s,D),lambda t:(0,0,0,0),pipeline_mode=ONE)]+[w(nc+1+j) for j in range(nc)]
            +[pl.BlockSpec((8,D),lambda t:(1,0)),pl.BlockSpec((1,FF),lambda t:(0,0))],
        out_specs=[row,row,row,pl.BlockSpec((n,s,D),lambda t:(0,0,0)),pl.BlockSpec((n,1,s,D),lambda t:(0,cc(t),0,0)),
            pl.BlockSpec((per,nc,s,D),lambda t:(cc(t),0,0,0)),
            pl.BlockSpec((8,D),lambda t:(0,0)),pl.BlockSpec((1,FF),lambda t:(0,0))],
        out_shape=[jax.ShapeDtypeStruct((L,D),BF),jax.ShapeDtypeStruct((L,D),F32),jax.ShapeDtypeStruct((L,D),BF),
            jax.ShapeDtypeStruct((n,s,D),BF),jax.ShapeDtypeStruct((n,nc,s,D),BF),jax.ShapeDtypeStruct((n,nc,s,D),BF),
            jax.ShapeDtypeStruct((8,D),F32),jax.ShapeDtypeStruct((1,FF),F32)],
        scratch_shapes=[pltpu.VMEM((L,D),BF)]*4+[pltpu.VMEM((L,FF),BF)]*2+[pltpu.VMEM((bi,D),F32)],
        compiler_params=CP(),name="middle")(x,att,cot,*([g]*(2+nc)),vec,b_inner)

def pulled(ds,ws):
    out=None
    for g in range(len(ws)//3):
        for j,d in enumerate(ds):
            t=dot(d[:,g*GL:(g+1)*GL],whole(ws[3*g+j]),NT)
            out=t if out is None else out+t
    return out

def last_kernel(nb,bi,x_ref,dq_ref,dk_ref,dv_ref,dz_ref,em_ref,dr_ref,*rest):
    ws=rest[:-6]
    gi_ref,dwq_ref,dwk_ref,dwv_ref,dwp_ref,dbv_ref=rest[-6:]
    t=pl.program_id(0)
    @pl.when(t<nb)
    def _():
        rows=pl.ds(pl.multiple_of(t*bi,bi),bi)
        gi_ref[...]=dz_ref[...]+pulled([r[rows,:] for r in (dq_ref,dk_ref,dv_ref)],ws)
    @pl.when(t==nb)
    def _(): dwq_ref[...]=dot(x_ref[...],dq_ref[...],TN).astype(BF)
    @pl.when(t==nb+1)
    def _(): dwk_ref[...]=dot(x_ref[...],dk_ref[...],TN).astype(BF)
    @pl.when(t==nb+2)
    def _():
        dwv_ref[...]=dot(x_ref[...],dv_ref[...],TN).astype(BF)
        dbv_ref[...]=rowsum(dv_ref[...].astype(F32))
    @pl.when(t==nb+3)
    def _(): dwp_ref[...]=dot(em_ref[...],dr_ref[...],TN).astype(BF)

def last(x,dq,dk,dv,dz1,em,dr,gs,bi=256):
    L,D=x.shape; nb=L//bi; n,_,s,_=gs[0].shape
    w=[pl.BlockSpec((n,1,s,GL),lambda t,j=j:(0,j,0,0),pipeline_mode=ONE) for _ in gs for j in range(3)]
    row=pl.BlockSpec((bi,D),lambda t:(jnp.minimum(t,nb-1),0))
    full=lambda sh: pl.BlockSpec(sh,lambda t:(0,0),pipeline_mode=ONE)
    o=pl.BlockSpec((D,D),lambda t:(0,0))
    W=jax.ShapeDtypeStruct((D,D),BF)
    return pl.pallas_call(functools.partial(last_kernel,nb,bi),grid=(nb+4,),
        in_specs=[full((L,D))]*4+[row,full((2*L,D)),full((2*L,D))]+w,
        out_specs=[row,o,o,o,o,pl.BlockSpec((1,D),lambda t:(0,0))],
        out_shape=[jax.ShapeDtypeStruct((L,D),F32),W,W,W,W,jax.ShapeDtypeStruct((1,D),F32)],
        compiler_params=CP(),name="last")(x,dq,dk,dv,dz1,em,dr,*[g for g in gs for _ in range(3)])

VECTORS=(5,0,1,2,3,8,9,10,14,11,12,13)

def finish_kernel(dz_ref,dq_ref,dk_ref,dv_ref,*rest):
    ws=rest[:9]
    (wu_ref,wi_ref,wo_ref,g0_ref,g1_ref,g2_ref,sv_ref,
        gi_ref,owq_ref,owk_ref,owv_ref,owp_ref,owu_ref,owi_ref,owo_ref)=rest[9:24]
    vecs=rest[24:]
    gi_ref[...]=dz_ref[...]+pulled([r[...] for r in (dq_ref,dk_ref,dv_ref)],ws)
    @pl.when(pl.program_id(0)==0)
    def _():
        for j,o in enumerate((owq_ref,owk_ref,owv_ref,owp_ref)):
            for g,r in enumerate((g0_ref,g1_ref,g2_ref)): o[:,g*GL:(g+1)*GL]=r[j]
        owu_ref[...]=wu_ref[...]; owi_ref[...]=wi_ref[...]; owo_ref[...]=wo_ref[...]
        for r,o in zip(VECTORS,vecs): o[...]=sv_ref[r:r+o.shape[0],:o.shape[1]]

def finish(dq,dk,dv,dz1,gs,wu,wi,wo,groups,sv,bi=256):
    L,D=dq.shape; nb=L//bi; n,_,s,_=gs[0].shape; fs=wu.shape[0]
    w=[pl.BlockSpec((n,1,s,GL),lambda t,j=j:(0,j,0,0),pipeline_mode=ONE) for _ in gs for j in range(3)]
    row=pl.BlockSpec((bi,D),lambda t:(t,0))
    full=lambda sh: pl.BlockSpec(sh,lambda t:(0,)*len(sh),pipeline_mode=ONE)
    outs=[(s,D)]*4+[wu.shape,wi.shape,wo.shape]+[(2,s) if r==3 else (1,fs) if r==14 else (1,s) for r in VECTORS]
    return pl.pallas_call(finish_kernel,grid=(nb,),
        in_specs=[row]*4+w+[full(wu.shape),full(wi.shape),full(wo.shape)]+[full(g_.shape) for g_ in groups]+[full(sv.shape)],
        out_specs=[row]+[full(o) for o in outs],
        out_shape=[jax.ShapeDtypeStruct((L,D),F32)]+[jax.ShapeDtypeStruct(o,F32) for o in outs],
        compiler_params=CP(),name="finish")(dz1,dq,dk,dv,*[g for g in gs for _ in range(3)],wu,wi,wo,*groups,sv)

def local(R,inputs,token_types,buckets,wq,wk,wv,bv,wp,bc,bp,bt,te,wo,bo,ga,sa,wi,b_i,wu,bu,gf,sf,cot):
    s,D=wq.shape; n=D//s; FF=wi.shape[1]; fs=FF//n; kk=FF//D
    SL=-(-max(s,fs)//128)*128
    z=jnp.zeros((s,),BF)
    wide=lambda a: jnp.pad(a,((0,0),(0,SL-a.shape[1])))
    small=jnp.concatenate([wide(jnp.stack([bc,bp,bt,te[0],te[1],bv,z,z,bo,ga,sa,bu,gf,sf])),wide(b_i[None]),jnp.zeros((1,SL),BF)])
    x=inputs[0]
    bk=jnp.pad(buckets,(0,1))[None]
    e,att,linv,q,k,v,r,g2,ga_,gb_,gc_,vec,fb,oh,xt,et=fore(R,x,wq,wk,wv,wp,wo,wi,wu,small,token_types,bk)
    g1=(ga_,gb_,gc_)
    out,dz1,datt,dwo,dwi,dwu,dvec2,dbi=middle(x,att,cot[0],g2,vec,fb)
    res=att_bwd(R,q,k,v,r,oh,vec,e,att,linv,datt,dwu,dwi,dwo,xt,et,dvec2,dbi)
    dq,dk,dv=res[:3]
    if is_square(n,R):
        wu_,wi_,wo_,*gr,sv=res[3:]
        o=finish(dq,dk,dv,dz1,g1,wu_,wi_,wo_,gr,sv)
        gin,dwq,dwk,dwv,dwp,dwu,dwi,dwo=o[:8]
        c=[a[0] for a in o[8:]]
        return (out[None],gin[None],dwq,dwk,dwv,c[0],dwp,c[1],c[2],c[3],o[12],dwo,c[5],c[6],c[7],dwi,c[8],dwu,c[9],c[10],c[11])
    dr,dvec=res[3:]
    gin,dwq,dwk,dwv,dwp,dbv=last(x,dq,dk,dv,dz1,et.T,dr,g1)
    blk=lambda a: a.reshape(n,-1,D)
    r1=jnp.concatenate([blk(dwo),blk(dwi),blk(dwu)],axis=1)
    sv=jnp.concatenate([dbv,dvec[:5],dvec2[:6]]).reshape(12,n,s).transpose(1,0,2).reshape(n,12*s)
    pad=-(12*s+fs)%D
    sv=jnp.concatenate([sv,dbi.reshape(n,fs),jnp.zeros((n,pad),F32)],axis=1).astype(BF).reshape(n,-1,D)
    r2=jnp.concatenate([blk(dwq),blk(dwk),blk(dwv),blk(dwp),sv],axis=1)
    t1=lax.psum_scatter(r1,"shard",scatter_dimension=0,tiled=False).astype(F32)
    t1=lax.psum(t1,"rep")
    t2=lax.psum_scatter(r2,"shard",scatter_dimension=0,tiled=False).astype(F32)
    t2=lax.psum(t2,"rep")
    tv=t2[4*s:].reshape(-1)
    c=lambda j: tv[j*s:(j+1)*s]
    return (out[None],gin[None],t2[:s],t2[s:2*s],t2[2*s:3*s],c(0),t2[3*s:4*s],c(1),c(2),c(3),jnp.stack([c(4),c(5)]),
        t1[:s],c(6),c(7),c(8),jnp.concatenate([t1[(1+j)*s:(2+j)*s] for j in range(kk)],axis=1),tv[12*s:12*s+fs],t1[(1+kk)*s:],c(9),c(10),c(11))

def solution(mesh):
    both=("rep","shard")
    v=P("shard"); w=P("shard",None); a3=P(both,None,None)
    in_specs=(a3,P(both,None),P(),w,w,w,v,w,v,v,v,P(None,"shard"),w,v,v,v,w,v,w,v,v,v,a3)
    out_specs=(a3,a3,w,w,w,v,w,v,v,v,P(None,"shard"),w,v,v,v,w,v,w,v,v,v)
    return jax.shard_map(functools.partial(local,mesh.shape["rep"]),mesh=mesh,in_specs=in_specs,out_specs=out_specs,check_vma=False)
```
